32 devices in a mesh: req: 8 (over y, x, core), mlp: 4 (over z).
Axes of the slice: x: 2, y: 2, z: 4, core: 2. Of those that a mesh axis runs over, the one named last changes fastest.
Arguments:
- layer_input: bfloat16 [1024, 4096], P(('req', 'mlp')), may hold values from -6 to 6
- request_lengths: int32 [8, 4], P('req'), may hold values from 1 to 80, 128 in all within a row
- request_adapter: int32 [8, 4], P('req'), may hold values from 0 to 63, as said below
- slot_adapter_index: int32 [8], replicated, may hold values from 0 to 63, as said below
- query_weight: bfloat16 [4096, 2048], P(None, 'mlp'), may hold values from -0.09375 to 0.09375
- key_weight: bfloat16 [4096, 2048], P(None, 'mlp'), may hold values from -0.09375 to 0.09375
- value_weight: bfloat16 [4096, 2048], P(None, 'mlp'), may hold values from -0.09375 to 0.09375
- output_weight: bfloat16 [2048, 4096], P('mlp'), may hold values from -0.125 to 0.125
- query_norm_gain: float32 [2048], P('mlp'), may hold values from 0.1 to 1.9
- key_norm_gain: float32 [2048], P('mlp'), may hold values from 0.1 to 1.9
- query_down_factors: bfloat16 [4096, 128], replicated, may hold values from -0.09375 to 0.09375
- value_down_factors: bfloat16 [4096, 128], replicated, may hold values from -0.09375 to 0.09375
- query_up_factors: bfloat16 [128, 2048], P(None, 'mlp'), may hold values from -1.5 to 1.5
- value_up_factors: bfloat16 [128, 2048], P(None, 'mlp'), may hold values from -1.5 to 1.5
- attention_norm_gain: float32 [4096], replicated, may hold values from 0.1 to 1.9
- feedforward_norm_gain: float32 [4096], replicated, may hold values from 0.1 to 1.9
- gate_weight: bfloat16 [4096, 6144], P(None, ('req', 'mlp')), may hold values from -0.09375 to 0.09375
- up_weight: bfloat16 [4096, 6144], P(None, ('req', 'mlp')), may hold values from -0.09375 to 0.09375
- down_weight_transposed: bfloat16 [4096, 6144], P(None, ('req', 'mlp')), may hold values from -0.078125 to 0.078125
Outputs:
- layer_out: bfloat16 [1024, 4096], P(('req', 'mlp'))
The draws below stay inside these ranges and needn't reach their ends.
Inputs may be any that keep to these rules, and one draw needn't show every extreme that they name: `request_lengths`: the lengths of a group's requests sum to 128, and the longest request of every group has exactly 80 tokens. `slot_adapter_index`: 8 distinct adapter numbers. `request_adapter`: every request's adapter is one of the numbers in slot_adapter_index.
All inputs are finite; a program needn't handle non-finite values.
Results may differ from the reference program's by a relative error of at most 0.024.
Values may be sent and summed in bfloat16 or wider, within the bound.
No kernel may reach another device: no remote copies, remote signals or barrier semaphores. Data moves between devices by JAX's collectives and lax.ppermute only.
A program may use at most 128 MiB of HBM per device.

```python
import math
import jax
import jax.numpy as jnp
import numpy as np
from jax import lax

MODEL_WIDTH = 4096
HEAD_SIZE = 128
LOCAL_HEADS = 16
FF = 6144
ADAPTER_RANK = 16
ADAPTERS = 64
ADAPTER_SLOTS = 8
REQ_G = 4
SINKS = 4
TOK_GROUP = 128
TOKENS = 1024
GROUPS = 8
LONGEST = 80
WINDOW = 48


def choose_adapters(key):
    others = jax.random.permutation(jax.random.fold_in(key, 101), ADAPTERS - 1)[:ADAPTER_SLOTS - 1].astype(jnp.int32)
    loaded = jnp.concatenate([others, jnp.full((1,), ADAPTERS - 1, jnp.int32)])
    arrangement = jax.random.permutation(jax.random.fold_in(key, 202), ADAPTER_SLOTS)
    loaded = loaded[arrangement]
    chosen_slots = jax.random.randint(jax.random.fold_in(key, 303), (GROUPS, REQ_G), 0, ADAPTER_SLOTS)
    return (loaded, loaded[chosen_slots])


def draw_slot_adapter_index(key, part):
    return choose_adapters(key)[0]


def draw_request_adapter(key, part):
    return choose_adapters(key)[1]


def levels(own_key, dims, split, low, top_value):
    def one(axis_at, blocks):
        draws = jax.random.uniform(jax.random.fold_in(jax.random.fold_in(own_key, 6), axis_at), (blocks,), jnp.float32, low / len(split), top_value / len(split))
        return jnp.repeat(jnp.exp(draws), dims[axis_at] // blocks).reshape((-1,) + (1,) * (len(dims) - axis_at - 1))

    level = one(*split[0])
    for cut in split[1:]:
        level = level * one(*cut)
    return level


def length_profile(number_of, total, bound, slope):
    portions = [(1 << 20) // math.isqrt(rank ** slope) + 1 for rank in range(2, number_of + 1)]
    spare, given = total - bound - (number_of - 1), [1] * (number_of - 1)
    while spare > 0:
        movable = [i for i in range(number_of - 1) if given[i] < bound]
        pool, left = sum([portions[i] for i in movable]), spare
        for i in movable:
            extra = min(bound - given[i], max(1, left * portions[i] // pool), spare)
            given[i] = given[i] + extra
            spare = spare - extra
    return np.array([bound] + given)


def ragged_sizes(rng, count, total, limit, skew):
    if count == 2:
        one = jax.random.randint(rng, (), max(1, total - limit), min(limit, total - 1) + 1)
        return jnp.stack([one, total - one])
    sizes = jnp.asarray(length_profile(count, total, limit, skew), jnp.int32)
    twos = (count - 1) // 2
    donor, taker = sizes[1:1 + 2 * twos:2], sizes[2:2 + 2 * twos:2]
    slack = jnp.minimum(donor - 1, limit - taker)
    moved = jax.random.randint(jax.random.fold_in(rng, 1), (twos,), 0, 1 << 20) % (slack + 1)
    sizes = sizes.at[1:1 + 2 * twos:2].set(donor - moved).at[2:2 + 2 * twos:2].set(taker + moved)
    return sizes[jax.random.permutation(jax.random.fold_in(rng, 2), count)]


def bell_draw(own_key, shape, spread, limit, shards=(), kind=jnp.bfloat16):
    loudness = levels(own_key, shape, shards, -0.22, 0.18) if shards else 1.0
    drawn = jax.random.normal(own_key, shape, jnp.float32) * spread * loudness
    return jnp.minimum(jnp.maximum(drawn, -limit), limit).astype(kind)


def setup_inputs(seed: int = 0) -> dict:
    key_of = jax.random.split(jax.random.key(seed), 20)
    layer_input = bell_draw(key_of[0], (TOKENS, MODEL_WIDTH), 1.0, 6.0, ((0, 32),))
    request_lengths = jax.vmap(lambda own: ragged_sizes(own, REQ_G, TOK_GROUP, LONGEST, 2))(jax.random.split(key_of[1], GROUPS)).reshape((GROUPS, REQ_G)).astype(jnp.int32)
    request_adapter = draw_request_adapter(jax.random.fold_in(key_of[19], 71), 0)
    slot_adapter_index = draw_slot_adapter_index(jax.random.fold_in(key_of[19], 71), 0)
    query_weight = bell_draw(key_of[4], (MODEL_WIDTH, LOCAL_HEADS * HEAD_SIZE), MODEL_WIDTH ** -0.5, 0.09375, ((1, 4),))
    key_weight = bell_draw(key_of[5], (MODEL_WIDTH, LOCAL_HEADS * HEAD_SIZE), MODEL_WIDTH ** -0.5, 0.09375, ((1, 4),))
    value_weight = bell_draw(key_of[6], (MODEL_WIDTH, LOCAL_HEADS * HEAD_SIZE), MODEL_WIDTH ** -0.5, 0.09375, ((1, 4),))
    output_weight = bell_draw(key_of[7], (LOCAL_HEADS * HEAD_SIZE, MODEL_WIDTH), (LOCAL_HEADS * HEAD_SIZE) ** -0.5, 0.125, ((0, 4),))
    query_norm_gain = jnp.clip(1.0 + 0.18 * jax.random.normal(key_of[8], (LOCAL_HEADS * HEAD_SIZE,), jnp.float32), 0.1, 1.9)
    key_norm_gain = jnp.clip(1.0 + 0.18 * jax.random.normal(key_of[9], (LOCAL_HEADS * HEAD_SIZE,), jnp.float32), 0.1, 1.9)
    query_down_factors = bell_draw(key_of[10], (MODEL_WIDTH, ADAPTER_SLOTS * ADAPTER_RANK), MODEL_WIDTH ** -0.5, 0.09375)
    value_down_factors = bell_draw(key_of[11], (MODEL_WIDTH, ADAPTER_SLOTS * ADAPTER_RANK), MODEL_WIDTH ** -0.5, 0.09375)
    query_up_factors = bell_draw(key_of[12], (ADAPTER_SLOTS * ADAPTER_RANK, LOCAL_HEADS * HEAD_SIZE), ADAPTER_RANK ** -0.5, 1.5, ((1, 4),))
    value_up_factors = bell_draw(key_of[13], (ADAPTER_SLOTS * ADAPTER_RANK, LOCAL_HEADS * HEAD_SIZE), ADAPTER_RANK ** -0.5, 1.5, ((1, 4),))
    attention_norm_gain = jnp.clip(1.0 + 0.18 * jax.random.normal(key_of[14], (MODEL_WIDTH,), jnp.float32), 0.1, 1.9)
    feedforward_norm_gain = jnp.clip(1.0 + 0.18 * jax.random.normal(key_of[15], (MODEL_WIDTH,), jnp.float32), 0.1, 1.9)
    gate_weight = bell_draw(key_of[16], (MODEL_WIDTH, FF), MODEL_WIDTH ** -0.5, 0.09375, ((1, 32),))
    up_weight = bell_draw(key_of[17], (MODEL_WIDTH, FF), MODEL_WIDTH ** -0.5, 0.09375, ((1, 32),))
    down_weight_transposed = bell_draw(key_of[18], (MODEL_WIDTH, FF), FF ** -0.5, 0.078125, ((1, 32),))
    return {"layer_input": layer_input, "request_lengths": request_lengths, "request_adapter": request_adapter, "slot_adapter_index": slot_adapter_index, "query_weight": query_weight, "key_weight": key_weight, "value_weight": value_weight, "output_weight": output_weight, "query_norm_gain": query_norm_gain, "key_norm_gain": key_norm_gain, "query_down_factors": query_down_factors, "value_down_factors": value_down_factors, "query_up_factors": query_up_factors, "value_up_factors": value_up_factors, "attention_norm_gain": attention_norm_gain, "feedforward_norm_gain": feedforward_norm_gain, "gate_weight": gate_weight, "up_weight": up_weight, "down_weight_transposed": down_weight_transposed}


epsilon = 1e-06
adapter_scale = 0.5
rope_theta = 500000.0

def rms_scale(inputs):
    return inputs * lax.rsqrt(lax.optimization_barrier(jnp.mean(inputs * inputs, axis=-1, keepdims=True)) + epsilon)

def rotary(inputs, position):
    half_dim = inputs.shape[-1] // 2
    exponent = jnp.arange(half_dim, dtype=jnp.float32) * (2.0 / inputs.shape[-1])
    frequency = rope_theta ** (-exponent)
    angles = position.astype(jnp.float32)[:, None] * frequency[None, :]
    cosine = jnp.cos(angles)[:, None, :]
    sine_part = jnp.sin(angles)[:, None, :]
    first_half = inputs[..., :half_dim]
    second = inputs[..., half_dim:]
    return jnp.concatenate([first_half * cosine - second * sine_part, second * cosine + first_half * sine_part], axis=-1)

def layout(lengths, adapters, slot_adapter_index, row_count):
    req_ends = jnp.cumsum(lengths).astype(jnp.int32)
    starts = req_ends - lengths
    places = jnp.arange(row_count, dtype=jnp.int32)
    member = ((places[:, None] >= starts[None, :]) & (places[:, None] < req_ends[None, :])).astype(jnp.int32)
    request = lax.optimization_barrier(jnp.sum(member * jnp.arange(lengths.shape[0], dtype=jnp.int32)[None, :], axis=1))
    position = places - lax.optimization_barrier(jnp.sum(member * starts[None, :], axis=1))
    chosen = lax.optimization_barrier(jnp.sum(member * adapters[None, :], axis=1))
    slot_ids = jnp.arange(slot_adapter_index.shape[0], dtype=jnp.int32)
    token_slot = lax.optimization_barrier(jnp.sum((chosen[:, None] == slot_adapter_index[None, :]).astype(jnp.int32) * slot_ids[None, :], axis=1))
    return (request, position, token_slot)

def attention(queries, key_heads, value_heads, request, position):
    scores = jnp.einsum('qhd,khd->hqk', queries.astype(jnp.float32), key_heads.astype(jnp.float32)) * HEAD_SIZE ** (-0.5)
    distance = position[:, None] - position[None, :]
    allowed = (request[:, None] == request[None, :]) & (distance >= 0) & ((distance < WINDOW) | (position[None, :] < SINKS))
    scores = jnp.where(allowed[None, :, :], scores, -1e+30)
    row_peak = lax.optimization_barrier(jnp.max(scores, axis=-1, keepdims=True))
    weights = jnp.exp(scores - row_peak)
    weights = (weights / lax.optimization_barrier(jnp.sum(weights, axis=-1, keepdims=True))).astype(jnp.bfloat16)
    context = jnp.einsum('hqk,khd->qhd', weights.astype(jnp.float32), value_heads.astype(jnp.float32))
    return context.astype(jnp.bfloat16)

def reference(layer_input, request_lengths, request_adapter, slot_adapter_index, query_weight, key_weight, value_weight, output_weight, query_norm_gain, key_norm_gain, query_down_factors, value_down_factors, query_up_factors, value_up_factors, attention_norm_gain, feedforward_norm_gain, gate_weight, up_weight, down_weight_transposed):

    def one_group(group_items):
        group_token_rows, lengths, adapters = group_items
        request, position, token_slot = layout(lengths, adapters, slot_adapter_index, TOK_GROUP)
        columns = jnp.arange(ADAPTER_SLOTS * ADAPTER_RANK, dtype=jnp.int32) // ADAPTER_RANK
        slot_match_mask = (columns[None, :] == token_slot[:, None]).astype(jnp.bfloat16)
        query_reduced = jnp.dot(group_token_rows, query_down_factors, preferred_element_type=jnp.float32).astype(jnp.bfloat16) * slot_match_mask
        value_reduced = jnp.dot(group_token_rows, value_down_factors, preferred_element_type=jnp.float32).astype(jnp.bfloat16) * slot_match_mask
        query_before_norm = jnp.dot(group_token_rows, query_weight, preferred_element_type=jnp.float32) + adapter_scale * jnp.dot(query_reduced, query_up_factors, preferred_element_type=jnp.float32)
        key_pre = jnp.dot(group_token_rows, key_weight, preferred_element_type=jnp.float32)
        value_before_adapter = jnp.dot(group_token_rows, value_weight, preferred_element_type=jnp.float32) + adapter_scale * jnp.dot(value_reduced, value_up_factors, preferred_element_type=jnp.float32)
        queries = rotary(rms_scale(query_before_norm.reshape(TOK_GROUP, LOCAL_HEADS, HEAD_SIZE)) * query_norm_gain.reshape(LOCAL_HEADS, HEAD_SIZE), position).astype(jnp.bfloat16)
        key_heads = rotary(rms_scale(key_pre.reshape(TOK_GROUP, LOCAL_HEADS, HEAD_SIZE)) * key_norm_gain.reshape(LOCAL_HEADS, HEAD_SIZE), position).astype(jnp.bfloat16)
        value_heads = value_before_adapter.astype(jnp.bfloat16).reshape(TOK_GROUP, LOCAL_HEADS, HEAD_SIZE)
        context = attention(queries, key_heads, value_heads, request, position).reshape(TOK_GROUP, LOCAL_HEADS * HEAD_SIZE)
        attn_out = jnp.dot(context, output_weight, preferred_element_type=jnp.float32)
        residual_mid = (group_token_rows.astype(jnp.float32) + rms_scale(attn_out) * attention_norm_gain).astype(jnp.bfloat16)
        gate_act = jnp.dot(residual_mid, gate_weight, preferred_element_type=jnp.float32)
        up_act = jnp.dot(residual_mid, up_weight, preferred_element_type=jnp.float32)
        hidden_act = (jax.nn.silu(gate_act) * up_act).astype(jnp.bfloat16)
        mlp_out = jnp.dot(hidden_act, down_weight_transposed.T, preferred_element_type=jnp.float32)
        return (residual_mid.astype(jnp.float32) + rms_scale(mlp_out) * feedforward_norm_gain).astype(jnp.bfloat16)
    grouped = layer_input.reshape(GROUPS, TOK_GROUP, MODEL_WIDTH)
    results = lax.map(one_group, (grouped, request_lengths, request_adapter))
    return results.reshape(TOKENS, MODEL_WIDTH)
```

```python
import math

import jax
import jax.numpy as jnp
from jax import lax
from jax.sharding import Mesh, PartitionSpec as P

HEAD_SIZE = 128
ADAPTER_RANK = 16
ADAPTER_SLOTS = 8
SINKS = 4
REQ = ("y", "x", "core")
STATIONARY_TOKENS = 2048


epsilon = 1e-06
adapter_scale = 0.5
rope_theta = 500000.0


def rms_scale(inputs):
    return inputs * lax.rsqrt(jnp.mean(inputs * inputs, axis=-1, keepdims=True) + epsilon)


def rotary(inputs, position):
    half_dim = inputs.shape[-1] // 2
    exponent = jnp.arange(half_dim, dtype=jnp.float32) * (2.0 / inputs.shape[-1])
    frequency = rope_theta ** (-exponent)
    angles = position.astype(jnp.float32)[:, None] * frequency[None, :]
    cosine = jnp.cos(angles)[:, None, :]
    sine_part = jnp.sin(angles)[:, None, :]
    first_half = inputs[..., :half_dim]
    second = inputs[..., half_dim:]
    return jnp.concatenate(
        [first_half * cosine - second * sine_part, second * cosine + first_half * sine_part],
        axis=-1,
    )


def layout(lengths, adapters, slot_adapter_index, row_count):
    req_ends = jnp.cumsum(lengths)
    starts = req_ends - lengths
    places = jnp.arange(row_count, dtype=jnp.int32)
    member = ((places[:, None] >= starts[None, :]) & (places[:, None] < req_ends[None, :])).astype(
        jnp.int32
    )
    request = jnp.sum(member * jnp.arange(lengths.shape[0], dtype=jnp.int32)[None, :], axis=1)
    position = places - jnp.sum(member * starts[None, :], axis=1)
    chosen = jnp.sum(member * adapters[None, :], axis=1)
    slot_ids = jnp.arange(slot_adapter_index.shape[0], dtype=jnp.int32)
    token_slot = jnp.sum(
        (chosen[:, None] == slot_adapter_index[None, :]).astype(jnp.int32) * slot_ids[None, :],
        axis=1,
    )
    return (request, position, token_slot)


def attention(queries, key_heads, value_heads, request, position, window):
    scores = jnp.einsum(
        "qhd,khd->hqk", queries, key_heads, preferred_element_type=jnp.float32
    ) * HEAD_SIZE ** (-0.5)
    distance = position[:, None] - position[None, :]
    allowed = (
        (request[:, None] == request[None, :])
        & (distance >= 0)
        & ((distance < window) | (position[None, :] < SINKS))
    )
    scores = jnp.where(allowed[None, :, :], scores, -1e30)
    row_peak = jnp.max(scores, axis=-1, keepdims=True)
    weights = jnp.exp(scores - row_peak)
    weights = (weights / jnp.sum(weights, axis=-1, keepdims=True)).astype(jnp.bfloat16)
    context = jnp.einsum("hqk,khd->qhd", weights, value_heads, preferred_element_type=jnp.float32)
    return context.astype(jnp.bfloat16)


def hidden_units(states, gate_rows, up_rows):
    contract = (((1,), (1,)), ((), ()))
    gate_act = lax.dot_general(states, gate_rows, contract, preferred_element_type=jnp.float32)
    up_act = lax.dot_general(states, up_rows, contract, preferred_element_type=jnp.float32)
    return (jax.nn.silu(gate_act) * up_act).astype(jnp.bfloat16)


def feed_forward(states, gate_rows, up_rows, down_rows):
    return jnp.dot(
        hidden_units(states, gate_rows, up_rows), down_rows, preferred_element_type=jnp.float32
    )


def shards(
    layer_input,
    request_lengths,
    request_adapter,
    slot_adapter_index,
    query_weight,
    key_weight,
    value_weight,
    output_weight,
    query_norm_gain,
    key_norm_gain,
    query_down_factors,
    value_down_factors,
    query_up_factors,
    value_up_factors,
    attention_norm_gain,
    feedforward_norm_gain,
    gate_weight,
    up_weight,
    down_weight_transposed,
):
    tok_dev = layer_input.shape[0]
    tok_group = tok_dev * lax.axis_size("mlp")
    window = tok_group * 3 // 8
    heads_local = query_weight.shape[1] // HEAD_SIZE
    request, position, token_slot = layout(
        request_lengths[0], request_adapter[0], slot_adapter_index, tok_group
    )
    group_token_rows = lax.all_gather(layer_input, "mlp", axis=0, tiled=True)
    columns = jnp.arange(ADAPTER_SLOTS * ADAPTER_RANK, dtype=jnp.int32) // ADAPTER_RANK
    slot_match_mask = (columns[None, :] == token_slot[:, None]).astype(jnp.bfloat16)
    query_reduced = (
        jnp.dot(group_token_rows, query_down_factors, preferred_element_type=jnp.float32).astype(
            jnp.bfloat16
        )
        * slot_match_mask
    )
    value_reduced = (
        jnp.dot(group_token_rows, value_down_factors, preferred_element_type=jnp.float32).astype(
            jnp.bfloat16
        )
        * slot_match_mask
    )
    query_before_norm = jnp.dot(
        group_token_rows, query_weight, preferred_element_type=jnp.float32
    ) + adapter_scale * jnp.dot(query_reduced, query_up_factors, preferred_element_type=jnp.float32)
    key_pre = jnp.dot(group_token_rows, key_weight, preferred_element_type=jnp.float32)
    value_before_adapter = jnp.dot(
        group_token_rows, value_weight, preferred_element_type=jnp.float32
    ) + adapter_scale * jnp.dot(value_reduced, value_up_factors, preferred_element_type=jnp.float32)
    queries = rotary(
        rms_scale(query_before_norm.reshape(tok_group, heads_local, HEAD_SIZE))
        * query_norm_gain.reshape(heads_local, HEAD_SIZE),
        position,
    ).astype(jnp.bfloat16)
    key_heads = rotary(
        rms_scale(key_pre.reshape(tok_group, heads_local, HEAD_SIZE))
        * key_norm_gain.reshape(heads_local, HEAD_SIZE),
        position,
    ).astype(jnp.bfloat16)
    value_heads = value_before_adapter.astype(jnp.bfloat16).reshape(
        tok_group, heads_local, HEAD_SIZE
    )
    context = attention(queries, key_heads, value_heads, request, position, window).reshape(
        tok_group, heads_local * HEAD_SIZE
    )
    attn_own = lax.psum_scatter(
        jnp.dot(context, output_weight, preferred_element_type=jnp.float32).astype(jnp.bfloat16),
        "mlp",
        scatter_dimension=0,
        tiled=True,
    ).astype(jnp.float32)
    residual_own = (
        layer_input.astype(jnp.float32) + rms_scale(attn_own) * attention_norm_gain
    ).astype(jnp.bfloat16)
    gate_rows, up_rows, down_rows = gate_weight.T, up_weight.T, down_weight_transposed.T
    if tok_group * lax.axis_size(REQ) <= STATIONARY_TOKENS:
        token_axes = ("y", "x", "mlp")
        swap = [(0, 1), (1, 0)]
        gate_rows, up_rows, down_rows = (
            jnp.concatenate([rows, lax.ppermute(rows, "core", swap)])
            for rows in (gate_rows, up_rows, down_rows)
        )
    else:
        token_axes = ("mlp",)
        gate_rows, up_rows, down_rows = (
            lax.all_gather(rows, REQ, axis=0, tiled=True) for rows in (gate_rows, up_rows, down_rows)
        )
    residual_all = lax.all_gather(residual_own, token_axes, axis=0, tiled=True)
    partial_value = feed_forward(residual_all, gate_rows, up_rows, down_rows)
    mlp_own = lax.psum_scatter(
        partial_value.astype(jnp.bfloat16), token_axes, scatter_dimension=0, tiled=True
    ).astype(jnp.float32)
    return (residual_own.astype(jnp.float32) + rms_scale(mlp_own) * feedforward_norm_gain).astype(
        jnp.bfloat16
    )


def solution(mesh):
    req, mlp = mesh.devices.shape
    side = math.isqrt(req // 2)
    fine = Mesh(mesh.devices.reshape(req // 2 // side, side, 2, mlp), ("y", "x", "core", "mlp"))
    return jax.shard_map(
        shards,
        mesh=fine,
        in_specs=(
            P((*REQ, "mlp"), None),
            P(REQ, None),
            P(REQ, None),
            P(),
            P(None, "mlp"),
            P(None, "mlp"),
            P(None, "mlp"),
            P("mlp", None),
            P("mlp"),
            P("mlp"),
            P(),
            P(),
            P(None, "mlp"),
            P(None, "mlp"),
            P(),
            P(),
            P(None, (*REQ, "mlp")),
            P(None, (*REQ, "mlp")),
            P(None, (*REQ, "mlp")),
        ),
        out_specs=P((*REQ, "mlp"), None),
        check_vma=False,
    )
```

```python
import math

import jax
import jax.numpy as jnp
from jax import lax
from jax.sharding import Mesh, PartitionSpec as P

HEAD_SIZE = 128
ADAPTER_RANK = 16
ADAPTER_SLOTS = 8
SINKS = 4
REQ = ("y", "x", "core")


epsilon = 1e-06
adapter_scale = 0.5
rope_theta = 500000.0


def rms_scale(inputs):
    return inputs * lax.rsqrt(jnp.mean(inputs * inputs, axis=-1, keepdims=True) + epsilon)


def rotary(inputs, position):
    half_dim = inputs.shape[-1] // 2
    exponent = jnp.arange(half_dim, dtype=jnp.float32) * (2.0 / inputs.shape[-1])
    frequency = rope_theta ** (-exponent)
    angles = position.astype(jnp.float32)[:, None] * frequency[None, :]
    cosine = jnp.cos(angles)[:, None, :]
    sine_part = jnp.sin(angles)[:, None, :]
    first_half = inputs[..., :half_dim]
    second = inputs[..., half_dim:]
    return jnp.concatenate(
        [first_half * cosine - second * sine_part, second * cosine + first_half * sine_part],
        axis=-1,
    )


def layout(lengths, adapters, slot_adapter_index, places):
    req_ends = jnp.cumsum(lengths)
    starts = req_ends - lengths
    member = ((places[:, None] >= starts[None, :]) & (places[:, None] < req_ends[None, :])).astype(
        jnp.int32
    )
    request = jnp.sum(member * jnp.arange(lengths.shape[0], dtype=jnp.int32)[None, :], axis=1)
    position = places - jnp.sum(member * starts[None, :], axis=1)
    chosen = jnp.sum(member * adapters[None, :], axis=1)
    slot_ids = jnp.arange(slot_adapter_index.shape[0], dtype=jnp.int32)
    token_slot = jnp.sum(
        (chosen[:, None] == slot_adapter_index[None, :]).astype(jnp.int32) * slot_ids[None, :],
        axis=1,
    )
    return (request, position, token_slot)


def attention(queries, key_heads, value_heads, request, position, window):
    scores = jnp.einsum(
        "qhd,khd->hqk", queries, key_heads, preferred_element_type=jnp.float32
    ) * HEAD_SIZE ** (-0.5)
    distance = position[:, None] - position[None, :]
    allowed = (
        (request[:, None] == request[None, :])
        & (distance >= 0)
        & ((distance < window) | (position[None, :] < SINKS))
    )
    scores = jnp.where(allowed[None, :, :], scores, -1e30)
    row_peak = jnp.max(scores, axis=-1, keepdims=True)
    weights = jnp.exp(scores - row_peak)
    weights = (weights / jnp.sum(weights, axis=-1, keepdims=True)).astype(jnp.bfloat16)
    context = jnp.einsum("hqk,khd->qhd", weights, value_heads, preferred_element_type=jnp.float32)
    return context.astype(jnp.bfloat16)


def hidden_units(states, gate_rows, up_rows):
    contract = (((1,), (1,)), ((), ()))
    gate_act = lax.dot_general(states, gate_rows, contract, preferred_element_type=jnp.float32)
    up_act = lax.dot_general(states, up_rows, contract, preferred_element_type=jnp.float32)
    return (jax.nn.silu(gate_act) * up_act).astype(jnp.bfloat16)


def exchange(block, axis):
    return lax.ppermute(block, axis, [(0, 1), (1, 0)])


def line_gather(block):
    index = lax.axis_index("mlp")
    from_right = lax.ppermute(block, "mlp", [(1, 0), (2, 1), (3, 2)])
    from_left = lax.ppermute(block, "mlp", [(0, 1), (1, 2), (2, 3)])
    across = lax.ppermute(block, "mlp", [(0, 2), (1, 3), (2, 0), (3, 1)])
    far = lax.ppermute(across, "mlp", [(1, 0), (2, 3)])
    return [
        block,
        jnp.where(index == 3, far, from_right),
        across,
        jnp.where(index == 0, far, from_left),
    ]


def line_scatter(parts):
    index = lax.axis_index("mlp")
    far = lax.ppermute(jnp.where(index == 0, parts[3], parts[1]), "mlp", [(0, 1), (3, 2)])
    to_right = lax.ppermute(parts[1], "mlp", [(0, 1), (1, 2), (2, 3)])
    to_left = lax.ppermute(parts[3], "mlp", [(1, 0), (2, 1), (3, 2)])
    across = (parts[2].astype(jnp.float32) + far.astype(jnp.float32)).astype(parts[2].dtype)
    across = lax.ppermute(across, "mlp", [(0, 2), (1, 3), (2, 0), (3, 1)])
    return sum(part.astype(jnp.float32) for part in (parts[0], to_right, to_left, across))


def gather_group(block, direct):
    if direct:
        return jnp.concatenate(line_gather(block))
    return lax.all_gather(block, "mlp", axis=0, tiled=True)


def scatter_group(rows, direct):
    if direct:
        return line_scatter(jnp.split(rows, 4))
    return lax.psum_scatter(rows, "mlp", scatter_dimension=0, tiled=True).astype(jnp.float32)


def spread_weights(gate_rows, up_rows, down_rows):
    gate_x, up_x = exchange(gate_rows, "x"), exchange(up_rows, "x")
    half = down_rows.shape[1] // 2
    y = lax.axis_index("y")
    own = lax.dynamic_slice_in_dim(down_rows, y * half, half, axis=1)
    other = exchange(lax.dynamic_slice_in_dim(down_rows, (1 - y) * half, half, axis=1), "y")
    own_x, other_x = exchange(own, "x"), exchange(other, "x")

    def quad(rows, rows_x):
        return jnp.concatenate([rows, exchange(rows, "core"), rows_x, exchange(rows_x, "core")])

    return quad(gate_rows, gate_x), quad(up_rows, up_x), quad(own, own_x), quad(other, other_x)


def shards(
    layer_input,
    request_lengths,
    request_adapter,
    slot_adapter_index,
    query_weight,
    key_weight,
    value_weight,
    output_weight,
    query_norm_gain,
    key_norm_gain,
    query_down_factors,
    value_down_factors,
    query_up_factors,
    value_up_factors,
    attention_norm_gain,
    feedforward_norm_gain,
    gate_weight,
    up_weight,
    down_weight_transposed,
):
    tok_dev = layer_input.shape[0]
    tok_group = tok_dev * lax.axis_size("mlp")
    window = tok_group * 3 // 8
    heads_local = query_weight.shape[1] // HEAD_SIZE
    direct = [lax.axis_size(axis) for axis in (*REQ, "mlp")] == [2, 2, 2, 4]
    places = jnp.arange(tok_group, dtype=jnp.int32)
    if direct:
        places = (places + lax.axis_index("mlp") * tok_dev) % tok_group
    request, position, token_slot = layout(
        request_lengths[0], request_adapter[0], slot_adapter_index, places
    )
    gate_rows, up_rows, down_rows = gate_weight.T, up_weight.T, down_weight_transposed.T
    if direct:
        gate_rows, up_rows, down_near, down_far = spread_weights(gate_rows, up_rows, down_rows)
    group_token_rows = gather_group(layer_input, direct)
    columns = jnp.arange(ADAPTER_SLOTS * ADAPTER_RANK, dtype=jnp.int32) // ADAPTER_RANK
    slot_match_mask = (columns[None, :] == token_slot[:, None]).astype(jnp.bfloat16)
    query_reduced = (
        jnp.dot(group_token_rows, query_down_factors, preferred_element_type=jnp.float32).astype(
            jnp.bfloat16
        )
        * slot_match_mask
    )
    value_reduced = (
        jnp.dot(group_token_rows, value_down_factors, preferred_element_type=jnp.float32).astype(
            jnp.bfloat16
        )
        * slot_match_mask
    )
    query_before_norm = jnp.dot(
        group_token_rows, query_weight, preferred_element_type=jnp.float32
    ) + adapter_scale * jnp.dot(query_reduced, query_up_factors, preferred_element_type=jnp.float32)
    key_pre = jnp.dot(group_token_rows, key_weight, preferred_element_type=jnp.float32)
    value_before_adapter = jnp.dot(
        group_token_rows, value_weight, preferred_element_type=jnp.float32
    ) + adapter_scale * jnp.dot(value_reduced, value_up_factors, preferred_element_type=jnp.float32)
    queries = rotary(
        rms_scale(query_before_norm.reshape(tok_group, heads_local, HEAD_SIZE))
        * query_norm_gain.reshape(heads_local, HEAD_SIZE),
        position,
    ).astype(jnp.bfloat16)
    key_heads = rotary(
        rms_scale(key_pre.reshape(tok_group, heads_local, HEAD_SIZE))
        * key_norm_gain.reshape(heads_local, HEAD_SIZE),
        position,
    ).astype(jnp.bfloat16)
    value_heads = value_before_adapter.astype(jnp.bfloat16).reshape(
        tok_group, heads_local, HEAD_SIZE
    )
    context = attention(queries, key_heads, value_heads, request, position, window).reshape(
        tok_group, heads_local * HEAD_SIZE
    )
    attn_own = scatter_group(
        jnp.dot(context, output_weight, preferred_element_type=jnp.float32).astype(jnp.bfloat16),
        direct,
    )
    residual_own = (
        layer_input.astype(jnp.float32) + rms_scale(attn_own) * attention_norm_gain
    ).astype(jnp.bfloat16)
    if direct:
        line = line_gather(residual_own)
        other = [exchange(block, "y") for block in line]
        states = jnp.concatenate(line + other)
        hidden = hidden_units(states, gate_rows, up_rows)
        hidden_other = jnp.concatenate(
            [exchange(hidden[tok_group:], "y"), exchange(hidden[:tok_group], "y")]
        )
        part = jnp.dot(hidden, down_near, preferred_element_type=jnp.float32)
        part = part + jnp.dot(hidden_other, down_far, preferred_element_type=jnp.float32)
        part = part.astype(jnp.bfloat16).reshape(2, 4, tok_dev, -1)
        summed = line_scatter([part[:, k] for k in range(4)])
        own_half = summed[0]
        other_half = exchange(summed[1].astype(jnp.bfloat16), "y").astype(jnp.float32)
        upper = lax.axis_index("y") == 1
        mlp_own = jnp.concatenate(
            [jnp.where(upper, other_half, own_half), jnp.where(upper, own_half, other_half)], axis=1
        )
    else:
        gate_rows, up_rows, down_rows = (
            lax.all_gather(rows, REQ, axis=0, tiled=True) for rows in (gate_rows, up_rows, down_rows)
        )
        hidden = hidden_units(gather_group(residual_own, direct), gate_rows, up_rows)
        part = jnp.dot(hidden, down_rows, preferred_element_type=jnp.float32)
        mlp_own = scatter_group(part.astype(jnp.bfloat16), direct)
    return (residual_own.astype(jnp.float32) + rms_scale(mlp_own) * feedforward_norm_gain).astype(
        jnp.bfloat16
    )


def solution(mesh):
    req, mlp = mesh.devices.shape
    side = math.isqrt(req // 2)
    fine = Mesh(mesh.devices.reshape(req // 2 // side, side, 2, mlp), ("y", "x", "core", "mlp"))
    return jax.shard_map(
        shards,
        mesh=fine,
        in_specs=(
            P((*REQ, "mlp"), None),
            P(REQ, None),
            P(REQ, None),
            P(),
            P(None, "mlp"),
            P(None, "mlp"),
            P(None, "mlp"),
            P("mlp", None),
            P("mlp"),
            P("mlp"),
            P(),
            P(),
            P(None, "mlp"),
            P(None, "mlp"),
            P(),
            P(),
            P(None, (*REQ, "mlp")),
            P(None, (*REQ, "mlp")),
            P(None, (*REQ, "mlp")),
        ),
        out_specs=P((*REQ, "mlp"), None),
        check_vma=False,
    )
```

```python
import math

import jax
import jax.numpy as jnp
from jax import lax
from jax.sharding import Mesh, PartitionSpec as P

HEAD_SIZE = 128
ADAPTER_RANK = 16
ADAPTER_SLOTS = 8
SINKS = 4
REQ = ("y", "x", "core")


epsilon = 1e-06
adapter_scale = 0.5
rope_theta = 500000.0


def rms_scale(inputs):
    return inputs * lax.rsqrt(jnp.mean(inputs * inputs, axis=-1, keepdims=True) + epsilon)


def rotary(inputs, position):
    half_dim = inputs.shape[-1] // 2
    exponent = jnp.arange(half_dim, dtype=jnp.float32) * (2.0 / inputs.shape[-1])
    frequency = rope_theta ** (-exponent)
    angles = position.astype(jnp.float32)[:, None] * frequency[None, :]
    cosine = jnp.cos(angles)[:, None, :]
    sine_part = jnp.sin(angles)[:, None, :]
    first_half = inputs[..., :half_dim]
    second = inputs[..., half_dim:]
    return jnp.concatenate(
        [first_half * cosine - second * sine_part, second * cosine + first_half * sine_part],
        axis=-1,
    )


def layout(lengths, adapters, slot_adapter_index, places):
    req_ends = jnp.cumsum(lengths)
    starts = req_ends - lengths
    member = ((places[:, None] >= starts[None, :]) & (places[:, None] < req_ends[None, :])).astype(
        jnp.int32
    )
    request = jnp.sum(member * jnp.arange(lengths.shape[0], dtype=jnp.int32)[None, :], axis=1)
    position = places - jnp.sum(member * starts[None, :], axis=1)
    chosen = jnp.sum(member * adapters[None, :], axis=1)
    slot_ids = jnp.arange(slot_adapter_index.shape[0], dtype=jnp.int32)
    token_slot = jnp.sum(
        (chosen[:, None] == slot_adapter_index[None, :]).astype(jnp.int32) * slot_ids[None, :],
        axis=1,
    )
    return (request, position, token_slot)


def attention(queries, key_heads, value_heads, request, position, window):
    scores = jnp.einsum(
        "qhd,khd->hqk", queries, key_heads, preferred_element_type=jnp.float32
    ) * HEAD_SIZE ** (-0.5)
    distance = position[:, None] - position[None, :]
    allowed = (
        (request[:, None] == request[None, :])
        & (distance >= 0)
        & ((distance < window) | (position[None, :] < SINKS))
    )
    scores = jnp.where(allowed[None, :, :], scores, -1e30)
    row_peak = jnp.max(scores, axis=-1, keepdims=True)
    weights = jnp.exp(scores - row_peak)
    weights = (weights / jnp.sum(weights, axis=-1, keepdims=True)).astype(jnp.bfloat16)
    context = jnp.einsum("hqk,khd->qhd", weights, value_heads, preferred_element_type=jnp.float32)
    return context.astype(jnp.bfloat16)


def hidden_units(states, gate_rows, up_rows):
    contract = (((1,), (1,)), ((), ()))
    gate_act = lax.dot_general(states, gate_rows, contract, preferred_element_type=jnp.float32)
    up_act = lax.dot_general(states, up_rows, contract, preferred_element_type=jnp.float32)
    return (jax.nn.silu(gate_act) * up_act).astype(jnp.bfloat16)


def exchange(block, axis):
    return lax.ppermute(block, axis, [(0, 1), (1, 0)])


def shift(block, hops):
    return lax.ppermute(block, "mlp", [((k + hops) % 4, k) for k in range(4)])


def line_gather(block):
    across = shift(block, 2)
    return [block, shift(block, 1), across, shift(block, 3)]


def line_scatter(parts):
    across = shift(parts[2], 2)
    arrived = (parts[0], shift(parts[3], 1), across, shift(parts[1], 3))
    return sum(part.astype(jnp.float32) for part in arrived)


def gather_group(block, direct):
    if direct:
        return jnp.concatenate(line_gather(block))
    return lax.all_gather(block, "mlp", axis=0, tiled=True)


def scatter_group(rows, direct):
    if direct:
        return line_scatter(jnp.split(rows, 4))
    return lax.psum_scatter(rows, "mlp", scatter_dimension=0, tiled=True).astype(jnp.float32)


def after(value, *events):
    return lax.optimization_barrier((value, *events))[0]


def both_cores(rows, rows_x):
    return jnp.concatenate([rows, exchange(rows, "core"), rows_x, exchange(rows_x, "core")])


def shards(
    layer_input,
    request_lengths,
    request_adapter,
    slot_adapter_index,
    query_weight,
    key_weight,
    value_weight,
    output_weight,
    query_norm_gain,
    key_norm_gain,
    query_down_factors,
    value_down_factors,
    query_up_factors,
    value_up_factors,
    attention_norm_gain,
    feedforward_norm_gain,
    gate_weight,
    up_weight,
    down_weight_transposed,
):
    tok_dev = layer_input.shape[0]
    tok_group = tok_dev * lax.axis_size("mlp")
    window = tok_group * 3 // 8
    heads_local = query_weight.shape[1] // HEAD_SIZE
    direct = [lax.axis_size(axis) for axis in (*REQ, "mlp")] == [2, 2, 2, 4]
    places = jnp.arange(tok_group, dtype=jnp.int32)
    if direct:
        places = (places + lax.axis_index("mlp") * tok_dev) % tok_group
    request, position, token_slot = layout(
        request_lengths[0], request_adapter[0], slot_adapter_index, places
    )
    gate_rows, up_rows, down_rows = gate_weight.T, up_weight.T, down_weight_transposed.T
    if direct:
        gate_x = exchange(gate_rows, "x")
        half = down_rows.shape[1] // 2
        y = lax.axis_index("y")
        near = lax.dynamic_slice_in_dim(down_rows, y * half, half, axis=1)
        far = exchange(lax.dynamic_slice_in_dim(down_rows, (1 - y) * half, half, axis=1), "y")
    group_token_rows = gather_group(layer_input, direct)
    columns = jnp.arange(ADAPTER_SLOTS * ADAPTER_RANK, dtype=jnp.int32) // ADAPTER_RANK
    slot_match_mask = (columns[None, :] == token_slot[:, None]).astype(jnp.bfloat16)
    query_reduced = (
        jnp.dot(group_token_rows, query_down_factors, preferred_element_type=jnp.float32).astype(
            jnp.bfloat16
        )
        * slot_match_mask
    )
    value_reduced = (
        jnp.dot(group_token_rows, value_down_factors, preferred_element_type=jnp.float32).astype(
            jnp.bfloat16
        )
        * slot_match_mask
    )
    query_before_norm = jnp.dot(
        group_token_rows, query_weight, preferred_element_type=jnp.float32
    ) + adapter_scale * jnp.dot(query_reduced, query_up_factors, preferred_element_type=jnp.float32)
    key_pre = jnp.dot(group_token_rows, key_weight, preferred_element_type=jnp.float32)
    value_before_adapter = jnp.dot(
        group_token_rows, value_weight, preferred_element_type=jnp.float32
    ) + adapter_scale * jnp.dot(value_reduced, value_up_factors, preferred_element_type=jnp.float32)
    queries = rotary(
        rms_scale(query_before_norm.reshape(tok_group, heads_local, HEAD_SIZE))
        * query_norm_gain.reshape(heads_local, HEAD_SIZE),
        position,
    ).astype(jnp.bfloat16)
    key_heads = rotary(
        rms_scale(key_pre.reshape(tok_group, heads_local, HEAD_SIZE))
        * key_norm_gain.reshape(heads_local, HEAD_SIZE),
        position,
    ).astype(jnp.bfloat16)
    value_heads = value_before_adapter.astype(jnp.bfloat16).reshape(
        tok_group, heads_local, HEAD_SIZE
    )
    context = attention(queries, key_heads, value_heads, request, position, window).reshape(
        tok_group, heads_local * HEAD_SIZE
    )
    if direct:
        context = after(context, gate_x, far)
        up_x = exchange(after(up_rows, gate_x), "x")
    attn_own = scatter_group(
        jnp.dot(context, output_weight, preferred_element_type=jnp.float32).astype(jnp.bfloat16),
        direct,
    )
    if direct:
        attn_own = after(attn_own, up_x)
        near_x = exchange(after(near, up_x), "x")
        far_x = exchange(after(far, up_x), "x")
    residual_own = (
        layer_input.astype(jnp.float32) + rms_scale(attn_own) * attention_norm_gain
    ).astype(jnp.bfloat16)
    if direct:
        line = line_gather(residual_own)
        other = [exchange(block, "y") for block in line]
        states = after(jnp.concatenate(line + other), near_x, far_x)
        hidden = hidden_units(states, both_cores(gate_rows, gate_x), both_cores(up_rows, up_x))
        hidden_other = jnp.concatenate(
            [exchange(hidden[tok_group:], "y"), exchange(hidden[:tok_group], "y")]
        )
        part = jnp.dot(hidden, both_cores(near, near_x), preferred_element_type=jnp.float32)
        part = part + jnp.dot(
            hidden_other, both_cores(far, far_x), preferred_element_type=jnp.float32
        )
        part = part.astype(jnp.bfloat16).reshape(2, 4, tok_dev, -1)
        summed = line_scatter([part[:, k] for k in range(4)])
        own_half = summed[0]
        other_half = exchange(summed[1].astype(jnp.bfloat16), "y").astype(jnp.float32)
        upper = lax.axis_index("y") == 1
        mlp_own = jnp.concatenate(
            [jnp.where(upper, other_half, own_half), jnp.where(upper, own_half, other_half)], axis=1
        )
    else:
        gate_rows, up_rows, down_rows = (
            lax.all_gather(rows, REQ, axis=0, tiled=True) for rows in (gate_rows, up_rows, down_rows)
        )
        hidden = hidden_units(gather_group(residual_own, direct), gate_rows, up_rows)
        part = jnp.dot(hidden, down_rows, preferred_element_type=jnp.float32)
        mlp_own = scatter_group(part.astype(jnp.bfloat16), direct)
    return (residual_own.astype(jnp.float32) + rms_scale(mlp_own) * feedforward_norm_gain).astype(
        jnp.bfloat16
    )


def solution(mesh):
    req, mlp = mesh.devices.shape
    side = math.isqrt(req // 2)
    fine = Mesh(mesh.devices.reshape(req // 2 // side, side, 2, mlp), ("y", "x", "core", "mlp"))
    return jax.shard_map(
        shards,
        mesh=fine,
        in_specs=(
            P((*REQ, "mlp"), None),
            P(REQ, None),
            P(REQ, None),
            P(),
            P(None, "mlp"),
            P(None, "mlp"),
            P(None, "mlp"),
            P("mlp", None),
            P("mlp"),
            P("mlp"),
            P(),
            P(),
            P(None, "mlp"),
            P(None, "mlp"),
            P(),
            P(),
            P(None, (*REQ, "mlp")),
            P(None, (*REQ, "mlp")),
            P(None, (*REQ, "mlp")),
        ),
        out_specs=P((*REQ, "mlp"), None),
        check_vma=False,
    )
```

```python
import math

import jax
import jax.numpy as jnp
from jax import lax
from jax.sharding import Mesh, PartitionSpec as P

HEAD_SIZE = 128
ADAPTER_RANK = 16
ADAPTER_SLOTS = 8
SINKS = 4
REQ = ("y", "x", "core")


epsilon = 1e-06
adapter_scale = 0.5
rope_theta = 500000.0


def rms_scale(inputs):
    return inputs * lax.rsqrt(jnp.mean(inputs * inputs, axis=-1, keepdims=True) + epsilon)


def rotary(inputs, position):
    half_dim = inputs.shape[-1] // 2
    exponent = jnp.arange(half_dim, dtype=jnp.float32) * (2.0 / inputs.shape[-1])
    frequency = rope_theta ** (-exponent)
    angles = position.astype(jnp.float32)[:, None] * frequency[None, :]
    cosine = jnp.cos(angles)[:, None, :]
    sine_part = jnp.sin(angles)[:, None, :]
    first_half = inputs[..., :half_dim]
    second = inputs[..., half_dim:]
    return jnp.concatenate(
        [first_half * cosine - second * sine_part, second * cosine + first_half * sine_part],
        axis=-1,
    )


def layout(lengths, adapters, slot_adapter_index, places):
    req_ends = jnp.cumsum(lengths)
    starts = req_ends - lengths
    member = ((places[:, None] >= starts[None, :]) & (places[:, None] < req_ends[None, :])).astype(
        jnp.int32
    )
    request = jnp.sum(member * jnp.arange(lengths.shape[0], dtype=jnp.int32)[None, :], axis=1)
    position = places - jnp.sum(member * starts[None, :], axis=1)
    chosen = jnp.sum(member * adapters[None, :], axis=1)
    slot_ids = jnp.arange(slot_adapter_index.shape[0], dtype=jnp.int32)
    token_slot = jnp.sum(
        (chosen[:, None] == slot_adapter_index[None, :]).astype(jnp.int32) * slot_ids[None, :],
        axis=1,
    )
    return (request, position, token_slot)


def attention(queries, key_heads, value_heads, request, position, window):
    scores = jnp.einsum(
        "qhd,khd->hqk", queries, key_heads, preferred_element_type=jnp.float32
    ) * HEAD_SIZE ** (-0.5)
    distance = position[:, None] - position[None, :]
    allowed = (
        (request[:, None] == request[None, :])
        & (distance >= 0)
        & ((distance < window) | (position[None, :] < SINKS))
    )
    scores = jnp.where(allowed[None, :, :], scores, -1e30)
    row_peak = jnp.max(scores, axis=-1, keepdims=True)
    weights = jnp.exp(scores - row_peak)
    weights = (weights / jnp.sum(weights, axis=-1, keepdims=True)).astype(jnp.bfloat16)
    context = jnp.einsum("hqk,khd->qhd", weights, value_heads, preferred_element_type=jnp.float32)
    return context.astype(jnp.bfloat16)


def hidden_units(states, gate_rows, up_rows):
    contract = (((1,), (1,)), ((), ()))
    gate_act = lax.dot_general(states, gate_rows, contract, preferred_element_type=jnp.float32)
    up_act = lax.dot_general(states, up_rows, contract, preferred_element_type=jnp.float32)
    return (jax.nn.silu(gate_act) * up_act).astype(jnp.bfloat16)


def exchange(block, axis):
    return lax.ppermute(block, axis, [(0, 1), (1, 0)])


def shift(block, hops):
    return lax.ppermute(block, "mlp", [((k + hops) % 4, k) for k in range(4)])


def line_gather(block):
    across = shift(block, 2)
    return [block, shift(block, 1), across, shift(block, 3)]


def line_scatter(parts):
    across = shift(parts[2], 2)
    arrived = (parts[0], shift(parts[3], 1), across, shift(parts[1], 3))
    return sum(part.astype(jnp.float32) for part in arrived)


def line_relay(block, beside):
    index = lax.axis_index("mlp")
    end = (index == 0) | (index == 3)
    other, fetched = [exchange(block, "y")], [exchange(beside[0], "x")]
    from_right = lax.ppermute(block, "mlp", [(1, 0), (2, 1), (3, 2)])
    from_left = lax.ppermute(block, "mlp", [(0, 1), (1, 2), (2, 3)])
    from_right, from_left, fetched[0], beside[1] = together(
        from_right, from_left, fetched[0], beside[1]
    )
    first = jnp.where(index < 2, from_right, from_left)
    other.append(exchange(first, "y"))
    fetched.append(exchange(beside[1], "x"))
    across = jnp.where(
        index < 2,
        lax.ppermute(from_right, "mlp", [(1, 0), (2, 1)]),
        lax.ppermute(from_left, "mlp", [(1, 2), (2, 3)]),
    )
    across, fetched[1], other[0], beside[2] = together(across, fetched[1], other[0], beside[2])
    second = jnp.where(end, across, jnp.where(index == 1, from_left, from_right))
    other.append(exchange(second, "y"))
    fetched.append(exchange(beside[2], "x"))
    last = lax.ppermute(across, "mlp", [(1, 0), (2, 3)])
    last, fetched[2], other[1], beside[3] = together(last, fetched[2], other[1], beside[3])
    third = jnp.where(end, last, across)
    other.append(exchange(third, "y"))
    fetched.append(exchange(beside[3], "x"))
    return [block, *by_distance(first, second, third), other[0], *by_distance(*other[1:])], fetched


def by_distance(first, second, third):
    index = lax.axis_index("mlp")
    return [
        jnp.where(index < 2, first, jnp.where(index == 2, second, third)),
        jnp.where((index == 0) | (index == 3), second, third),
        jnp.where(index > 1, first, jnp.where(index == 1, second, third)),
    ]


def gather_group(block, direct):
    if direct:
        return jnp.concatenate(line_gather(block))
    return lax.all_gather(block, "mlp", axis=0, tiled=True)


def scatter_group(rows, direct):
    if direct:
        return line_scatter(jnp.split(rows, 4))
    return lax.psum_scatter(rows, "mlp", scatter_dimension=0, tiled=True).astype(jnp.float32)


def together(*values):
    return lax.optimization_barrier(values)


def both_cores(rows, rows_x):
    return jnp.concatenate([rows, exchange(rows, "core"), rows_x, exchange(rows_x, "core")])


def shards(
    layer_input,
    request_lengths,
    request_adapter,
    slot_adapter_index,
    query_weight,
    key_weight,
    value_weight,
    output_weight,
    query_norm_gain,
    key_norm_gain,
    query_down_factors,
    value_down_factors,
    query_up_factors,
    value_up_factors,
    attention_norm_gain,
    feedforward_norm_gain,
    gate_weight,
    up_weight,
    down_weight_transposed,
):
    tok_dev = layer_input.shape[0]
    tok_group = tok_dev * lax.axis_size("mlp")
    window = tok_group * 3 // 8
    heads_local = query_weight.shape[1] // HEAD_SIZE
    direct = [lax.axis_size(axis) for axis in (*REQ, "mlp")] == [2, 2, 2, 4]
    places = jnp.arange(tok_group, dtype=jnp.int32)
    if direct:
        places = (places + lax.axis_index("mlp") * tok_dev) % tok_group
    request, position, token_slot = layout(
        request_lengths[0], request_adapter[0], slot_adapter_index, places
    )
    gate_rows, up_rows, down_rows = gate_weight.T, up_weight.T, down_weight_transposed.T
    if direct:
        gate_x = exchange(gate_rows, "x")
        half = down_rows.shape[1] // 2
        y = lax.axis_index("y")
    group_token_rows = gather_group(layer_input, direct)
    columns = jnp.arange(ADAPTER_SLOTS * ADAPTER_RANK, dtype=jnp.int32) // ADAPTER_RANK
    slot_match_mask = (columns[None, :] == token_slot[:, None]).astype(jnp.bfloat16)
    query_reduced = (
        jnp.dot(group_token_rows, query_down_factors, preferred_element_type=jnp.float32).astype(
            jnp.bfloat16
        )
        * slot_match_mask
    )
    value_reduced = (
        jnp.dot(group_token_rows, value_down_factors, preferred_element_type=jnp.float32).astype(
            jnp.bfloat16
        )
        * slot_match_mask
    )
    query_before_norm = jnp.dot(
        group_token_rows, query_weight, preferred_element_type=jnp.float32
    ) + adapter_scale * jnp.dot(query_reduced, query_up_factors, preferred_element_type=jnp.float32)
    key_pre = jnp.dot(group_token_rows, key_weight, preferred_element_type=jnp.float32)
    value_before_adapter = jnp.dot(
        group_token_rows, value_weight, preferred_element_type=jnp.float32
    ) + adapter_scale * jnp.dot(value_reduced, value_up_factors, preferred_element_type=jnp.float32)
    queries = rotary(
        rms_scale(query_before_norm.reshape(tok_group, heads_local, HEAD_SIZE))
        * query_norm_gain.reshape(heads_local, HEAD_SIZE),
        position,
    ).astype(jnp.bfloat16)
    key_heads = rotary(
        rms_scale(key_pre.reshape(tok_group, heads_local, HEAD_SIZE))
        * key_norm_gain.reshape(heads_local, HEAD_SIZE),
        position,
    ).astype(jnp.bfloat16)
    value_heads = value_before_adapter.astype(jnp.bfloat16).reshape(
        tok_group, heads_local, HEAD_SIZE
    )
    context = attention(queries, key_heads, value_heads, request, position, window).reshape(
        tok_group, heads_local * HEAD_SIZE
    )
    if direct:
        context, gate_x, down_rows, up_rows_late = together(context, gate_x, down_rows, up_rows)
        near = lax.dynamic_slice_in_dim(down_rows, y * half, half, axis=1)
        far = exchange(lax.dynamic_slice_in_dim(down_rows, (1 - y) * half, half, axis=1), "y")
        up_x = exchange(up_rows_late, "x")
    attn_own = scatter_group(
        jnp.dot(context, output_weight, preferred_element_type=jnp.float32).astype(jnp.bfloat16),
        direct,
    )
    if direct:
        attn_own, near, far, up_x = together(attn_own, near, far, up_x)
    residual_own = (
        layer_input.astype(jnp.float32) + rms_scale(attn_own) * attention_norm_gain
    ).astype(jnp.bfloat16)
    if direct:
        blocks, fetched = line_relay(residual_own, [*jnp.split(near, 2), *jnp.split(far, 2)])
        states = jnp.concatenate(blocks)
        near_x, far_x = jnp.concatenate(fetched[:2]), jnp.concatenate(fetched[2:])
        hidden = hidden_units(states, both_cores(gate_rows, gate_x), both_cores(up_rows, up_x))
        hidden_other = jnp.concatenate(
            [exchange(hidden[tok_group:], "y"), exchange(hidden[:tok_group], "y")]
        )
        part = jnp.dot(hidden, both_cores(near, near_x), preferred_element_type=jnp.float32)
        part = part + jnp.dot(
            hidden_other, both_cores(far, far_x), preferred_element_type=jnp.float32
        )
        part = part.astype(jnp.bfloat16).reshape(2, 4, tok_dev, -1)
        summed = line_scatter([part[:, k] for k in range(4)])
        own_half = summed[0]
        other_half = exchange(summed[1].astype(jnp.bfloat16), "y").astype(jnp.float32)
        upper = lax.axis_index("y") == 1
        mlp_own = jnp.concatenate(
            [jnp.where(upper, other_half, own_half), jnp.where(upper, own_half, other_half)], axis=1
        )
    else:
        gate_rows, up_rows, down_rows = (
            lax.all_gather(rows, REQ, axis=0, tiled=True) for rows in (gate_rows, up_rows, down_rows)
        )
        hidden = hidden_units(gather_group(residual_own, direct), gate_rows, up_rows)
        part = jnp.dot(hidden, down_rows, preferred_element_type=jnp.float32)
        mlp_own = scatter_group(part.astype(jnp.bfloat16), direct)
    return (residual_own.astype(jnp.float32) + rms_scale(mlp_own) * feedforward_norm_gain).astype(
        jnp.bfloat16
    )


def solution(mesh):
    req, mlp = mesh.devices.shape
    side = math.isqrt(req // 2)
    fine = Mesh(mesh.devices.reshape(req // 2 // side, side, 2, mlp), ("y", "x", "core", "mlp"))
    return jax.shard_map(
        shards,
        mesh=fine,
        in_specs=(
            P((*REQ, "mlp"), None),
            P(REQ, None),
            P(REQ, None),
            P(),
            P(None, "mlp"),
            P(None, "mlp"),
            P(None, "mlp"),
            P("mlp", None),
            P("mlp"),
            P("mlp"),
            P(),
            P(),
            P(None, "mlp"),
            P(None, "mlp"),
            P(),
            P(),
            P(None, (*REQ, "mlp")),
            P(None, (*REQ, "mlp")),
            P(None, (*REQ, "mlp")),
        ),
        out_specs=P((*REQ, "mlp"), None),
        check_vma=False,
    )
```

```python
import math

import jax
import jax.numpy as jnp
from jax import lax
from jax.experimental import pallas as pl
from jax.experimental.pallas import tpu as pltpu
from jax.sharding import Mesh, PartitionSpec as P

HEAD_SIZE = 128
ADAPTER_RANK = 16
ADAPTER_SLOTS = 8
SINKS = 4
REQ = ("y", "x", "core")


epsilon = 1e-06
adapter_scale = 0.5
rope_theta = 500000.0


def rms_scale(inputs):
    return inputs * lax.rsqrt(jnp.mean(inputs * inputs, axis=-1, keepdims=True) + epsilon)


def rotary_angles(position):
    exponent = jnp.arange(HEAD_SIZE // 2, dtype=jnp.float32) * (2.0 / HEAD_SIZE)
    frequency = rope_theta ** (-exponent)
    return position.astype(jnp.float32)[:, None] * frequency[None, :]


def rotary(inputs, position):
    half_dim = inputs.shape[-1] // 2
    angles = rotary_angles(position)
    cosine = jnp.cos(angles)[:, None, :]
    sine_part = jnp.sin(angles)[:, None, :]
    first_half = inputs[..., :half_dim]
    second = inputs[..., half_dim:]
    return jnp.concatenate(
        [first_half * cosine - second * sine_part, second * cosine + first_half * sine_part],
        axis=-1,
    )


def layout(lengths, adapters, slot_adapter_index, places):
    req_ends = jnp.cumsum(lengths)
    starts = req_ends - lengths
    member = ((places[:, None] >= starts[None, :]) & (places[:, None] < req_ends[None, :])).astype(
        jnp.int32
    )
    request = jnp.sum(member * jnp.arange(lengths.shape[0], dtype=jnp.int32)[None, :], axis=1)
    position = places - jnp.sum(member * starts[None, :], axis=1)
    chosen = jnp.sum(member * adapters[None, :], axis=1)
    slot_ids = jnp.arange(slot_adapter_index.shape[0], dtype=jnp.int32)
    token_slot = jnp.sum(
        (chosen[:, None] == slot_adapter_index[None, :]).astype(jnp.int32) * slot_ids[None, :],
        axis=1,
    )
    return (request, position, token_slot)


def allowed_keys(request, position, window):
    distance = position[:, None] - position[None, :]
    return (
        (request[:, None] == request[None, :])
        & (distance >= 0)
        & ((distance < window) | (position[None, :] < SINKS))
    )


def attention(queries, key_heads, value_heads, request, position, window):
    scores = jnp.einsum(
        "qhd,khd->hqk", queries, key_heads, preferred_element_type=jnp.float32
    ) * HEAD_SIZE ** (-0.5)
    allowed = allowed_keys(request, position, window)
    scores = jnp.where(allowed[None, :, :], scores, -1e30)
    row_peak = jnp.max(scores, axis=-1, keepdims=True)
    weights = jnp.exp(scores - row_peak)
    weights = (weights / jnp.sum(weights, axis=-1, keepdims=True)).astype(jnp.bfloat16)
    context = jnp.einsum("hqk,khd->qhd", weights, value_heads, preferred_element_type=jnp.float32)
    return context.astype(jnp.bfloat16)


def hidden_units(states, gate_rows, up_rows):
    contract = (((1,), (1,)), ((), ()))
    gate_act = lax.dot_general(states, gate_rows, contract, preferred_element_type=jnp.float32)
    up_act = lax.dot_general(states, up_rows, contract, preferred_element_type=jnp.float32)
    return (jax.nn.silu(gate_act) * up_act).astype(jnp.bfloat16)


def exchange(block, axis):
    return lax.ppermute(block, axis, [(0, 1), (1, 0)])


def shift(block, hops):
    return lax.ppermute(block, "mlp", [((k + hops) % 4, k) for k in range(4)])


def line_gather(block):
    across = shift(block, 2)
    return [block, shift(block, 1), across, shift(block, 3)]


def line_scatter(parts):
    across = shift(parts[2], 2)
    arrived = (parts[0], shift(parts[3], 1), across, shift(parts[1], 3))
    return sum(part.astype(jnp.float32) for part in arrived)


def together(*values):
    return lax.optimization_barrier(values)


def both_cores(rows, rows_x):
    return jnp.concatenate([rows, exchange(rows, "core"), rows_x, exchange(rows_x, "core")])


def in_vmem(*arrays):
    return [pltpu.with_memory_space_constraint(array, pltpu.VMEM) for array in arrays]


def vmem_call(kernel, outs, scratch, operands, vmem_mib):
    whole = pl.BlockSpec(memory_space=pltpu.VMEM)
    return pl.pallas_call(
        kernel,
        out_shape=outs,
        in_specs=[whole] * len(operands),
        out_specs=[whole] * len(outs),
        scratch_shapes=scratch,
        compiler_params=pltpu.CompilerParams(vmem_limit_bytes=vmem_mib << 20),
        cost_estimate=pl.CostEstimate(flops=1 << 20, bytes_accessed=1 << 20, transcendentals=0),
    )(*operands)


NT = (((1,), (1,)), ((), ()))


def attention_kernel(
    block_0,
    block_1,
    block_2,
    block_3,
    query_weight,
    key_weight,
    value_weight,
    output_weight,
    query_down,
    value_down,
    query_up,
    value_up,
    query_gain,
    key_gain,
    cosine,
    sine,
    slot_mask,
    allowed,
    out_0,
    out_1,
    out_2,
    out_3,
    rows,
    context,
):
    tok_dev = block_0.shape[0]
    for k, block in enumerate((block_0, block_1, block_2, block_3)):
        rows[k * tok_dev : (k + 1) * tok_dev, :] = block[...]

    def project(weight):
        return jnp.dot(rows[...], weight[...], preferred_element_type=jnp.float32)

    def adapted(weight, down, up):
        low = project(down).astype(jnp.bfloat16) * slot_mask[...]
        return project(weight) + adapter_scale * jnp.dot(
            low, up[...], preferred_element_type=jnp.float32
        )

    def heads(inputs, gain):
        inputs = rms_scale(inputs) * gain
        turned = pltpu.roll(inputs, HEAD_SIZE // 2, 1)
        return (inputs * cosine[...] + turned * sine[...]).astype(jnp.bfloat16)

    queries = adapted(query_weight, query_down, query_up)
    keys = project(key_weight)
    values = adapted(value_weight, value_down, value_up).astype(jnp.bfloat16)
    for start in range(0, queries.shape[1], HEAD_SIZE):
        at = slice(start, start + HEAD_SIZE)
        scores = lax.dot_general(
            heads(queries[:, at], query_gain[:, at]),
            heads(keys[:, at], key_gain[:, at]),
            NT,
            preferred_element_type=jnp.float32,
        ) * HEAD_SIZE ** (-0.5)
        scores = jnp.where(allowed[...] > 0, scores, -1e30)
        weights = jnp.exp(scores - jnp.max(scores, axis=-1, keepdims=True))
        weights = (weights / jnp.sum(weights, axis=-1, keepdims=True)).astype(jnp.bfloat16)
        context[:, at] = jnp.dot(
            weights, values[:, at], preferred_element_type=jnp.float32
        ).astype(jnp.bfloat16)
    step = 1024
    for start in range(0, output_weight.shape[1], step):
        at = slice(start, start + step)
        part = jnp.dot(context[...], output_weight[:, at], preferred_element_type=jnp.float32)
        part = part.astype(jnp.bfloat16)
        for k, out in enumerate((out_0, out_1, out_2, out_3)):
            out[:, at] = part[k * tok_dev : (k + 1) * tok_dev]


def hidden_kernel(states, gate_rows, up_rows, hidden_own, hidden_other):
    half = hidden_own.shape[0]
    step = 256
    for start in range(0, gate_rows.shape[0], step):
        at = slice(start, start + step)
        gate_act = lax.dot_general(
            states[...], gate_rows[at, :], NT, preferred_element_type=jnp.float32
        )
        up_act = lax.dot_general(
            states[...], up_rows[at, :], NT, preferred_element_type=jnp.float32
        )
        hidden = (gate_act / (1.0 + jnp.exp(-gate_act)) * up_act).astype(jnp.bfloat16)
        hidden_own[:, at] = hidden[:half]
        hidden_other[:, at] = hidden[half:]


def down_kernel(own, other, far_own, far_other, near_rows, far_rows, out_0, out_1, out_2, out_3):
    tok_dev = out_0.shape[0] // 2
    step = 512
    for start in range(0, near_rows.shape[1], step):
        at = slice(start, start + step)
        for side, (near, far) in enumerate(((own, far_own), (other, far_other))):
            part = jnp.dot(near[...], near_rows[:, at], preferred_element_type=jnp.float32)
            part += jnp.dot(far[...], far_rows[:, at], preferred_element_type=jnp.float32)
            part = part.astype(jnp.bfloat16)
            for k, out in enumerate((out_0, out_1, out_2, out_3)):
                out[side * tok_dev : (side + 1) * tok_dev, at] = part[
                    k * tok_dev : (k + 1) * tok_dev
                ]


def add_normed(base, added, gain):
    return (base.astype(jnp.float32) + rms_scale(added) * gain).astype(jnp.bfloat16)


def layer_direct(
    layer_input, angles, slot_mask, allowed, projections, adapters, head_gains, gains, ffn_rows
):
    tok_dev, width = layer_input.shape
    gate_rows, up_rows, down_rows = ffn_rows
    y = lax.axis_index("y")
    half = width // 2
    gate_x, up_x = exchange(gate_rows, "x"), exchange(up_rows, "x")
    cosine, sine = jnp.cos(angles), jnp.sin(angles)
    block = jax.ShapeDtypeStruct((tok_dev, width), jnp.bfloat16)
    parts = vmem_call(
        attention_kernel,
        [block] * 4,
        [
            pltpu.VMEM((4 * tok_dev, width), jnp.bfloat16),
            pltpu.VMEM((4 * tok_dev, projections[0].shape[1]), jnp.bfloat16),
        ],
        [
            *line_gather(layer_input),
            *in_vmem(*projections, *adapters[:2]),
            *adapters[2:],
            *head_gains,
            jnp.concatenate([cosine, cosine], axis=1),
            jnp.concatenate([-sine, sine], axis=1),
            slot_mask,
            allowed,
        ],
        24,
    )
    *parts, down_rows = together(*parts, down_rows)
    near = lax.dynamic_slice_in_dim(down_rows, y * half, half, axis=1)
    far = exchange(lax.dynamic_slice_in_dim(down_rows, (1 - y) * half, half, axis=1), "y")
    near_x, far_x = exchange(near, "x"), exchange(far, "x")
    attn_own, gate_x = together(line_scatter(parts), gate_x)
    residual_own = add_normed(layer_input, attn_own, gains[0])
    *line, other, up_x, near_x = together(
        *line_gather(residual_own), exchange(residual_own, "y"), up_x, near_x
    )
    *others, far_x = together(*[exchange(rows, "y") for rows in line[1:]], far_x)
    states = jnp.concatenate([*line, other, *others])
    group = jax.ShapeDtypeStruct((4 * tok_dev, 4 * gate_rows.shape[0]), jnp.bfloat16)
    hidden_own, hidden_other = vmem_call(
        hidden_kernel,
        [group] * 2,
        [],
        [states, *in_vmem(both_cores(gate_rows, gate_x), both_cores(up_rows, up_x))],
        24,
    )
    parts = vmem_call(
        down_kernel,
        [jax.ShapeDtypeStruct((2 * tok_dev, half), jnp.bfloat16)] * 4,
        [],
        [
            hidden_own,
            hidden_other,
            exchange(hidden_other, "y"),
            exchange(hidden_own, "y"),
            *in_vmem(both_cores(near, near_x), both_cores(far, far_x)),
        ],
        24,
    )
    summed = line_scatter(parts)
    own_half = summed[:tok_dev]
    other_half = exchange(summed[tok_dev:].astype(jnp.bfloat16), "y").astype(jnp.float32)
    mlp_own = jnp.concatenate(
        [jnp.where(y == 1, other_half, own_half), jnp.where(y == 1, own_half, other_half)], axis=1
    )
    return add_normed(residual_own, mlp_own, gains[1])


def shards(
    layer_input,
    request_lengths,
    request_adapter,
    slot_adapter_index,
    query_weight,
    key_weight,
    value_weight,
    output_weight,
    query_norm_gain,
    key_norm_gain,
    query_down_factors,
    value_down_factors,
    query_up_factors,
    value_up_factors,
    attention_norm_gain,
    feedforward_norm_gain,
    gate_weight,
    up_weight,
    down_weight_transposed,
):
    tok_dev = layer_input.shape[0]
    tok_group = tok_dev * lax.axis_size("mlp")
    window = tok_group * 3 // 8
    heads_local = query_weight.shape[1] // HEAD_SIZE
    direct = [lax.axis_size(axis) for axis in (*REQ, "mlp")] == [2, 2, 2, 4]
    places = jnp.arange(tok_group, dtype=jnp.int32)
    if direct:
        places = (places + lax.axis_index("mlp") * tok_dev) % tok_group
    request, position, token_slot = layout(
        request_lengths[0], request_adapter[0], slot_adapter_index, places
    )
    columns = jnp.arange(ADAPTER_SLOTS * ADAPTER_RANK, dtype=jnp.int32) // ADAPTER_RANK
    slot_match_mask = (columns[None, :] == token_slot[:, None]).astype(jnp.bfloat16)
    gate_rows, up_rows, down_rows = gate_weight.T, up_weight.T, down_weight_transposed.T
    if direct:
        return layer_direct(
            layer_input,
            rotary_angles(position),
            slot_match_mask,
            allowed_keys(request, position, window).astype(jnp.float32),
            (query_weight, key_weight, value_weight, output_weight),
            (query_down_factors, value_down_factors, query_up_factors, value_up_factors),
            (query_norm_gain[None, :], key_norm_gain[None, :]),
            (attention_norm_gain, feedforward_norm_gain),
            (gate_rows, up_rows, down_rows),
        )
    group_token_rows = lax.all_gather(layer_input, "mlp", axis=0, tiled=True)
    query_reduced = (
        jnp.dot(group_token_rows, query_down_factors, preferred_element_type=jnp.float32).astype(
            jnp.bfloat16
        )
        * slot_match_mask
    )
    value_reduced = (
        jnp.dot(group_token_rows, value_down_factors, preferred_element_type=jnp.float32).astype(
            jnp.bfloat16
        )
        * slot_match_mask
    )
    query_before_norm = jnp.dot(
        group_token_rows, query_weight, preferred_element_type=jnp.float32
    ) + adapter_scale * jnp.dot(query_reduced, query_up_factors, preferred_element_type=jnp.float32)
    key_pre = jnp.dot(group_token_rows, key_weight, preferred_element_type=jnp.float32)
    value_before_adapter = jnp.dot(
        group_token_rows, value_weight, preferred_element_type=jnp.float32
    ) + adapter_scale * jnp.dot(value_reduced, value_up_factors, preferred_element_type=jnp.float32)
    queries = rotary(
        rms_scale(query_before_norm.reshape(tok_group, heads_local, HEAD_SIZE))
        * query_norm_gain.reshape(heads_local, HEAD_SIZE),
        position,
    ).astype(jnp.bfloat16)
    key_heads = rotary(
        rms_scale(key_pre.reshape(tok_group, heads_local, HEAD_SIZE))
        * key_norm_gain.reshape(heads_local, HEAD_SIZE),
        position,
    ).astype(jnp.bfloat16)
    value_heads = value_before_adapter.astype(jnp.bfloat16).reshape(
        tok_group, heads_local, HEAD_SIZE
    )
    context = attention(queries, key_heads, value_heads, request, position, window).reshape(
        tok_group, heads_local * HEAD_SIZE
    )
    attn_own = lax.psum_scatter(
        jnp.dot(context, output_weight, preferred_element_type=jnp.float32).astype(jnp.bfloat16),
        "mlp",
        scatter_dimension=0,
        tiled=True,
    ).astype(jnp.float32)
    residual_own = add_normed(layer_input, attn_own, attention_norm_gain)
    gate_rows, up_rows, down_rows = (
        lax.all_gather(rows, REQ, axis=0, tiled=True) for rows in (gate_rows, up_rows, down_rows)
    )
    hidden = hidden_units(
        lax.all_gather(residual_own, "mlp", axis=0, tiled=True), gate_rows, up_rows
    )
    part = jnp.dot(hidden, down_rows, preferred_element_type=jnp.float32)
    mlp_own = lax.psum_scatter(
        part.astype(jnp.bfloat16), "mlp", scatter_dimension=0, tiled=True
    ).astype(jnp.float32)
    return add_normed(residual_own, mlp_own, feedforward_norm_gain)


def solution(mesh):
    req, mlp = mesh.devices.shape
    side = math.isqrt(req // 2)
    fine = Mesh(mesh.devices.reshape(req // 2 // side, side, 2, mlp), ("y", "x", "core", "mlp"))
    return jax.shard_map(
        shards,
        mesh=fine,
        in_specs=(
            P((*REQ, "mlp"), None),
            P(REQ, None),
            P(REQ, None),
            P(),
            P(None, "mlp"),
            P(None, "mlp"),
            P(None, "mlp"),
            P("mlp", None),
            P("mlp"),
            P("mlp"),
            P(),
            P(),
            P(None, "mlp"),
            P(None, "mlp"),
            P(),
            P(),
            P(None, (*REQ, "mlp")),
            P(None, (*REQ, "mlp")),
            P(None, (*REQ, "mlp")),
        ),
        out_specs=P((*REQ, "mlp"), None),
        check_vma=False,
    )
```

```python
import math

import jax
import jax.numpy as jnp
from jax import lax
from jax.experimental import pallas as pl
from jax.experimental.pallas import tpu as pltpu
from jax.sharding import Mesh, PartitionSpec as P

HEAD_SIZE = 128
ADAPTER_RANK = 16
ADAPTER_SLOTS = 8
SINKS = 4
REQ = ("y", "x", "core")


epsilon = 1e-06
adapter_scale = 0.5
rope_theta = 500000.0


def rms_scale(inputs):
    return inputs * lax.rsqrt(jnp.mean(inputs * inputs, axis=-1, keepdims=True) + epsilon)


def rotary_angles(position):
    exponent = jnp.arange(HEAD_SIZE // 2, dtype=jnp.float32) * (2.0 / HEAD_SIZE)
    frequency = rope_theta ** (-exponent)
    return position.astype(jnp.float32)[:, None] * frequency[None, :]


def rotary(inputs, position):
    half_dim = inputs.shape[-1] // 2
    angles = rotary_angles(position)
    cosine = jnp.cos(angles)[:, None, :]
    sine_part = jnp.sin(angles)[:, None, :]
    first_half = inputs[..., :half_dim]
    second = inputs[..., half_dim:]
    return jnp.concatenate(
        [first_half * cosine - second * sine_part, second * cosine + first_half * sine_part],
        axis=-1,
    )


def layout(lengths, adapters, slot_adapter_index, places):
    req_ends = jnp.cumsum(lengths)
    starts = req_ends - lengths
    member = ((places[:, None] >= starts[None, :]) & (places[:, None] < req_ends[None, :])).astype(
        jnp.int32
    )
    request = jnp.sum(member * jnp.arange(lengths.shape[0], dtype=jnp.int32)[None, :], axis=1)
    position = places - jnp.sum(member * starts[None, :], axis=1)
    chosen = jnp.sum(member * adapters[None, :], axis=1)
    slot_ids = jnp.arange(slot_adapter_index.shape[0], dtype=jnp.int32)
    token_slot = jnp.sum(
        (chosen[:, None] == slot_adapter_index[None, :]).astype(jnp.int32) * slot_ids[None, :],
        axis=1,
    )
    return (request, position, token_slot)


def allowed_keys(request, position, window):
    distance = position[:, None] - position[None, :]
    return (
        (request[:, None] == request[None, :])
        & (distance >= 0)
        & ((distance < window) | (position[None, :] < SINKS))
    )


def attention(queries, key_heads, value_heads, request, position, window):
    scores = jnp.einsum(
        "qhd,khd->hqk", queries, key_heads, preferred_element_type=jnp.float32
    ) * HEAD_SIZE ** (-0.5)
    allowed = allowed_keys(request, position, window)
    scores = jnp.where(allowed[None, :, :], scores, -1e30)
    row_peak = jnp.max(scores, axis=-1, keepdims=True)
    weights = jnp.exp(scores - row_peak)
    weights = (weights / jnp.sum(weights, axis=-1, keepdims=True)).astype(jnp.bfloat16)
    context = jnp.einsum("hqk,khd->qhd", weights, value_heads, preferred_element_type=jnp.float32)
    return context.astype(jnp.bfloat16)


def hidden_units(states, gate_rows, up_rows):
    contract = (((1,), (1,)), ((), ()))
    gate_act = lax.dot_general(states, gate_rows, contract, preferred_element_type=jnp.float32)
    up_act = lax.dot_general(states, up_rows, contract, preferred_element_type=jnp.float32)
    return (jax.nn.silu(gate_act) * up_act).astype(jnp.bfloat16)


def exchange(block, axis):
    return lax.ppermute(block, axis, [(0, 1), (1, 0)])


def shift(block, hops):
    return lax.ppermute(block, "mlp", [((k + hops) % 4, k) for k in range(4)])


def line_gather(block):
    across = shift(block, 2)
    return [block, shift(block, 1), across, shift(block, 3)]


def line_scatter(parts):
    across = shift(parts[2], 2)
    arrived = (parts[0], shift(parts[3], 1), across, shift(parts[1], 3))
    return sum(part.astype(jnp.float32) for part in arrived)


def together(*values):
    return lax.optimization_barrier(values)


def four_pieces(rows, rows_x, place=lambda rows: rows):
    return [place(rows), exchange(rows, "core"), rows_x, exchange(rows_x, "core")]


def vmem_call(kernel, outs, scratch, operands, vmem_mib):
    whole = pl.BlockSpec(memory_space=pltpu.VMEM)
    return pl.pallas_call(
        kernel,
        out_shape=outs,
        in_specs=[whole] * len(operands),
        out_specs=[whole] * len(outs),
        scratch_shapes=scratch,
        compiler_params=pltpu.CompilerParams(vmem_limit_bytes=vmem_mib << 20),
        cost_estimate=pl.CostEstimate(flops=1 << 20, bytes_accessed=1 << 20, transcendentals=0),
    )(*operands)


def in_hbm(array):
    return pltpu.with_memory_space_constraint(array, pltpu.HBM)


def staged(*groups):
    arrays = [array for group in groups for array in group]

    def kernel(*refs):
        sources, targets, sems = refs[: len(arrays)], refs[len(arrays) : -1], refs[-1]
        copies = []
        for group, target in zip(groups, targets):
            start = 0
            for array in group:
                at = len(copies)
                rows = target.at[pl.ds(start, array.shape[0]), :]
                copies.append(pltpu.make_async_copy(sources[at], rows, sems.at[at]))
                copies[-1].start()
                start += array.shape[0]
        for copy in copies:
            copy.wait()

    outs = [(sum(array.shape[0] for array in group), group[0].shape[1]) for group in groups]
    size = sum(array.size * array.dtype.itemsize for array in arrays)
    return pl.pallas_call(
        kernel,
        out_shape=[pltpu.VMEM(shape, group[0].dtype) for shape, group in zip(outs, groups)],
        in_specs=[pl.BlockSpec(memory_space=pl.ANY)] * len(arrays),
        out_specs=[pl.BlockSpec(memory_space=pltpu.VMEM)] * len(groups),
        scratch_shapes=[pltpu.SemaphoreType.DMA((len(arrays),))],
        compiler_params=pltpu.CompilerParams(vmem_limit_bytes=1 << 20),
        cost_estimate=pl.CostEstimate(flops=0, bytes_accessed=2 * size, transcendentals=0),
    )(*arrays)


NT = (((1,), (1,)), ((), ()))


def attention_kernel(
    block_0,
    block_1,
    block_2,
    block_3,
    query_weight,
    key_weight,
    value_weight,
    output_weight,
    query_down,
    value_down,
    query_up,
    value_up,
    query_gain,
    key_gain,
    cosine,
    sine,
    slot_mask,
    allowed,
    out_0,
    out_1,
    out_2,
    out_3,
    rows,
    context,
):
    tok_dev = block_0.shape[0]
    for k, block in enumerate((block_0, block_1, block_2, block_3)):
        rows[k * tok_dev : (k + 1) * tok_dev, :] = block[...]

    def project(weight):
        return jnp.dot(rows[...], weight[...], preferred_element_type=jnp.float32)

    def adapted(weight, down, up):
        low = project(down).astype(jnp.bfloat16) * slot_mask[...]
        return project(weight) + adapter_scale * jnp.dot(
            low, up[...], preferred_element_type=jnp.float32
        )

    def heads(inputs, gain):
        inputs = rms_scale(inputs) * gain
        turned = pltpu.roll(inputs, HEAD_SIZE // 2, 1)
        return (inputs * cosine[...] + turned * sine[...]).astype(jnp.bfloat16)

    queries = adapted(query_weight, query_down, query_up)
    keys = project(key_weight)
    values = adapted(value_weight, value_down, value_up).astype(jnp.bfloat16)
    for start in range(0, queries.shape[1], HEAD_SIZE):
        at = slice(start, start + HEAD_SIZE)
        scores = lax.dot_general(
            heads(queries[:, at], query_gain[:, at]),
            heads(keys[:, at], key_gain[:, at]),
            NT,
            preferred_element_type=jnp.float32,
        ) * HEAD_SIZE ** (-0.5)
        scores = jnp.where(allowed[...] > 0, scores, -1e30)
        weights = jnp.exp(scores - jnp.max(scores, axis=-1, keepdims=True))
        weights = (weights / jnp.sum(weights, axis=-1, keepdims=True)).astype(jnp.bfloat16)
        context[:, at] = jnp.dot(
            weights, values[:, at], preferred_element_type=jnp.float32
        ).astype(jnp.bfloat16)
    step = 1024
    for start in range(0, output_weight.shape[1], step):
        at = slice(start, start + step)
        part = jnp.dot(context[...], output_weight[:, at], preferred_element_type=jnp.float32)
        part = part.astype(jnp.bfloat16)
        for k, out in enumerate((out_0, out_1, out_2, out_3)):
            out[:, at] = part[k * tok_dev : (k + 1) * tok_dev]


def hidden_kernel(states, gate_rows, up_rows, hidden_own, hidden_other):
    half = hidden_own.shape[0]
    step = 256
    for start in range(0, gate_rows.shape[0], step):
        at = slice(start, start + step)
        gate_act = lax.dot_general(
            states[...], gate_rows[at, :], NT, preferred_element_type=jnp.float32
        )
        up_act = lax.dot_general(
            states[...], up_rows[at, :], NT, preferred_element_type=jnp.float32
        )
        hidden = (gate_act / (1.0 + jnp.exp(-gate_act)) * up_act).astype(jnp.bfloat16)
        hidden_own[:, at] = hidden[:half]
        hidden_other[:, at] = hidden[half:]


def down_kernel(own, other, far_own, far_other, near_rows, far_rows, out_0, out_1, out_2, out_3):
    tok_dev = out_0.shape[0] // 2
    step = 512
    for start in range(0, near_rows.shape[1], step):
        at = slice(start, start + step)
        for side, (near, far) in enumerate(((own, far_own), (other, far_other))):
            part = jnp.dot(near[...], near_rows[:, at], preferred_element_type=jnp.float32)
            part += jnp.dot(far[...], far_rows[:, at], preferred_element_type=jnp.float32)
            part = part.astype(jnp.bfloat16)
            for k, out in enumerate((out_0, out_1, out_2, out_3)):
                out[side * tok_dev : (side + 1) * tok_dev, at] = part[
                    k * tok_dev : (k + 1) * tok_dev
                ]


def add_normed(base, added, gain):
    return (base.astype(jnp.float32) + rms_scale(added) * gain).astype(jnp.bfloat16)


def layer_direct(
    layer_input, angles, slot_mask, allowed, projections, adapters, head_gains, gains, ffn_rows
):
    tok_dev, width = layer_input.shape
    gate_rows, up_rows, down_rows = ffn_rows
    y = lax.axis_index("y")
    half = width // 2
    gate_x, up_x = exchange(gate_rows, "x"), exchange(up_rows, "x")
    cosine, sine = jnp.cos(angles), jnp.sin(angles)
    block = jax.ShapeDtypeStruct((tok_dev, width), jnp.bfloat16)
    *staged_rows, own_block = staged(
        *([in_hbm(array)] for array in (*projections, *adapters, *head_gains, layer_input))
    )
    parts = vmem_call(
        attention_kernel,
        [block] * 4,
        [
            pltpu.VMEM((4 * tok_dev, width), jnp.bfloat16),
            pltpu.VMEM((4 * tok_dev, projections[0].shape[1]), jnp.bfloat16),
        ],
        [
            own_block,
            *line_gather(layer_input)[1:],
            *staged_rows,
            jnp.concatenate([cosine, cosine], axis=1),
            jnp.concatenate([-sine, sine], axis=1),
            slot_mask,
            allowed,
        ],
        8,
    )
    *parts, down_rows = together(*parts, down_rows)
    near = lax.dynamic_slice_in_dim(down_rows, y * half, half, axis=1)
    far = exchange(lax.dynamic_slice_in_dim(down_rows, (1 - y) * half, half, axis=1), "y")
    near_x, far_x = exchange(near, "x"), exchange(far, "x")
    attn_own, gate_x, near, far = together(line_scatter(parts), gate_x, near, far)
    residual_own = add_normed(layer_input, attn_own, gains[0])
    *line, other = together(*line_gather(residual_own), exchange(residual_own, "y"))
    *line, gate_x, up_x, near_x = together(*line, gate_x, up_x, near_x)
    (gate_all,) = staged(four_pieces(gate_rows, gate_x, in_hbm))
    (up_all,) = staged(four_pieces(up_rows, up_x, in_hbm))
    *others, gate_all, up_all, far_x = together(
        *[exchange(rows, "y") for rows in line[1:]], gate_all, up_all, far_x
    )
    group = jax.ShapeDtypeStruct((4 * tok_dev, 4 * gate_rows.shape[0]), jnp.bfloat16)
    hidden_own, hidden_other = vmem_call(
        hidden_kernel,
        [group] * 2,
        [],
        [jnp.concatenate([*line, other, *others]), gate_all, up_all],
        8,
    )
    hidden_own, hidden_other, near_x, far_x = together(hidden_own, hidden_other, near_x, far_x)
    (near_all,) = staged(four_pieces(near, near_x))
    (far_all,) = staged(four_pieces(far, far_x))
    from_other, from_own, near_all, far_all = together(
        exchange(hidden_other, "y"), exchange(hidden_own, "y"), near_all, far_all
    )
    parts = vmem_call(
        down_kernel,
        [jax.ShapeDtypeStruct((2 * tok_dev, half), jnp.bfloat16)] * 4,
        [],
        [hidden_own, hidden_other, from_other, from_own, near_all, far_all],
        8,
    )
    summed = line_scatter(parts)
    own_half = summed[:tok_dev]
    other_half = exchange(summed[tok_dev:].astype(jnp.bfloat16), "y").astype(jnp.float32)
    mlp_own = jnp.concatenate(
        [jnp.where(y == 1, other_half, own_half), jnp.where(y == 1, own_half, other_half)], axis=1
    )
    return add_normed(residual_own, mlp_own, gains[1])


def shards(
    layer_input,
    request_lengths,
    request_adapter,
    slot_adapter_index,
    query_weight,
    key_weight,
    value_weight,
    output_weight,
    query_norm_gain,
    key_norm_gain,
    query_down_factors,
    value_down_factors,
    query_up_factors,
    value_up_factors,
    attention_norm_gain,
    feedforward_norm_gain,
    gate_weight,
    up_weight,
    down_weight_transposed,
):
    tok_dev = layer_input.shape[0]
    tok_group = tok_dev * lax.axis_size("mlp")
    window = tok_group * 3 // 8
    heads_local = query_weight.shape[1] // HEAD_SIZE
    direct = [lax.axis_size(axis) for axis in (*REQ, "mlp")] == [2, 2, 2, 4]
    places = jnp.arange(tok_group, dtype=jnp.int32)
    if direct:
        places = (places + lax.axis_index("mlp") * tok_dev) % tok_group
    request, position, token_slot = layout(
        request_lengths[0], request_adapter[0], slot_adapter_index, places
    )
    columns = jnp.arange(ADAPTER_SLOTS * ADAPTER_RANK, dtype=jnp.int32) // ADAPTER_RANK
    slot_match_mask = (columns[None, :] == token_slot[:, None]).astype(jnp.bfloat16)
    gate_rows, up_rows, down_rows = gate_weight.T, up_weight.T, down_weight_transposed.T
    if direct:
        return layer_direct(
            layer_input,
            rotary_angles(position),
            slot_match_mask,
            allowed_keys(request, position, window).astype(jnp.float32),
            (query_weight, key_weight, value_weight, output_weight),
            (query_down_factors, value_down_factors, query_up_factors, value_up_factors),
            (query_norm_gain[None, :], key_norm_gain[None, :]),
            (attention_norm_gain, feedforward_norm_gain),
            (gate_rows, up_rows, down_rows),
        )
    group_token_rows = lax.all_gather(layer_input, "mlp", axis=0, tiled=True)
    query_reduced = (
        jnp.dot(group_token_rows, query_down_factors, preferred_element_type=jnp.float32).astype(
            jnp.bfloat16
        )
        * slot_match_mask
    )
    value_reduced = (
        jnp.dot(group_token_rows, value_down_factors, preferred_element_type=jnp.float32).astype(
            jnp.bfloat16
        )
        * slot_match_mask
    )
    query_before_norm = jnp.dot(
        group_token_rows, query_weight, preferred_element_type=jnp.float32
    ) + adapter_scale * jnp.dot(query_reduced, query_up_factors, preferred_element_type=jnp.float32)
    key_pre = jnp.dot(group_token_rows, key_weight, preferred_element_type=jnp.float32)
    value_before_adapter = jnp.dot(
        group_token_rows, value_weight, preferred_element_type=jnp.float32
    ) + adapter_scale * jnp.dot(value_reduced, value_up_factors, preferred_element_type=jnp.float32)
    queries = rotary(
        rms_scale(query_before_norm.reshape(tok_group, heads_local, HEAD_SIZE))
        * query_norm_gain.reshape(heads_local, HEAD_SIZE),
        position,
    ).astype(jnp.bfloat16)
    key_heads = rotary(
        rms_scale(key_pre.reshape(tok_group, heads_local, HEAD_SIZE))
        * key_norm_gain.reshape(heads_local, HEAD_SIZE),
        position,
    ).astype(jnp.bfloat16)
    value_heads = value_before_adapter.astype(jnp.bfloat16).reshape(
        tok_group, heads_local, HEAD_SIZE
    )
    context = attention(queries, key_heads, value_heads, request, position, window).reshape(
        tok_group, heads_local * HEAD_SIZE
    )
    attn_own = lax.psum_scatter(
        jnp.dot(context, output_weight, preferred_element_type=jnp.float32).astype(jnp.bfloat16),
        "mlp",
        scatter_dimension=0,
        tiled=True,
    ).astype(jnp.float32)
    residual_own = add_normed(layer_input, attn_own, attention_norm_gain)
    gate_rows, up_rows, down_rows = (
        lax.all_gather(rows, REQ, axis=0, tiled=True) for rows in (gate_rows, up_rows, down_rows)
    )
    hidden = hidden_units(
        lax.all_gather(residual_own, "mlp", axis=0, tiled=True), gate_rows, up_rows
    )
    part = jnp.dot(hidden, down_rows, preferred_element_type=jnp.float32)
    mlp_own = lax.psum_scatter(
        part.astype(jnp.bfloat16), "mlp", scatter_dimension=0, tiled=True
    ).astype(jnp.float32)
    return add_normed(residual_own, mlp_own, feedforward_norm_gain)


def solution(mesh):
    req, mlp = mesh.devices.shape
    side = math.isqrt(req // 2)
    fine = Mesh(mesh.devices.reshape(req // 2 // side, side, 2, mlp), ("y", "x", "core", "mlp"))
    return jax.shard_map(
        shards,
        mesh=fine,
        in_specs=(
            P((*REQ, "mlp"), None),
            P(REQ, None),
            P(REQ, None),
            P(),
            P(None, "mlp"),
            P(None, "mlp"),
            P(None, "mlp"),
            P("mlp", None),
            P("mlp"),
            P("mlp"),
            P(),
            P(),
            P(None, "mlp"),
            P(None, "mlp"),
            P(),
            P(),
            P(None, (*REQ, "mlp")),
            P(None, (*REQ, "mlp")),
            P(None, (*REQ, "mlp")),
        ),
        out_specs=P((*REQ, "mlp"), None),
        check_vma=False,
    )
```

```python
import math

import jax
import jax.numpy as jnp
from jax import lax
from jax.experimental import pallas as pl
from jax.experimental.pallas import tpu as pltpu
from jax.sharding import Mesh, PartitionSpec as P

HEAD_SIZE = 128
ADAPTER_RANK = 16
ADAPTER_SLOTS = 8
SINKS = 4
REQ = ("y", "x", "core")


epsilon = 1e-06
adapter_scale = 0.5
rope_theta = 500000.0


def rms_scale(inputs):
    return inputs * lax.rsqrt(jnp.mean(inputs * inputs, axis=-1, keepdims=True) + epsilon)


def rotary_angles(position):
    exponent = jnp.arange(HEAD_SIZE // 2, dtype=jnp.float32) * (2.0 / HEAD_SIZE)
    frequency = rope_theta ** (-exponent)
    return position.astype(jnp.float32)[:, None] * frequency[None, :]


def rotary(inputs, position):
    half_dim = inputs.shape[-1] // 2
    angles = rotary_angles(position)
    cosine = jnp.cos(angles)[:, None, :]
    sine_part = jnp.sin(angles)[:, None, :]
    first_half = inputs[..., :half_dim]
    second = inputs[..., half_dim:]
    return jnp.concatenate(
        [first_half * cosine - second * sine_part, second * cosine + first_half * sine_part],
        axis=-1,
    )


def layout(lengths, adapters, slot_adapter_index, places):
    req_ends = jnp.cumsum(lengths)
    starts = req_ends - lengths
    member = ((places[:, None] >= starts[None, :]) & (places[:, None] < req_ends[None, :])).astype(
        jnp.int32
    )
    request = jnp.sum(member * jnp.arange(lengths.shape[0], dtype=jnp.int32)[None, :], axis=1)
    position = places - jnp.sum(member * starts[None, :], axis=1)
    chosen = jnp.sum(member * adapters[None, :], axis=1)
    slot_ids = jnp.arange(slot_adapter_index.shape[0], dtype=jnp.int32)
    token_slot = jnp.sum(
        (chosen[:, None] == slot_adapter_index[None, :]).astype(jnp.int32) * slot_ids[None, :],
        axis=1,
    )
    return (request, position, token_slot)


def allowed_keys(request, position, window):
    distance = position[:, None] - position[None, :]
    return (
        (request[:, None] == request[None, :])
        & (distance >= 0)
        & ((distance < window) | (position[None, :] < SINKS))
    )


def attention(queries, key_heads, value_heads, request, position, window):
    scores = jnp.einsum(
        "qhd,khd->hqk", queries, key_heads, preferred_element_type=jnp.float32
    ) * HEAD_SIZE ** (-0.5)
    allowed = allowed_keys(request, position, window)
    scores = jnp.where(allowed[None, :, :], scores, -1e30)
    row_peak = jnp.max(scores, axis=-1, keepdims=True)
    weights = jnp.exp(scores - row_peak)
    weights = (weights / jnp.sum(weights, axis=-1, keepdims=True)).astype(jnp.bfloat16)
    context = jnp.einsum("hqk,khd->qhd", weights, value_heads, preferred_element_type=jnp.float32)
    return context.astype(jnp.bfloat16)


def hidden_units(states, gate_rows, up_rows):
    contract = (((1,), (1,)), ((), ()))
    gate_act = lax.dot_general(states, gate_rows, contract, preferred_element_type=jnp.float32)
    up_act = lax.dot_general(states, up_rows, contract, preferred_element_type=jnp.float32)
    return (jax.nn.silu(gate_act) * up_act).astype(jnp.bfloat16)


def exchange(block, axis):
    return lax.ppermute(block, axis, [(0, 1), (1, 0)])


def shift(block, hops):
    return lax.ppermute(block, "mlp", [((k + hops) % 4, k) for k in range(4)])


def line_gather(block):
    copies = jnp.broadcast_to(block[None], (lax.axis_size("mlp"), *block.shape))
    return lax.all_to_all(copies, "mlp", 0, 0, tiled=True).reshape(-1, block.shape[1])


def line_scatter(parts):
    return jnp.sum(lax.all_to_all(parts, "mlp", 0, 0, tiled=True).astype(jnp.float32), axis=0)


def together(*values):
    return lax.optimization_barrier(values)


def four_pieces(rows, rows_x, place=lambda rows: rows):
    return [place(rows), exchange(rows, "core"), rows_x, exchange(rows_x, "core")]


def vmem_call(kernel, outs, scratch, operands, vmem_mib):
    whole = pl.BlockSpec(memory_space=pltpu.VMEM)
    return pl.pallas_call(
        kernel,
        out_shape=outs,
        in_specs=[whole] * len(operands),
        out_specs=[whole] * len(outs),
        scratch_shapes=scratch,
        compiler_params=pltpu.CompilerParams(vmem_limit_bytes=vmem_mib << 20),
        cost_estimate=pl.CostEstimate(flops=1 << 20, bytes_accessed=1 << 20, transcendentals=0),
    )(*operands)


def in_hbm(array):
    return pltpu.with_memory_space_constraint(array, pltpu.HBM)


def staged(*groups):
    arrays = [array for group in groups for array in group]

    def kernel(*refs):
        sources, targets, sems = refs[: len(arrays)], refs[len(arrays) : -1], refs[-1]
        copies = []
        for group, target in zip(groups, targets):
            start = 0
            for array in group:
                at = len(copies)
                rows = target.at[pl.ds(start, array.shape[0]), :]
                copies.append(pltpu.make_async_copy(sources[at], rows, sems.at[at]))
                copies[-1].start()
                start += array.shape[0]
        for copy in copies:
            copy.wait()

    outs = [(sum(array.shape[0] for array in group), group[0].shape[1]) for group in groups]
    size = sum(array.size * array.dtype.itemsize for array in arrays)
    return pl.pallas_call(
        kernel,
        out_shape=[pltpu.VMEM(shape, group[0].dtype) for shape, group in zip(outs, groups)],
        in_specs=[pl.BlockSpec(memory_space=pl.ANY)] * len(arrays),
        out_specs=[pl.BlockSpec(memory_space=pltpu.VMEM)] * len(groups),
        scratch_shapes=[pltpu.SemaphoreType.DMA((len(arrays),))],
        compiler_params=pltpu.CompilerParams(vmem_limit_bytes=1 << 20),
        cost_estimate=pl.CostEstimate(flops=0, bytes_accessed=2 * size, transcendentals=0),
    )(*arrays)


NT = (((1,), (1,)), ((), ()))


def attention_kernel(
    block_0,
    block_1,
    block_2,
    block_3,
    query_weight,
    key_weight,
    value_weight,
    output_weight,
    query_down,
    value_down,
    query_up,
    value_up,
    query_gain,
    key_gain,
    cosine,
    sine,
    slot_mask,
    allowed,
    out,
    rows,
    context,
):
    tok_dev = out.shape[1]
    for k, block in enumerate((block_0, block_1, block_2, block_3)):
        rows[k * tok_dev : (k + 1) * tok_dev, :] = block[...]

    def project(weight):
        return jnp.dot(rows[...], weight[...], preferred_element_type=jnp.float32)

    def adapted(weight, down, up):
        low = project(down).astype(jnp.bfloat16) * slot_mask[...]
        return project(weight) + adapter_scale * jnp.dot(
            low, up[...], preferred_element_type=jnp.float32
        )

    def heads(inputs, gain):
        inputs = rms_scale(inputs) * gain
        turned = pltpu.roll(inputs, HEAD_SIZE // 2, 1)
        return (inputs * cosine[...] + turned * sine[...]).astype(jnp.bfloat16)

    queries = adapted(query_weight, query_down, query_up)
    keys = project(key_weight)
    values = adapted(value_weight, value_down, value_up).astype(jnp.bfloat16)
    for start in range(0, queries.shape[1], HEAD_SIZE):
        at = slice(start, start + HEAD_SIZE)
        scores = lax.dot_general(
            heads(queries[:, at], query_gain[:, at]),
            heads(keys[:, at], key_gain[:, at]),
            NT,
            preferred_element_type=jnp.float32,
        ) * HEAD_SIZE ** (-0.5)
        scores = jnp.where(allowed[...] > 0, scores, -1e30)
        weights = jnp.exp(scores - jnp.max(scores, axis=-1, keepdims=True))
        weights = (weights / jnp.sum(weights, axis=-1, keepdims=True)).astype(jnp.bfloat16)
        context[:, at] = jnp.dot(
            weights, values[:, at], preferred_element_type=jnp.float32
        ).astype(jnp.bfloat16)
    step = 1024
    for start in range(0, output_weight.shape[1], step):
        at = slice(start, start + step)
        part = jnp.dot(context[...], output_weight[:, at], preferred_element_type=jnp.float32)
        part = part.astype(jnp.bfloat16)
        for k in range(4):
            owner = lax.rem(lax.axis_index("mlp") + k, 4)
            out[owner, :, at] = part[k * tok_dev : (k + 1) * tok_dev]


def hidden_kernel(states, gate_rows, up_rows, hidden_own, hidden_other):
    half = hidden_own.shape[0]
    step = 256
    for start in range(0, gate_rows.shape[0], step):
        at = slice(start, start + step)
        gate_act = lax.dot_general(
            states[...], gate_rows[at, :], NT, preferred_element_type=jnp.float32
        )
        up_act = lax.dot_general(
            states[...], up_rows[at, :], NT, preferred_element_type=jnp.float32
        )
        hidden = (gate_act / (1.0 + jnp.exp(-gate_act)) * up_act).astype(jnp.bfloat16)
        hidden_own[:, at] = hidden[:half]
        hidden_other[:, at] = hidden[half:]


def down_kernel(own, other, far_own, far_other, near_rows, far_rows, out):
    tok_dev = out.shape[1] // 2
    step = 512
    for start in range(0, near_rows.shape[1], step):
        at = slice(start, start + step)
        for side, (near, far) in enumerate(((own, far_own), (other, far_other))):
            part = jnp.dot(near[...], near_rows[:, at], preferred_element_type=jnp.float32)
            part += jnp.dot(far[...], far_rows[:, at], preferred_element_type=jnp.float32)
            part = part.astype(jnp.bfloat16)
            for k in range(out.shape[0]):
                out[k, side * tok_dev : (side + 1) * tok_dev, at] = part[
                    k * tok_dev : (k + 1) * tok_dev
                ]


def add_normed(base, added, gain):
    return (base.astype(jnp.float32) + rms_scale(added) * gain).astype(jnp.bfloat16)


def layer_direct(
    layer_input, angles, slot_mask, allowed, projections, adapters, head_gains, gains, ffn_rows
):
    tok_dev, width = layer_input.shape
    gate_rows, up_rows, down_rows = ffn_rows
    y = lax.axis_index("y")
    half = width // 2
    gate_x, up_x = exchange(gate_rows, "x"), exchange(up_rows, "x")
    cosine, sine = jnp.cos(angles), jnp.sin(angles)
    staged_rows = staged(*([in_hbm(array)] for array in (*projections, *adapters, *head_gains)))
    blocks = [layer_input, *(shift(layer_input, hops) for hops in (1, 2, 3))]
    (parts,) = vmem_call(
        attention_kernel,
        [jax.ShapeDtypeStruct((4, tok_dev, width), jnp.bfloat16)],
        [
            pltpu.VMEM((4 * tok_dev, width), jnp.bfloat16),
            pltpu.VMEM((4 * tok_dev, projections[0].shape[1]), jnp.bfloat16),
        ],
        [
            *blocks,
            *staged_rows,
            jnp.concatenate([cosine, cosine], axis=1),
            jnp.concatenate([-sine, sine], axis=1),
            slot_mask,
            allowed,
        ],
        8,
    )
    parts, down_rows = together(parts, down_rows)
    near = lax.dynamic_slice_in_dim(down_rows, y * half, half, axis=1)
    far = exchange(lax.dynamic_slice_in_dim(down_rows, (1 - y) * half, half, axis=1), "y")
    near_x, far_x = exchange(near, "x"), exchange(far, "x")
    attn_own, near, far = together(line_scatter(parts), near, far)
    residual_own = add_normed(layer_input, attn_own, gains[0])
    line = line_gather(residual_own)
    line, gate_x, up_x, near_x = together(line, gate_x, up_x, near_x)
    (gate_all,) = staged(four_pieces(gate_rows, gate_x, in_hbm))
    (up_all,) = staged(four_pieces(up_rows, up_x, in_hbm))
    others, gate_all, up_all, far_x = together(exchange(line, "y"), gate_all, up_all, far_x)
    group = jax.ShapeDtypeStruct((4 * tok_dev, 4 * gate_rows.shape[0]), jnp.bfloat16)
    hidden_own, hidden_other = vmem_call(
        hidden_kernel,
        [group] * 2,
        [],
        [jnp.concatenate([line, others]), gate_all, up_all],
        8,
    )
    hidden_own, hidden_other, near_x, far_x = together(hidden_own, hidden_other, near_x, far_x)
    (near_all,) = staged(four_pieces(near, near_x))
    (far_all,) = staged(four_pieces(far, far_x))
    from_other, from_own, near_all, far_all = together(
        exchange(hidden_other, "y"), exchange(hidden_own, "y"), near_all, far_all
    )
    (parts,) = vmem_call(
        down_kernel,
        [jax.ShapeDtypeStruct((4, 2 * tok_dev, half), jnp.bfloat16)],
        [],
        [hidden_own, hidden_other, from_other, from_own, near_all, far_all],
        8,
    )
    summed = line_scatter(parts)
    own_half = summed[:tok_dev]
    other_half = exchange(summed[tok_dev:].astype(jnp.bfloat16), "y").astype(jnp.float32)
    mlp_own = jnp.concatenate(
        [jnp.where(y == 1, other_half, own_half), jnp.where(y == 1, own_half, other_half)], axis=1
    )
    return add_normed(residual_own, mlp_own, gains[1])


def shards(
    layer_input,
    request_lengths,
    request_adapter,
    slot_adapter_index,
    query_weight,
    key_weight,
    value_weight,
    output_weight,
    query_norm_gain,
    key_norm_gain,
    query_down_factors,
    value_down_factors,
    query_up_factors,
    value_up_factors,
    attention_norm_gain,
    feedforward_norm_gain,
    gate_weight,
    up_weight,
    down_weight_transposed,
):
    tok_dev = layer_input.shape[0]
    tok_group = tok_dev * lax.axis_size("mlp")
    window = tok_group * 3 // 8
    heads_local = query_weight.shape[1] // HEAD_SIZE
    direct = [lax.axis_size(axis) for axis in (*REQ, "mlp")] == [2, 2, 2, 4]
    places = jnp.arange(tok_group, dtype=jnp.int32)
    if direct:
        places = (places + lax.axis_index("mlp") * tok_dev) % tok_group
    request, position, token_slot = layout(
        request_lengths[0], request_adapter[0], slot_adapter_index, places
    )
    columns = jnp.arange(ADAPTER_SLOTS * ADAPTER_RANK, dtype=jnp.int32) // ADAPTER_RANK
    slot_match_mask = (columns[None, :] == token_slot[:, None]).astype(jnp.bfloat16)
    gate_rows, up_rows, down_rows = gate_weight.T, up_weight.T, down_weight_transposed.T
    if direct:
        return layer_direct(
            layer_input,
            rotary_angles(position),
            slot_match_mask,
            allowed_keys(request, position, window).astype(jnp.float32),
            (query_weight, key_weight, value_weight, output_weight),
            (query_down_factors, value_down_factors, query_up_factors, value_up_factors),
            (query_norm_gain[None, :], key_norm_gain[None, :]),
            (attention_norm_gain, feedforward_norm_gain),
            (gate_rows, up_rows, down_rows),
        )
    group_token_rows = lax.all_gather(layer_input, "mlp", axis=0, tiled=True)
    query_reduced = (
        jnp.dot(group_token_rows, query_down_factors, preferred_element_type=jnp.float32).astype(
            jnp.bfloat16
        )
        * slot_match_mask
    )
    value_reduced = (
        jnp.dot(group_token_rows, value_down_factors, preferred_element_type=jnp.float32).astype(
            jnp.bfloat16
        )
        * slot_match_mask
    )
    query_before_norm = jnp.dot(
        group_token_rows, query_weight, preferred_element_type=jnp.float32
    ) + adapter_scale * jnp.dot(query_reduced, query_up_factors, preferred_element_type=jnp.float32)
    key_pre = jnp.dot(group_token_rows, key_weight, preferred_element_type=jnp.float32)
    value_before_adapter = jnp.dot(
        group_token_rows, value_weight, preferred_element_type=jnp.float32
    ) + adapter_scale * jnp.dot(value_reduced, value_up_factors, preferred_element_type=jnp.float32)
    queries = rotary(
        rms_scale(query_before_norm.reshape(tok_group, heads_local, HEAD_SIZE))
        * query_norm_gain.reshape(heads_local, HEAD_SIZE),
        position,
    ).astype(jnp.bfloat16)
    key_heads = rotary(
        rms_scale(key_pre.reshape(tok_group, heads_local, HEAD_SIZE))
        * key_norm_gain.reshape(heads_local, HEAD_SIZE),
        position,
    ).astype(jnp.bfloat16)
    value_heads = value_before_adapter.astype(jnp.bfloat16).reshape(
        tok_group, heads_local, HEAD_SIZE
    )
    context = attention(queries, key_heads, value_heads, request, position, window).reshape(
        tok_group, heads_local * HEAD_SIZE
    )
    attn_own = lax.psum_scatter(
        jnp.dot(context, output_weight, preferred_element_type=jnp.float32).astype(jnp.bfloat16),
        "mlp",
        scatter_dimension=0,
        tiled=True,
    ).astype(jnp.float32)
    residual_own = add_normed(layer_input, attn_own, attention_norm_gain)
    gate_rows, up_rows, down_rows = (
        lax.all_gather(rows, REQ, axis=0, tiled=True) for rows in (gate_rows, up_rows, down_rows)
    )
    hidden = hidden_units(
        lax.all_gather(residual_own, "mlp", axis=0, tiled=True), gate_rows, up_rows
    )
    part = jnp.dot(hidden, down_rows, preferred_element_type=jnp.float32)
    mlp_own = lax.psum_scatter(
        part.astype(jnp.bfloat16), "mlp", scatter_dimension=0, tiled=True
    ).astype(jnp.float32)
    return add_normed(residual_own, mlp_own, feedforward_norm_gain)


def solution(mesh):
    req, mlp = mesh.devices.shape
    side = math.isqrt(req // 2)
    fine = Mesh(mesh.devices.reshape(req // 2 // side, side, 2, mlp), ("y", "x", "core", "mlp"))
    return jax.shard_map(
        shards,
        mesh=fine,
        in_specs=(
            P((*REQ, "mlp"), None),
            P(REQ, None),
            P(REQ, None),
            P(),
            P(None, "mlp"),
            P(None, "mlp"),
            P(None, "mlp"),
            P("mlp", None),
            P("mlp"),
            P("mlp"),
            P(),
            P(),
            P(None, "mlp"),
            P(None, "mlp"),
            P(),
            P(),
            P(None, (*REQ, "mlp")),
            P(None, (*REQ, "mlp")),
            P(None, (*REQ, "mlp")),
        ),
        out_specs=P((*REQ, "mlp"), None),
        check_vma=False,
    )
```

```python
import math

import jax
import jax.numpy as jnp
from jax import lax
from jax.experimental import pallas as pl
from jax.experimental.pallas import tpu as pltpu
from jax.sharding import Mesh, PartitionSpec as P

HEAD_SIZE = 128
ADAPTER_RANK = 16
ADAPTER_SLOTS = 8
SINKS = 4
REQ = ("y", "x", "core")


epsilon = 1e-06
adapter_scale = 0.5
rope_theta = 500000.0


def rms_scale(inputs):
    return inputs * lax.rsqrt(jnp.mean(inputs * inputs, axis=-1, keepdims=True) + epsilon)


def rotary_angles(position):
    exponent = jnp.arange(HEAD_SIZE // 2, dtype=jnp.float32) * (2.0 / HEAD_SIZE)
    frequency = rope_theta ** (-exponent)
    return position.astype(jnp.float32)[:, None] * frequency[None, :]


def rotary(inputs, position):
    half_dim = inputs.shape[-1] // 2
    angles = rotary_angles(position)
    cosine = jnp.cos(angles)[:, None, :]
    sine_part = jnp.sin(angles)[:, None, :]
    first_half = inputs[..., :half_dim]
    second = inputs[..., half_dim:]
    return jnp.concatenate(
        [first_half * cosine - second * sine_part, second * cosine + first_half * sine_part],
        axis=-1,
    )


def layout(lengths, adapters, slot_adapter_index, places):
    req_ends = jnp.cumsum(lengths)
    starts = req_ends - lengths
    member = ((places[:, None] >= starts[None, :]) & (places[:, None] < req_ends[None, :])).astype(
        jnp.int32
    )
    request = jnp.sum(member * jnp.arange(lengths.shape[0], dtype=jnp.int32)[None, :], axis=1)
    position = places - jnp.sum(member * starts[None, :], axis=1)
    chosen = jnp.sum(member * adapters[None, :], axis=1)
    slot_ids = jnp.arange(slot_adapter_index.shape[0], dtype=jnp.int32)
    token_slot = jnp.sum(
        (chosen[:, None] == slot_adapter_index[None, :]).astype(jnp.int32) * slot_ids[None, :],
        axis=1,
    )
    return (request, position, token_slot)


def allowed_keys(request, position, window):
    distance = position[:, None] - position[None, :]
    return (
        (request[:, None] == request[None, :])
        & (distance >= 0)
        & ((distance < window) | (position[None, :] < SINKS))
    )


def attention(queries, key_heads, value_heads, request, position, window):
    scores = jnp.einsum(
        "qhd,khd->hqk", queries, key_heads, preferred_element_type=jnp.float32
    ) * HEAD_SIZE ** (-0.5)
    allowed = allowed_keys(request, position, window)
    scores = jnp.where(allowed[None, :, :], scores, -1e30)
    row_peak = jnp.max(scores, axis=-1, keepdims=True)
    weights = jnp.exp(scores - row_peak)
    weights = (weights / jnp.sum(weights, axis=-1, keepdims=True)).astype(jnp.bfloat16)
    context = jnp.einsum("hqk,khd->qhd", weights, value_heads, preferred_element_type=jnp.float32)
    return context.astype(jnp.bfloat16)


def hidden_units(states, gate_rows, up_rows):
    contract = (((1,), (1,)), ((), ()))
    gate_act = lax.dot_general(states, gate_rows, contract, preferred_element_type=jnp.float32)
    up_act = lax.dot_general(states, up_rows, contract, preferred_element_type=jnp.float32)
    return (jax.nn.silu(gate_act) * up_act).astype(jnp.bfloat16)


def exchange(block, axis):
    return lax.ppermute(block, axis, [(0, 1), (1, 0)])


def shift(block, hops):
    return lax.ppermute(block, "mlp", [((k + hops) % 4, k) for k in range(4)])


def line_gather(block):
    across = shift(block, 2)
    return [block, shift(block, 1), across, shift(block, 3)]


def line_scatter(parts):
    across = shift(parts[2], 2)
    arrived = (parts[0], shift(parts[3], 1), across, shift(parts[1], 3))
    return sum(part.astype(jnp.float32) for part in arrived)


def together(*values):
    return lax.optimization_barrier(values)


def four_pieces(rows, rows_x, place=lambda rows: rows):
    return [place(rows), exchange(rows, "core"), rows_x, exchange(rows_x, "core")]


def vmem_call(kernel, outs, scratch, operands, vmem_mib):
    whole = pl.BlockSpec(memory_space=pltpu.VMEM)
    return pl.pallas_call(
        kernel,
        out_shape=outs,
        in_specs=[whole] * len(operands),
        out_specs=[whole] * len(outs),
        scratch_shapes=scratch,
        compiler_params=pltpu.CompilerParams(vmem_limit_bytes=vmem_mib << 20),
        cost_estimate=pl.CostEstimate(flops=1 << 20, bytes_accessed=1 << 20, transcendentals=0),
    )(*operands)


def in_hbm(array):
    return pltpu.with_memory_space_constraint(array, pltpu.HBM)


def staged(*groups):
    arrays = [array for group in groups for array in group]

    def kernel(*refs):
        sources, targets, sems = refs[: len(arrays)], refs[len(arrays) : -1], refs[-1]
        copies = []
        for group, target in zip(groups, targets):
            start = 0
            for array in group:
                at = len(copies)
                rows = target.at[pl.ds(start, array.shape[0]), :]
                copies.append(pltpu.make_async_copy(sources[at], rows, sems.at[at]))
                copies[-1].start()
                start += array.shape[0]
        for copy in copies:
            copy.wait()

    outs = [(sum(array.shape[0] for array in group), group[0].shape[1]) for group in groups]
    size = sum(array.size * array.dtype.itemsize for array in arrays)
    return pl.pallas_call(
        kernel,
        out_shape=[pltpu.VMEM(shape, group[0].dtype) for shape, group in zip(outs, groups)],
        in_specs=[pl.BlockSpec(memory_space=pl.ANY)] * len(arrays),
        out_specs=[pl.BlockSpec(memory_space=pltpu.VMEM)] * len(groups),
        scratch_shapes=[pltpu.SemaphoreType.DMA((len(arrays),))],
        compiler_params=pltpu.CompilerParams(vmem_limit_bytes=1 << 20),
        cost_estimate=pl.CostEstimate(flops=0, bytes_accessed=2 * size, transcendentals=0),
    )(*arrays)


NT = (((1,), (1,)), ((), ()))


def attention_kernel(
    block_0,
    block_1,
    block_2,
    block_3,
    query_weight,
    key_weight,
    value_weight,
    output_weight,
    query_down,
    value_down,
    query_up,
    value_up,
    query_gain,
    key_gain,
    cosine,
    sine,
    slot_mask,
    allowed,
    out_0,
    out_1,
    out_2,
    out_3,
    rows,
    context,
):
    tok_dev = block_0.shape[0]
    for k, block in enumerate((block_0, block_1, block_2, block_3)):
        rows[k * tok_dev : (k + 1) * tok_dev, :] = block[...]

    def project(weight):
        return jnp.dot(rows[...], weight[...], preferred_element_type=jnp.float32)

    def adapted(weight, down, up):
        low = project(down).astype(jnp.bfloat16) * slot_mask[...]
        return project(weight) + adapter_scale * jnp.dot(
            low, up[...], preferred_element_type=jnp.float32
        )

    def heads(inputs, gain):
        inputs = rms_scale(inputs) * gain
        turned = pltpu.roll(inputs, HEAD_SIZE // 2, 1)
        return (inputs * cosine[...] + turned * sine[...]).astype(jnp.bfloat16)

    queries = adapted(query_weight, query_down, query_up)
    keys = project(key_weight)
    values = adapted(value_weight, value_down, value_up).astype(jnp.bfloat16)
    for start in range(0, queries.shape[1], HEAD_SIZE):
        at = slice(start, start + HEAD_SIZE)
        scores = lax.dot_general(
            heads(queries[:, at], query_gain[:, at]),
            heads(keys[:, at], key_gain[:, at]),
            NT,
            preferred_element_type=jnp.float32,
        ) * HEAD_SIZE ** (-0.5)
        scores = jnp.where(allowed[...] > 0, scores, -1e30)
        weights = jnp.exp(scores - jnp.max(scores, axis=-1, keepdims=True))
        weights = (weights / jnp.sum(weights, axis=-1, keepdims=True)).astype(jnp.bfloat16)
        context[:, at] = jnp.dot(
            weights, values[:, at], preferred_element_type=jnp.float32
        ).astype(jnp.bfloat16)
    step = 1024
    for start in range(0, output_weight.shape[1], step):
        at = slice(start, start + step)
        part = jnp.dot(context[...], output_weight[:, at], preferred_element_type=jnp.float32)
        part = part.astype(jnp.bfloat16)
        for k, out in enumerate((out_0, out_1, out_2, out_3)):
            out[:, at] = part[k * tok_dev : (k + 1) * tok_dev]


def hidden_kernel(states, gate_rows, up_rows, out):
    step = 256
    for start in range(0, gate_rows.shape[0], step):
        at = slice(start, start + step)
        gate_act = lax.dot_general(
            states[...], gate_rows[at, :], NT, preferred_element_type=jnp.float32
        )
        up_act = lax.dot_general(
            states[...], up_rows[at, :], NT, preferred_element_type=jnp.float32
        )
        hidden = gate_act / (1.0 + jnp.exp(-gate_act)) * up_act
        out[:, at] = hidden.astype(jnp.bfloat16)


def down_kernel(own, other, far_own, far_other, near_rows, far_rows, out_0, out_1, out_2, out_3):
    tok_dev = out_0.shape[0] // 2
    step = 512
    for start in range(0, near_rows.shape[1], step):
        at = slice(start, start + step)
        for side, (near, far) in enumerate(((own, far_own), (other, far_other))):
            part = jnp.dot(near[...], near_rows[:, at], preferred_element_type=jnp.float32)
            part += jnp.dot(far[...], far_rows[:, at], preferred_element_type=jnp.float32)
            part = part.astype(jnp.bfloat16)
            for k, out in enumerate((out_0, out_1, out_2, out_3)):
                out[side * tok_dev : (side + 1) * tok_dev, at] = part[
                    k * tok_dev : (k + 1) * tok_dev
                ]


def add_normed(base, added, gain):
    return (base.astype(jnp.float32) + rms_scale(added) * gain).astype(jnp.bfloat16)


def layer_direct(
    layer_input, angles, slot_mask, allowed, projections, adapters, head_gains, gains, ffn_rows
):
    tok_dev, width = layer_input.shape
    gate_rows, up_rows, down_rows = ffn_rows
    y = lax.axis_index("y")
    half = width // 2
    gate_x, up_x = exchange(gate_rows, "x"), exchange(up_rows, "x")
    cosine, sine = jnp.cos(angles), jnp.sin(angles)
    block = jax.ShapeDtypeStruct((tok_dev, width), jnp.bfloat16)
    *staged_rows, own_block = staged(
        *([in_hbm(array)] for array in (*projections, *adapters, *head_gains, layer_input))
    )
    parts = vmem_call(
        attention_kernel,
        [block] * 4,
        [
            pltpu.VMEM((4 * tok_dev, width), jnp.bfloat16),
            pltpu.VMEM((4 * tok_dev, projections[0].shape[1]), jnp.bfloat16),
        ],
        [
            own_block,
            *line_gather(layer_input)[1:],
            *staged_rows,
            jnp.concatenate([cosine, cosine], axis=1),
            jnp.concatenate([-sine, sine], axis=1),
            slot_mask,
            allowed,
        ],
        8,
    )
    *parts, down_rows = together(*parts, down_rows)
    near = lax.dynamic_slice_in_dim(down_rows, y * half, half, axis=1)
    far = exchange(lax.dynamic_slice_in_dim(down_rows, (1 - y) * half, half, axis=1), "y")
    near_x, far_x = exchange(near, "x"), exchange(far, "x")
    attn_own, near, far = together(line_scatter(parts), near, far)
    residual_own = add_normed(layer_input, attn_own, gains[0])
    own, *line, other = together(*line_gather(residual_own), exchange(residual_own, "y"))
    line, gate_x, up_x, near_x = together(jnp.concatenate(line), gate_x, up_x, near_x)
    (gate_all,) = staged(four_pieces(gate_rows, gate_x, in_hbm))
    (up_all,) = staged(four_pieces(up_rows, up_x, in_hbm))

    def hidden_units_of(first, others):
        (hidden,) = vmem_call(
            hidden_kernel,
            [jax.ShapeDtypeStruct((4 * tok_dev, gate_all.shape[0]), jnp.bfloat16)],
            [],
            [jnp.concatenate([first, others]), gate_all, up_all],
            8,
        )
        return hidden

    line_other = exchange(line, "y")
    hidden_own = hidden_units_of(own, line)
    line_other, hidden_own, far_x = together(line_other, hidden_own, far_x)
    from_own = exchange(hidden_own, "y")
    hidden_other = hidden_units_of(other, line_other)
    from_other = exchange(hidden_other, "y")
    (near_all,) = staged(four_pieces(near, near_x))
    (far_all,) = staged(four_pieces(far, far_x))
    parts = vmem_call(
        down_kernel,
        [jax.ShapeDtypeStruct((2 * tok_dev, half), jnp.bfloat16)] * 4,
        [],
        [hidden_own, hidden_other, from_other, from_own, near_all, far_all],
        8,
    )
    summed = line_scatter(parts)
    own_half = summed[:tok_dev]
    other_half = exchange(summed[tok_dev:].astype(jnp.bfloat16), "y").astype(jnp.float32)
    mlp_own = jnp.concatenate(
        [jnp.where(y == 1, other_half, own_half), jnp.where(y == 1, own_half, other_half)], axis=1
    )
    return add_normed(residual_own, mlp_own, gains[1])


def shards(
    layer_input,
    request_lengths,
    request_adapter,
    slot_adapter_index,
    query_weight,
    key_weight,
    value_weight,
    output_weight,
    query_norm_gain,
    key_norm_gain,
    query_down_factors,
    value_down_factors,
    query_up_factors,
    value_up_factors,
    attention_norm_gain,
    feedforward_norm_gain,
    gate_weight,
    up_weight,
    down_weight_transposed,
):
    tok_dev = layer_input.shape[0]
    tok_group = tok_dev * lax.axis_size("mlp")
    window = tok_group * 3 // 8
    heads_local = query_weight.shape[1] // HEAD_SIZE
    direct = [lax.axis_size(axis) for axis in (*REQ, "mlp")] == [2, 2, 2, 4]
    places = jnp.arange(tok_group, dtype=jnp.int32)
    if direct:
        places = (places + lax.axis_index("mlp") * tok_dev) % tok_group
    request, position, token_slot = layout(
        request_lengths[0], request_adapter[0], slot_adapter_index, places
    )
    columns = jnp.arange(ADAPTER_SLOTS * ADAPTER_RANK, dtype=jnp.int32) // ADAPTER_RANK
    slot_match_mask = (columns[None, :] == token_slot[:, None]).astype(jnp.bfloat16)
    gate_rows, up_rows, down_rows = gate_weight.T, up_weight.T, down_weight_transposed.T
    if direct:
        return layer_direct(
            layer_input,
            rotary_angles(position),
            slot_match_mask,
            allowed_keys(request, position, window).astype(jnp.float32),
            (query_weight, key_weight, value_weight, output_weight),
            (query_down_factors, value_down_factors, query_up_factors, value_up_factors),
            (query_norm_gain[None, :], key_norm_gain[None, :]),
            (attention_norm_gain, feedforward_norm_gain),
            (gate_rows, up_rows, down_rows),
        )
    group_token_rows = lax.all_gather(layer_input, "mlp", axis=0, tiled=True)
    query_reduced = (
        jnp.dot(group_token_rows, query_down_factors, preferred_element_type=jnp.float32).astype(
            jnp.bfloat16
        )
        * slot_match_mask
    )
    value_reduced = (
        jnp.dot(group_token_rows, value_down_factors, preferred_element_type=jnp.float32).astype(
            jnp.bfloat16
        )
        * slot_match_mask
    )
    query_before_norm = jnp.dot(
        group_token_rows, query_weight, preferred_element_type=jnp.float32
    ) + adapter_scale * jnp.dot(query_reduced, query_up_factors, preferred_element_type=jnp.float32)
    key_pre = jnp.dot(group_token_rows, key_weight, preferred_element_type=jnp.float32)
    value_before_adapter = jnp.dot(
        group_token_rows, value_weight, preferred_element_type=jnp.float32
    ) + adapter_scale * jnp.dot(value_reduced, value_up_factors, preferred_element_type=jnp.float32)
    queries = rotary(
        rms_scale(query_before_norm.reshape(tok_group, heads_local, HEAD_SIZE))
        * query_norm_gain.reshape(heads_local, HEAD_SIZE),
        position,
    ).astype(jnp.bfloat16)
    key_heads = rotary(
        rms_scale(key_pre.reshape(tok_group, heads_local, HEAD_SIZE))
        * key_norm_gain.reshape(heads_local, HEAD_SIZE),
        position,
    ).astype(jnp.bfloat16)
    value_heads = value_before_adapter.astype(jnp.bfloat16).reshape(
        tok_group, heads_local, HEAD_SIZE
    )
    context = attention(queries, key_heads, value_heads, request, position, window).reshape(
        tok_group, heads_local * HEAD_SIZE
    )
    attn_own = lax.psum_scatter(
        jnp.dot(context, output_weight, preferred_element_type=jnp.float32).astype(jnp.bfloat16),
        "mlp",
        scatter_dimension=0,
        tiled=True,
    ).astype(jnp.float32)
    residual_own = add_normed(layer_input, attn_own, attention_norm_gain)
    gate_rows, up_rows, down_rows = (
        lax.all_gather(rows, REQ, axis=0, tiled=True) for rows in (gate_rows, up_rows, down_rows)
    )
    hidden = hidden_units(
        lax.all_gather(residual_own, "mlp", axis=0, tiled=True), gate_rows, up_rows
    )
    part = jnp.dot(hidden, down_rows, preferred_element_type=jnp.float32)
    mlp_own = lax.psum_scatter(
        part.astype(jnp.bfloat16), "mlp", scatter_dimension=0, tiled=True
    ).astype(jnp.float32)
    return add_normed(residual_own, mlp_own, feedforward_norm_gain)


def solution(mesh):
    req, mlp = mesh.devices.shape
    side = math.isqrt(req // 2)
    fine = Mesh(mesh.devices.reshape(req // 2 // side, side, 2, mlp), ("y", "x", "core", "mlp"))
    return jax.shard_map(
        shards,
        mesh=fine,
        in_specs=(
            P((*REQ, "mlp"), None),
            P(REQ, None),
            P(REQ, None),
            P(),
            P(None, "mlp"),
            P(None, "mlp"),
            P(None, "mlp"),
            P("mlp", None),
            P("mlp"),
            P("mlp"),
            P(),
            P(),
            P(None, "mlp"),
            P(None, "mlp"),
            P(),
            P(),
            P(None, (*REQ, "mlp")),
            P(None, (*REQ, "mlp")),
            P(None, (*REQ, "mlp")),
        ),
        out_specs=P((*REQ, "mlp"), None),
        check_vma=False,
    )
```

```python
import math

import jax
import jax.numpy as jnp
from jax import lax
from jax.experimental import pallas as pl
from jax.experimental.pallas import tpu as pltpu
from jax.sharding import Mesh, PartitionSpec as P

HEAD_SIZE = 128
ADAPTER_RANK = 16
ADAPTER_SLOTS = 8
SINKS = 4
REQ = ("y", "x", "core")


epsilon = 1e-06
adapter_scale = 0.5
rope_theta = 500000.0


def rms_scale(inputs):
    return inputs * lax.rsqrt(jnp.mean(inputs * inputs, axis=-1, keepdims=True) + epsilon)


def rotary_angles(position):
    exponent = jnp.arange(HEAD_SIZE // 2, dtype=jnp.float32) * (2.0 / HEAD_SIZE)
    frequency = rope_theta ** (-exponent)
    return position.astype(jnp.float32)[:, None] * frequency[None, :]


def rotary(inputs, position):
    half_dim = inputs.shape[-1] // 2
    angles = rotary_angles(position)
    cosine = jnp.cos(angles)[:, None, :]
    sine_part = jnp.sin(angles)[:, None, :]
    first_half = inputs[..., :half_dim]
    second = inputs[..., half_dim:]
    return jnp.concatenate(
        [first_half * cosine - second * sine_part, second * cosine + first_half * sine_part],
        axis=-1,
    )


def layout(lengths, adapters, slot_adapter_index, places):
    req_ends = jnp.cumsum(lengths)
    starts = req_ends - lengths
    member = ((places[:, None] >= starts[None, :]) & (places[:, None] < req_ends[None, :])).astype(
        jnp.int32
    )
    request = jnp.sum(member * jnp.arange(lengths.shape[0], dtype=jnp.int32)[None, :], axis=1)
    position = places - jnp.sum(member * starts[None, :], axis=1)
    chosen = jnp.sum(member * adapters[None, :], axis=1)
    slot_ids = jnp.arange(slot_adapter_index.shape[0], dtype=jnp.int32)
    token_slot = jnp.sum(
        (chosen[:, None] == slot_adapter_index[None, :]).astype(jnp.int32) * slot_ids[None, :],
        axis=1,
    )
    return (request, position, token_slot)


def allowed_keys(request, position, window):
    distance = position[:, None] - position[None, :]
    return (
        (request[:, None] == request[None, :])
        & (distance >= 0)
        & ((distance < window) | (position[None, :] < SINKS))
    )


def attention(queries, key_heads, value_heads, request, position, window):
    scores = jnp.einsum(
        "qhd,khd->hqk", queries, key_heads, preferred_element_type=jnp.float32
    ) * HEAD_SIZE ** (-0.5)
    allowed = allowed_keys(request, position, window)
    scores = jnp.where(allowed[None, :, :], scores, -1e30)
    row_peak = jnp.max(scores, axis=-1, keepdims=True)
    weights = jnp.exp(scores - row_peak)
    weights = (weights / jnp.sum(weights, axis=-1, keepdims=True)).astype(jnp.bfloat16)
    context = jnp.einsum("hqk,khd->qhd", weights, value_heads, preferred_element_type=jnp.float32)
    return context.astype(jnp.bfloat16)


def hidden_units(states, gate_rows, up_rows):
    contract = (((1,), (1,)), ((), ()))
    gate_act = lax.dot_general(states, gate_rows, contract, preferred_element_type=jnp.float32)
    up_act = lax.dot_general(states, up_rows, contract, preferred_element_type=jnp.float32)
    return (jax.nn.silu(gate_act) * up_act).astype(jnp.bfloat16)


def exchange(block, axis):
    return lax.ppermute(block, axis, [(0, 1), (1, 0)])


def shift(block, hops):
    return lax.ppermute(block, "mlp", [((k + hops) % 4, k) for k in range(4)])


def line_gather(block):
    across = shift(block, 2)
    return [block, shift(block, 1), across, shift(block, 3)]


def line_scatter(parts):
    across = shift(parts[2], 2)
    arrived = (parts[0], shift(parts[3], 1), across, shift(parts[1], 3))
    return sum(part.astype(jnp.float32) for part in arrived)


def together(*values):
    return lax.optimization_barrier(values)


def four_pieces(rows, rows_x):
    return [rows, exchange(rows, "core"), rows_x, exchange(rows_x, "core")]


def vmem_call(kernel, outs, scratch, operands, vmem_mib):
    whole = pl.BlockSpec(memory_space=pltpu.VMEM)
    return pl.pallas_call(
        kernel,
        out_shape=outs,
        in_specs=[whole] * len(operands),
        out_specs=[whole] * len(outs),
        scratch_shapes=scratch,
        compiler_params=pltpu.CompilerParams(vmem_limit_bytes=vmem_mib << 20),
        cost_estimate=pl.CostEstimate(flops=1 << 20, bytes_accessed=1 << 20, transcendentals=0),
    )(*operands)


def in_hbm(array):
    return pltpu.with_memory_space_constraint(array, pltpu.HBM)


def staged(*groups):
    groups = [
        [piece if isinstance(piece, tuple) else (piece, 0, piece.shape[0]) for piece in group]
        for group in groups
    ]
    arrays = []
    for piece in (piece for group in groups for piece in group):
        if not any(piece[0] is array for array in arrays):
            arrays.append(piece[0])
    places = [
        [next(k for k, array in enumerate(arrays) if array is piece[0]) for piece in group]
        for group in groups
    ]
    count = sum(len(group) for group in groups)

    def kernel(*refs):
        sources, targets, sems = refs[: len(arrays)], refs[len(arrays) : -1], refs[-1]
        copies = []
        for group, place, target in zip(groups, places, targets):
            at = 0
            for (_, start, rows), k in zip(group, place):
                copies.append(
                    pltpu.make_async_copy(
                        sources[k].at[pl.ds(start, rows), :],
                        target.at[pl.ds(at, rows), :],
                        sems.at[len(copies)],
                    )
                )
                copies[-1].start()
                at += rows
        for copy in copies:
            copy.wait()

    outs = [(sum(piece[2] for piece in group), group[0][0].shape[1]) for group in groups]
    size = sum(rows * columns for rows, columns in outs)
    return pl.pallas_call(
        kernel,
        out_shape=[pltpu.VMEM(shape, group[0][0].dtype) for shape, group in zip(outs, groups)],
        in_specs=[pl.BlockSpec(memory_space=pl.ANY)] * len(arrays),
        out_specs=[pl.BlockSpec(memory_space=pltpu.VMEM)] * len(groups),
        scratch_shapes=[pltpu.SemaphoreType.DMA((count,))],
        compiler_params=pltpu.CompilerParams(vmem_limit_bytes=1 << 20),
        cost_estimate=pl.CostEstimate(flops=0, bytes_accessed=4 * size, transcendentals=0),
    )(*arrays)


NT = (((1,), (1,)), ((), ()))


def attention_kernel(
    block_0,
    block_1,
    block_2,
    block_3,
    query_weight,
    key_weight,
    value_weight,
    output_weight,
    query_down,
    value_down,
    query_up,
    value_up,
    query_gain,
    key_gain,
    cosine,
    sine,
    slot_mask,
    allowed,
    out_0,
    out_1,
    out_2,
    out_3,
    rows,
    context,
):
    tok_dev = block_0.shape[0]
    for k, block in enumerate((block_0, block_1, block_2, block_3)):
        rows[k * tok_dev : (k + 1) * tok_dev, :] = block[...]

    def project(weight):
        return jnp.dot(rows[...], weight[...], preferred_element_type=jnp.float32)

    def adapted(weight, down, up):
        low = project(down).astype(jnp.bfloat16) * slot_mask[...]
        return project(weight) + adapter_scale * jnp.dot(
            low, up[...], preferred_element_type=jnp.float32
        )

    def heads(inputs, gain):
        inputs = rms_scale(inputs) * gain
        turned = pltpu.roll(inputs, HEAD_SIZE // 2, 1)
        return (inputs * cosine[...] + turned * sine[...]).astype(jnp.bfloat16)

    queries = adapted(query_weight, query_down, query_up)
    keys = project(key_weight)
    values = adapted(value_weight, value_down, value_up).astype(jnp.bfloat16)
    for start in range(0, queries.shape[1], HEAD_SIZE):
        at = slice(start, start + HEAD_SIZE)
        scores = lax.dot_general(
            heads(queries[:, at], query_gain[:, at]),
            heads(keys[:, at], key_gain[:, at]),
            NT,
            preferred_element_type=jnp.float32,
        ) * HEAD_SIZE ** (-0.5)
        scores = jnp.where(allowed[...] > 0, scores, -1e30)
        weights = jnp.exp(scores - jnp.max(scores, axis=-1, keepdims=True))
        weights = (weights / jnp.sum(weights, axis=-1, keepdims=True)).astype(jnp.bfloat16)
        context[:, at] = jnp.dot(
            weights, values[:, at], preferred_element_type=jnp.float32
        ).astype(jnp.bfloat16)
    step = 1024
    for start in range(0, output_weight.shape[1], step):
        at = slice(start, start + step)
        part = jnp.dot(context[...], output_weight[:, at], preferred_element_type=jnp.float32)
        part = part.astype(jnp.bfloat16)
        for k, out in enumerate((out_0, out_1, out_2, out_3)):
            out[:, at] = part[k * tok_dev : (k + 1) * tok_dev]


def hidden_kernel(states, gate_rows, up_rows, out):
    step = 256
    for start in range(0, gate_rows.shape[0], step):
        at = slice(start, start + step)
        gate_act = lax.dot_general(
            states[...], gate_rows[at, :], NT, preferred_element_type=jnp.float32
        )
        up_act = lax.dot_general(
            states[...], up_rows[at, :], NT, preferred_element_type=jnp.float32
        )
        hidden = gate_act / (1.0 + jnp.exp(-gate_act)) * up_act
        out[:, at] = hidden.astype(jnp.bfloat16)


def down_kernel(own, other, far_own, far_other, near_rows, far_rows, out_0, out_1, out_2, out_3):
    tok_dev = out_0.shape[0] // 2
    step = 512
    for start in range(0, near_rows.shape[1], step):
        at = slice(start, start + step)
        for side, (near, far) in enumerate(((own, far_own), (other, far_other))):
            part = jnp.dot(near[...], near_rows[:, at], preferred_element_type=jnp.float32)
            part += jnp.dot(far[...], far_rows[:, at], preferred_element_type=jnp.float32)
            part = part.astype(jnp.bfloat16)
            for k, out in enumerate((out_0, out_1, out_2, out_3)):
                out[side * tok_dev : (side + 1) * tok_dev, at] = part[
                    k * tok_dev : (k + 1) * tok_dev
                ]


def add_normed(base, added, gain):
    return (base.astype(jnp.float32) + rms_scale(added) * gain).astype(jnp.bfloat16)


def layer_direct(
    layer_input, angles, slot_mask, allowed, projections, adapters, head_gains, gains, ffn_rows
):
    tok_dev, width = layer_input.shape
    gate_rows, up_rows, down_rows = ffn_rows
    y = lax.axis_index("y")
    half = width // 2
    units = gate_rows.shape[0]
    (gate_up,) = staged([in_hbm(gate_rows), in_hbm(up_rows)])
    gate_up_x = exchange(gate_up, "x")
    cosine, sine = jnp.cos(angles), jnp.sin(angles)
    block = jax.ShapeDtypeStruct((tok_dev, width), jnp.bfloat16)
    *staged_rows, own_block = staged(
        *([in_hbm(array)] for array in (*projections, *adapters, *head_gains, layer_input))
    )
    parts = vmem_call(
        attention_kernel,
        [block] * 4,
        [
            pltpu.VMEM((4 * tok_dev, width), jnp.bfloat16),
            pltpu.VMEM((4 * tok_dev, projections[0].shape[1]), jnp.bfloat16),
        ],
        [
            own_block,
            *line_gather(layer_input)[1:],
            *staged_rows,
            jnp.concatenate([cosine, cosine], axis=1),
            jnp.concatenate([-sine, sine], axis=1),
            slot_mask,
            allowed,
        ],
        8,
    )
    *parts, down_rows = together(*parts, down_rows)
    near = lax.dynamic_slice_in_dim(down_rows, y * half, half, axis=1)
    far = exchange(lax.dynamic_slice_in_dim(down_rows, (1 - y) * half, half, axis=1), "y")
    near_x, far_x = exchange(near, "x"), exchange(far, "x")
    attn_own, near, far = together(line_scatter(parts), near, far)
    residual_own = add_normed(layer_input, attn_own, gains[0])
    own, *line, other = together(*line_gather(residual_own), exchange(residual_own, "y"))
    line, gate_up_x, near_x = together(jnp.concatenate(line), gate_up_x, near_x)
    pieces = [exchange(gate_up, "core"), gate_up_x, exchange(gate_up_x, "core")]
    gate_all, up_all = staged(
        [in_hbm(gate_rows), *((piece, 0, units) for piece in pieces)],
        [in_hbm(up_rows), *((piece, units, units) for piece in pieces)],
    )

    def hidden_units_of(first, others):
        (hidden,) = vmem_call(
            hidden_kernel,
            [jax.ShapeDtypeStruct((4 * tok_dev, gate_all.shape[0]), jnp.bfloat16)],
            [],
            [jnp.concatenate([first, others]), gate_all, up_all],
            8,
        )
        return hidden

    line_other = exchange(line, "y")
    hidden_own = hidden_units_of(own, line)
    line_other, hidden_own, far_x = together(line_other, hidden_own, far_x)
    from_own = exchange(hidden_own, "y")
    hidden_other = hidden_units_of(other, line_other)
    from_other = exchange(hidden_other, "y")
    (near_all,) = staged(four_pieces(near, near_x))
    (far_all,) = staged(four_pieces(far, far_x))
    parts = vmem_call(
        down_kernel,
        [jax.ShapeDtypeStruct((2 * tok_dev, half), jnp.bfloat16)] * 4,
        [],
        [hidden_own, hidden_other, from_other, from_own, near_all, far_all],
        8,
    )
    summed = line_scatter(parts)
    own_half = summed[:tok_dev]
    other_half = exchange(summed[tok_dev:].astype(jnp.bfloat16), "y").astype(jnp.float32)
    mlp_own = jnp.concatenate(
        [jnp.where(y == 1, other_half, own_half), jnp.where(y == 1, own_half, other_half)], axis=1
    )
    return add_normed(residual_own, mlp_own, gains[1])


def shards(
    layer_input,
    request_lengths,
    request_adapter,
    slot_adapter_index,
    query_weight,
    key_weight,
    value_weight,
    output_weight,
    query_norm_gain,
    key_norm_gain,
    query_down_factors,
    value_down_factors,
    query_up_factors,
    value_up_factors,
    attention_norm_gain,
    feedforward_norm_gain,
    gate_weight,
    up_weight,
    down_weight_transposed,
):
    tok_dev = layer_input.shape[0]
    tok_group = tok_dev * lax.axis_size("mlp")
    window = tok_group * 3 // 8
    heads_local = query_weight.shape[1] // HEAD_SIZE
    direct = [lax.axis_size(axis) for axis in (*REQ, "mlp")] == [2, 2, 2, 4]
    places = jnp.arange(tok_group, dtype=jnp.int32)
    if direct:
        places = (places + lax.axis_index("mlp") * tok_dev) % tok_group
    request, position, token_slot = layout(
        request_lengths[0], request_adapter[0], slot_adapter_index, places
    )
    columns = jnp.arange(ADAPTER_SLOTS * ADAPTER_RANK, dtype=jnp.int32) // ADAPTER_RANK
    slot_match_mask = (columns[None, :] == token_slot[:, None]).astype(jnp.bfloat16)
    gate_rows, up_rows, down_rows = gate_weight.T, up_weight.T, down_weight_transposed.T
    if direct:
        return layer_direct(
            layer_input,
            rotary_angles(position),
            slot_match_mask,
            allowed_keys(request, position, window).astype(jnp.float32),
            (query_weight, key_weight, value_weight, output_weight),
            (query_down_factors, value_down_factors, query_up_factors, value_up_factors),
            (query_norm_gain[None, :], key_norm_gain[None, :]),
            (attention_norm_gain, feedforward_norm_gain),
            (gate_rows, up_rows, down_rows),
        )
    group_token_rows = lax.all_gather(layer_input, "mlp", axis=0, tiled=True)
    query_reduced = (
        jnp.dot(group_token_rows, query_down_factors, preferred_element_type=jnp.float32).astype(
            jnp.bfloat16
        )
        * slot_match_mask
    )
    value_reduced = (
        jnp.dot(group_token_rows, value_down_factors, preferred_element_type=jnp.float32).astype(
            jnp.bfloat16
        )
        * slot_match_mask
    )
    query_before_norm = jnp.dot(
        group_token_rows, query_weight, preferred_element_type=jnp.float32
    ) + adapter_scale * jnp.dot(query_reduced, query_up_factors, preferred_element_type=jnp.float32)
    key_pre = jnp.dot(group_token_rows, key_weight, preferred_element_type=jnp.float32)
    value_before_adapter = jnp.dot(
        group_token_rows, value_weight, preferred_element_type=jnp.float32
    ) + adapter_scale * jnp.dot(value_reduced, value_up_factors, preferred_element_type=jnp.float32)
    queries = rotary(
        rms_scale(query_before_norm.reshape(tok_group, heads_local, HEAD_SIZE))
        * query_norm_gain.reshape(heads_local, HEAD_SIZE),
        position,
    ).astype(jnp.bfloat16)
    key_heads = rotary(
        rms_scale(key_pre.reshape(tok_group, heads_local, HEAD_SIZE))
        * key_norm_gain.reshape(heads_local, HEAD_SIZE),
        position,
    ).astype(jnp.bfloat16)
    value_heads = value_before_adapter.astype(jnp.bfloat16).reshape(
        tok_group, heads_local, HEAD_SIZE
    )
    context = attention(queries, key_heads, value_heads, request, position, window).reshape(
        tok_group, heads_local * HEAD_SIZE
    )
    attn_own = lax.psum_scatter(
        jnp.dot(context, output_weight, preferred_element_type=jnp.float32).astype(jnp.bfloat16),
        "mlp",
        scatter_dimension=0,
        tiled=True,
    ).astype(jnp.float32)
    residual_own = add_normed(layer_input, attn_own, attention_norm_gain)
    gate_rows, up_rows, down_rows = (
        lax.all_gather(rows, REQ, axis=0, tiled=True) for rows in (gate_rows, up_rows, down_rows)
    )
    hidden = hidden_units(
        lax.all_gather(residual_own, "mlp", axis=0, tiled=True), gate_rows, up_rows
    )
    part = jnp.dot(hidden, down_rows, preferred_element_type=jnp.float32)
    mlp_own = lax.psum_scatter(
        part.astype(jnp.bfloat16), "mlp", scatter_dimension=0, tiled=True
    ).astype(jnp.float32)
    return add_normed(residual_own, mlp_own, feedforward_norm_gain)


def solution(mesh):
    req, mlp = mesh.devices.shape
    side = math.isqrt(req // 2)
    fine = Mesh(mesh.devices.reshape(req // 2 // side, side, 2, mlp), ("y", "x", "core", "mlp"))
    return jax.shard_map(
        shards,
        mesh=fine,
        in_specs=(
            P((*REQ, "mlp"), None),
            P(REQ, None),
            P(REQ, None),
            P(),
            P(None, "mlp"),
            P(None, "mlp"),
            P(None, "mlp"),
            P("mlp", None),
            P("mlp"),
            P("mlp"),
            P(),
            P(),
            P(None, "mlp"),
            P(None, "mlp"),
            P(),
            P(),
            P(None, (*REQ, "mlp")),
            P(None, (*REQ, "mlp")),
            P(None, (*REQ, "mlp")),
        ),
        out_specs=P((*REQ, "mlp"), None),
        check_vma=False,
    )
```

```python
import math

import jax
import jax.numpy as jnp
from jax import lax
from jax.experimental import pallas as pl
from jax.experimental.pallas import tpu as pltpu
from jax.sharding import Mesh, PartitionSpec as P

HEAD_SIZE = 128
ADAPTER_RANK = 16
ADAPTER_SLOTS = 8
SINKS = 4
REQ = ("y", "x", "core")


epsilon = 1e-06
adapter_scale = 0.5
rope_theta = 500000.0


def rms_scale(inputs):
    return inputs * lax.rsqrt(jnp.mean(inputs * inputs, axis=-1, keepdims=True) + epsilon)


def rotary_angles(position):
    exponent = jnp.arange(HEAD_SIZE // 2, dtype=jnp.float32) * (2.0 / HEAD_SIZE)
    frequency = rope_theta ** (-exponent)
    return position.astype(jnp.float32)[:, None] * frequency[None, :]


def rotary(inputs, position):
    half_dim = inputs.shape[-1] // 2
    angles = rotary_angles(position)
    cosine = jnp.cos(angles)[:, None, :]
    sine_part = jnp.sin(angles)[:, None, :]
    first_half = inputs[..., :half_dim]
    second = inputs[..., half_dim:]
    return jnp.concatenate(
        [first_half * cosine - second * sine_part, second * cosine + first_half * sine_part],
        axis=-1,
    )


def layout(lengths, adapters, slot_adapter_index, places):
    req_ends = jnp.cumsum(lengths)
    starts = req_ends - lengths
    member = ((places[:, None] >= starts[None, :]) & (places[:, None] < req_ends[None, :])).astype(
        jnp.int32
    )
    request = jnp.sum(member * jnp.arange(lengths.shape[0], dtype=jnp.int32)[None, :], axis=1)
    position = places - jnp.sum(member * starts[None, :], axis=1)
    chosen = jnp.sum(member * adapters[None, :], axis=1)
    slot_ids = jnp.arange(slot_adapter_index.shape[0], dtype=jnp.int32)
    token_slot = jnp.sum(
        (chosen[:, None] == slot_adapter_index[None, :]).astype(jnp.int32) * slot_ids[None, :],
        axis=1,
    )
    return (request, position, token_slot)


def allowed_keys(request, position, window):
    distance = position[:, None] - position[None, :]
    return (
        (request[:, None] == request[None, :])
        & (distance >= 0)
        & ((distance < window) | (position[None, :] < SINKS))
    )


def attention(queries, key_heads, value_heads, request, position, window):
    scores = jnp.einsum(
        "qhd,khd->hqk", queries, key_heads, preferred_element_type=jnp.float32
    ) * HEAD_SIZE ** (-0.5)
    allowed = allowed_keys(request, position, window)
    scores = jnp.where(allowed[None, :, :], scores, -1e30)
    row_peak = jnp.max(scores, axis=-1, keepdims=True)
    weights = jnp.exp(scores - row_peak)
    weights = (weights / jnp.sum(weights, axis=-1, keepdims=True)).astype(jnp.bfloat16)
    context = jnp.einsum("hqk,khd->qhd", weights, value_heads, preferred_element_type=jnp.float32)
    return context.astype(jnp.bfloat16)


def hidden_units(states, gate_rows, up_rows):
    contract = (((1,), (1,)), ((), ()))
    gate_act = lax.dot_general(states, gate_rows, contract, preferred_element_type=jnp.float32)
    up_act = lax.dot_general(states, up_rows, contract, preferred_element_type=jnp.float32)
    return (jax.nn.silu(gate_act) * up_act).astype(jnp.bfloat16)


def exchange(block, axis):
    return lax.ppermute(block, axis, [(0, 1), (1, 0)])


def shift(block, hops):
    return lax.ppermute(block, "mlp", [((k + hops) % 4, k) for k in range(4)])


def line_gather(block):
    across = shift(block, 2)
    return [block, shift(block, 1), across, shift(block, 3)]


def line_scatter(parts):
    across = shift(parts[2], 2)
    arrived = (parts[0], shift(parts[3], 1), across, shift(parts[1], 3))
    return sum(part.astype(jnp.float32) for part in arrived)


def together(*values):
    return lax.optimization_barrier(values)


def four_pieces(rows, rows_x):
    return [rows, exchange(rows, "core"), rows_x, exchange(rows_x, "core")]


def vmem_call(kernel, outs, scratch, operands, vmem_mib):
    whole = pl.BlockSpec(memory_space=pltpu.VMEM)
    return pl.pallas_call(
        kernel,
        out_shape=outs,
        in_specs=[whole] * len(operands),
        out_specs=[whole] * len(outs),
        scratch_shapes=scratch,
        compiler_params=pltpu.CompilerParams(vmem_limit_bytes=vmem_mib << 20),
        cost_estimate=pl.CostEstimate(flops=1 << 20, bytes_accessed=1 << 20, transcendentals=0),
    )(*operands)


def in_hbm(array):
    return pltpu.with_memory_space_constraint(array, pltpu.HBM)


def staged(*groups, space=pltpu.VMEM):
    groups = [
        [piece if isinstance(piece, tuple) else (piece, 0, piece.shape[0]) for piece in group]
        for group in groups
    ]
    arrays = []
    for piece in (piece for group in groups for piece in group):
        if not any(piece[0] is array for array in arrays):
            arrays.append(piece[0])
    places = [
        [next(k for k, array in enumerate(arrays) if array is piece[0]) for piece in group]
        for group in groups
    ]
    count = sum(len(group) for group in groups)

    def kernel(*refs):
        sources, targets, sems = refs[: len(arrays)], refs[len(arrays) : -1], refs[-1]
        copies = []
        for group, place, target in zip(groups, places, targets):
            at = 0
            for (_, start, rows), k in zip(group, place):
                copies.append(
                    pltpu.make_async_copy(
                        sources[k].at[pl.ds(start, rows), :],
                        target.at[pl.ds(at, rows), :],
                        sems.at[len(copies)],
                    )
                )
                copies[-1].start()
                at += rows
        for copy in copies:
            copy.wait()

    outs = [(sum(piece[2] for piece in group), group[0][0].shape[1]) for group in groups]
    size = sum(rows * columns for rows, columns in outs)
    return pl.pallas_call(
        kernel,
        out_shape=[space(shape, group[0][0].dtype) for shape, group in zip(outs, groups)],
        in_specs=[pl.BlockSpec(memory_space=pl.ANY)] * len(arrays),
        out_specs=[pl.BlockSpec(memory_space=space)] * len(groups),
        scratch_shapes=[pltpu.SemaphoreType.DMA((count,))],
        compiler_params=pltpu.CompilerParams(vmem_limit_bytes=1 << 20),
        cost_estimate=pl.CostEstimate(flops=0, bytes_accessed=4 * size, transcendentals=0),
    )(*arrays)


NT = (((1,), (1,)), ((), ()))


def attention_kernel(
    block_0,
    block_1,
    block_2,
    block_3,
    query_weight,
    key_weight,
    value_weight,
    output_weight,
    query_down,
    value_down,
    query_up,
    value_up,
    query_gain,
    key_gain,
    cosine,
    sine,
    slot_mask,
    allowed,
    out_0,
    out_1,
    out_2,
    out_3,
    rows,
    context,
):
    tok_dev = block_0.shape[0]
    for k, block in enumerate((block_0, block_1, block_2, block_3)):
        rows[k * tok_dev : (k + 1) * tok_dev, :] = block[...]

    def project(weight):
        return jnp.dot(rows[...], weight[...], preferred_element_type=jnp.float32)

    def adapted(weight, down, up):
        low = project(down).astype(jnp.bfloat16) * slot_mask[...]
        return project(weight) + adapter_scale * jnp.dot(
            low, up[...], preferred_element_type=jnp.float32
        )

    def heads(inputs, gain):
        inputs = rms_scale(inputs) * gain
        turned = pltpu.roll(inputs, HEAD_SIZE // 2, 1)
        return (inputs * cosine[...] + turned * sine[...]).astype(jnp.bfloat16)

    queries = adapted(query_weight, query_down, query_up)
    keys = project(key_weight)
    values = adapted(value_weight, value_down, value_up).astype(jnp.bfloat16)
    for start in range(0, queries.shape[1], HEAD_SIZE):
        at = slice(start, start + HEAD_SIZE)
        scores = lax.dot_general(
            heads(queries[:, at], query_gain[:, at]),
            heads(keys[:, at], key_gain[:, at]),
            NT,
            preferred_element_type=jnp.float32,
        ) * HEAD_SIZE ** (-0.5)
        scores = jnp.where(allowed[...] > 0, scores, -1e30)
        weights = jnp.exp(scores - jnp.max(scores, axis=-1, keepdims=True))
        weights = (weights / jnp.sum(weights, axis=-1, keepdims=True)).astype(jnp.bfloat16)
        context[:, at] = jnp.dot(
            weights, values[:, at], preferred_element_type=jnp.float32
        ).astype(jnp.bfloat16)
    step = 1024
    for start in range(0, output_weight.shape[1], step):
        at = slice(start, start + step)
        part = jnp.dot(context[...], output_weight[:, at], preferred_element_type=jnp.float32)
        part = part.astype(jnp.bfloat16)
        for k, out in enumerate((out_0, out_1, out_2, out_3)):
            out[:, at] = part[k * tok_dev : (k + 1) * tok_dev]


def hidden_kernel(states, gate_rows, up_rows, out):
    step = 256
    for start in range(0, gate_rows.shape[0], step):
        at = slice(start, start + step)
        gate_act = lax.dot_general(
            states[...], gate_rows[at, :], NT, preferred_element_type=jnp.float32
        )
        up_act = lax.dot_general(
            states[...], up_rows[at, :], NT, preferred_element_type=jnp.float32
        )
        hidden = gate_act / (1.0 + jnp.exp(-gate_act)) * up_act
        out[:, at] = hidden.astype(jnp.bfloat16)


def down_kernel(own, other, far_own, far_other, near_rows, far_rows, out_0, out_1, out_2, out_3):
    tok_dev = out_0.shape[0] // 2
    step = 512
    for start in range(0, near_rows.shape[1], step):
        at = slice(start, start + step)
        for side, (near, far) in enumerate(((own, far_own), (other, far_other))):
            part = jnp.dot(near[...], near_rows[:, at], preferred_element_type=jnp.float32)
            part += jnp.dot(far[...], far_rows[:, at], preferred_element_type=jnp.float32)
            part = part.astype(jnp.bfloat16)
            for k, out in enumerate((out_0, out_1, out_2, out_3)):
                out[side * tok_dev : (side + 1) * tok_dev, at] = part[
                    k * tok_dev : (k + 1) * tok_dev
                ]


def add_normed(base, added, gain):
    return (base.astype(jnp.float32) + rms_scale(added) * gain).astype(jnp.bfloat16)


def layer_direct(
    layer_input, angles, slot_mask, allowed, projections, adapters, head_gains, gains, ffn_rows
):
    tok_dev, width = layer_input.shape
    gate_rows, up_rows, down_rows = ffn_rows
    y = lax.axis_index("y")
    half = width // 2
    units = gate_rows.shape[0]
    near = lax.dynamic_slice_in_dim(down_rows, y * half, half, axis=1)
    far = exchange(lax.dynamic_slice_in_dim(down_rows, (1 - y) * half, half, axis=1), "y")
    (gate_up,) = staged([in_hbm(gate_rows), in_hbm(up_rows)], space=pltpu.HBM)
    gate_up_x = exchange(gate_up, "x")
    cosine, sine = jnp.cos(angles), jnp.sin(angles)
    block = jax.ShapeDtypeStruct((tok_dev, width), jnp.bfloat16)
    *staged_rows, own_block = staged(
        *([in_hbm(array)] for array in (*projections, *adapters, *head_gains, layer_input))
    )
    *blocks, far = together(*line_gather(layer_input)[1:], far)
    parts = vmem_call(
        attention_kernel,
        [block] * 4,
        [
            pltpu.VMEM((4 * tok_dev, width), jnp.bfloat16),
            pltpu.VMEM((4 * tok_dev, projections[0].shape[1]), jnp.bfloat16),
        ],
        [
            own_block,
            *blocks,
            *staged_rows,
            jnp.concatenate([cosine, cosine], axis=1),
            jnp.concatenate([-sine, sine], axis=1),
            slot_mask,
            allowed,
        ],
        8,
    )
    near_x = [exchange(rows, "x") for rows in jnp.split(near, 2)]
    attn_own = line_scatter(parts)
    residual_own = add_normed(layer_input, attn_own, gains[0])
    own, *line, other = together(*line_gather(residual_own), exchange(residual_own, "y"))
    line, gate_up_x, near_x[0] = together(jnp.concatenate(line), gate_up_x, near_x[0])
    far_x = exchange(far, "x")
    pieces = [exchange(gate_up, "core"), gate_up_x, exchange(gate_up_x, "core")]
    gate_all, up_all = staged(
        [in_hbm(gate_rows), *((piece, 0, units) for piece in pieces)],
        [in_hbm(up_rows), *((piece, units, units) for piece in pieces)],
    )

    def hidden_units_of(first, others):
        (hidden,) = vmem_call(
            hidden_kernel,
            [jax.ShapeDtypeStruct((4 * tok_dev, gate_all.shape[0]), jnp.bfloat16)],
            [],
            [jnp.concatenate([first, others]), gate_all, up_all],
            8,
        )
        return hidden

    line_other = exchange(line, "y")
    hidden_own = hidden_units_of(own, line)
    line_other, hidden_own, far_x = together(line_other, hidden_own, far_x)
    from_own = exchange(hidden_own, "y")
    far_pieces = four_pieces(far, far_x)
    hidden_other, near_x[1] = together(hidden_units_of(other, line_other), near_x[1])
    from_other = exchange(hidden_other, "y")
    near_pieces = four_pieces(near, jnp.concatenate(near_x))
    from_own, *pieces = together(from_own, *near_pieces, *far_pieces)
    near_all, far_all = staged(pieces[:4], pieces[4:])
    parts = vmem_call(
        down_kernel,
        [jax.ShapeDtypeStruct((2 * tok_dev, half), jnp.bfloat16)] * 4,
        [],
        [hidden_own, hidden_other, from_other, from_own, near_all, far_all],
        8,
    )
    summed = line_scatter(parts)
    own_half = summed[:tok_dev]
    other_half = exchange(summed[tok_dev:].astype(jnp.bfloat16), "y").astype(jnp.float32)
    mlp_own = jnp.concatenate(
        [jnp.where(y == 1, other_half, own_half), jnp.where(y == 1, own_half, other_half)], axis=1
    )
    return add_normed(residual_own, mlp_own, gains[1])


def shards(
    layer_input,
    request_lengths,
    request_adapter,
    slot_adapter_index,
    query_weight,
    key_weight,
    value_weight,
    output_weight,
    query_norm_gain,
    key_norm_gain,
    query_down_factors,
    value_down_factors,
    query_up_factors,
    value_up_factors,
    attention_norm_gain,
    feedforward_norm_gain,
    gate_weight,
    up_weight,
    down_weight_transposed,
):
    tok_dev = layer_input.shape[0]
    tok_group = tok_dev * lax.axis_size("mlp")
    window = tok_group * 3 // 8
    heads_local = query_weight.shape[1] // HEAD_SIZE
    direct = [lax.axis_size(axis) for axis in (*REQ, "mlp")] == [2, 2, 2, 4]
    places = jnp.arange(tok_group, dtype=jnp.int32)
    if direct:
        places = (places + lax.axis_index("mlp") * tok_dev) % tok_group
    request, position, token_slot = layout(
        request_lengths[0], request_adapter[0], slot_adapter_index, places
    )
    columns = jnp.arange(ADAPTER_SLOTS * ADAPTER_RANK, dtype=jnp.int32) // ADAPTER_RANK
    slot_match_mask = (columns[None, :] == token_slot[:, None]).astype(jnp.bfloat16)
    gate_rows, up_rows, down_rows = gate_weight.T, up_weight.T, down_weight_transposed.T
    if direct:
        return layer_direct(
            layer_input,
            rotary_angles(position),
            slot_match_mask,
            allowed_keys(request, position, window).astype(jnp.float32),
            (query_weight, key_weight, value_weight, output_weight),
            (query_down_factors, value_down_factors, query_up_factors, value_up_factors),
            (query_norm_gain[None, :], key_norm_gain[None, :]),
            (attention_norm_gain, feedforward_norm_gain),
            (gate_rows, up_rows, down_rows),
        )
    group_token_rows = lax.all_gather(layer_input, "mlp", axis=0, tiled=True)
    query_reduced = (
        jnp.dot(group_token_rows, query_down_factors, preferred_element_type=jnp.float32).astype(
            jnp.bfloat16
        )
        * slot_match_mask
    )
    value_reduced = (
        jnp.dot(group_token_rows, value_down_factors, preferred_element_type=jnp.float32).astype(
            jnp.bfloat16
        )
        * slot_match_mask
    )
    query_before_norm = jnp.dot(
        group_token_rows, query_weight, preferred_element_type=jnp.float32
    ) + adapter_scale * jnp.dot(query_reduced, query_up_factors, preferred_element_type=jnp.float32)
    key_pre = jnp.dot(group_token_rows, key_weight, preferred_element_type=jnp.float32)
    value_before_adapter = jnp.dot(
        group_token_rows, value_weight, preferred_element_type=jnp.float32
    ) + adapter_scale * jnp.dot(value_reduced, value_up_factors, preferred_element_type=jnp.float32)
    queries = rotary(
        rms_scale(query_before_norm.reshape(tok_group, heads_local, HEAD_SIZE))
        * query_norm_gain.reshape(heads_local, HEAD_SIZE),
        position,
    ).astype(jnp.bfloat16)
    key_heads = rotary(
        rms_scale(key_pre.reshape(tok_group, heads_local, HEAD_SIZE))
        * key_norm_gain.reshape(heads_local, HEAD_SIZE),
        position,
    ).astype(jnp.bfloat16)
    value_heads = value_before_adapter.astype(jnp.bfloat16).reshape(
        tok_group, heads_local, HEAD_SIZE
    )
    context = attention(queries, key_heads, value_heads, request, position, window).reshape(
        tok_group, heads_local * HEAD_SIZE
    )
    attn_own = lax.psum_scatter(
        jnp.dot(context, output_weight, preferred_element_type=jnp.float32).astype(jnp.bfloat16),
        "mlp",
        scatter_dimension=0,
        tiled=True,
    ).astype(jnp.float32)
    residual_own = add_normed(layer_input, attn_own, attention_norm_gain)
    gate_rows, up_rows, down_rows = (
        lax.all_gather(rows, REQ, axis=0, tiled=True) for rows in (gate_rows, up_rows, down_rows)
    )
    hidden = hidden_units(
        lax.all_gather(residual_own, "mlp", axis=0, tiled=True), gate_rows, up_rows
    )
    part = jnp.dot(hidden, down_rows, preferred_element_type=jnp.float32)
    mlp_own = lax.psum_scatter(
        part.astype(jnp.bfloat16), "mlp", scatter_dimension=0, tiled=True
    ).astype(jnp.float32)
    return add_normed(residual_own, mlp_own, feedforward_norm_gain)


def solution(mesh):
    req, mlp = mesh.devices.shape
    side = math.isqrt(req // 2)
    fine = Mesh(mesh.devices.reshape(req // 2 // side, side, 2, mlp), ("y", "x", "core", "mlp"))
    return jax.shard_map(
        shards,
        mesh=fine,
        in_specs=(
            P((*REQ, "mlp"), None),
            P(REQ, None),
            P(REQ, None),
            P(),
            P(None, "mlp"),
            P(None, "mlp"),
            P(None, "mlp"),
            P("mlp", None),
            P("mlp"),
            P("mlp"),
            P(),
            P(),
            P(None, "mlp"),
            P(None, "mlp"),
            P(),
            P(),
            P(None, (*REQ, "mlp")),
            P(None, (*REQ, "mlp")),
            P(None, (*REQ, "mlp")),
        ),
        out_specs=P((*REQ, "mlp"), None),
        check_vma=False,
    )
```

```python
import math

import jax
import jax.numpy as jnp
from jax import lax
from jax.experimental import pallas as pl
from jax.experimental.pallas import tpu as pltpu
from jax.sharding import Mesh, PartitionSpec as P

HEAD_SIZE = 128
ADAPTER_RANK = 16
ADAPTER_SLOTS = 8
SINKS = 4
REQ = ("y", "x", "core")


epsilon = 1e-06
adapter_scale = 0.5
rope_theta = 500000.0


def rms_scale(inputs):
    return inputs * lax.rsqrt(jnp.mean(inputs * inputs, axis=-1, keepdims=True) + epsilon)


def rotary_angles(position):
    exponent = jnp.arange(HEAD_SIZE // 2, dtype=jnp.float32) * (2.0 / HEAD_SIZE)
    frequency = rope_theta ** (-exponent)
    return position.astype(jnp.float32)[:, None] * frequency[None, :]


def rotary(inputs, position):
    half_dim = inputs.shape[-1] // 2
    angles = rotary_angles(position)
    cosine = jnp.cos(angles)[:, None, :]
    sine_part = jnp.sin(angles)[:, None, :]
    first_half = inputs[..., :half_dim]
    second = inputs[..., half_dim:]
    return jnp.concatenate(
        [first_half * cosine - second * sine_part, second * cosine + first_half * sine_part],
        axis=-1,
    )


def layout(lengths, adapters, slot_adapter_index, places):
    req_ends = jnp.cumsum(lengths)
    starts = req_ends - lengths
    member = ((places[:, None] >= starts[None, :]) & (places[:, None] < req_ends[None, :])).astype(
        jnp.int32
    )
    request = jnp.sum(member * jnp.arange(lengths.shape[0], dtype=jnp.int32)[None, :], axis=1)
    position = places - jnp.sum(member * starts[None, :], axis=1)
    chosen = jnp.sum(member * adapters[None, :], axis=1)
    slot_ids = jnp.arange(slot_adapter_index.shape[0], dtype=jnp.int32)
    token_slot = jnp.sum(
        (chosen[:, None] == slot_adapter_index[None, :]).astype(jnp.int32) * slot_ids[None, :],
        axis=1,
    )
    return (request, position, token_slot)


def allowed_keys(request, position, window):
    distance = position[:, None] - position[None, :]
    return (
        (request[:, None] == request[None, :])
        & (distance >= 0)
        & ((distance < window) | (position[None, :] < SINKS))
    )


def attention(queries, key_heads, value_heads, request, position, window):
    scores = jnp.einsum(
        "qhd,khd->hqk", queries, key_heads, preferred_element_type=jnp.float32
    ) * HEAD_SIZE ** (-0.5)
    allowed = allowed_keys(request, position, window)
    scores = jnp.where(allowed[None, :, :], scores, -1e30)
    row_peak = jnp.max(scores, axis=-1, keepdims=True)
    weights = jnp.exp(scores - row_peak)
    weights = (weights / jnp.sum(weights, axis=-1, keepdims=True)).astype(jnp.bfloat16)
    context = jnp.einsum("hqk,khd->qhd", weights, value_heads, preferred_element_type=jnp.float32)
    return context.astype(jnp.bfloat16)


def hidden_units(states, gate_rows, up_rows):
    contract = (((1,), (1,)), ((), ()))
    gate_act = lax.dot_general(states, gate_rows, contract, preferred_element_type=jnp.float32)
    up_act = lax.dot_general(states, up_rows, contract, preferred_element_type=jnp.float32)
    return (jax.nn.silu(gate_act) * up_act).astype(jnp.bfloat16)


def exchange(block, axis):
    return lax.ppermute(block, axis, [(0, 1), (1, 0)])


def shift(block, hops):
    return lax.ppermute(block, "mlp", [((k + hops) % 4, k) for k in range(4)])


def line_gather(block):
    across = shift(block, 2)
    return [block, shift(block, 1), across, shift(block, 3)]


def line_scatter(parts):
    across = shift(parts[2], 2)
    arrived = (parts[0], shift(parts[3], 1), across, shift(parts[1], 3))
    return sum(part.astype(jnp.float32) for part in arrived)


def together(*values):
    return lax.optimization_barrier(values)


def four_pieces(rows, rows_x):
    return [rows, exchange(rows, "core"), rows_x, exchange(rows_x, "core")]


def vmem_call(kernel, outs, scratch, operands, vmem_mib):
    whole = pl.BlockSpec(memory_space=pltpu.VMEM)
    return pl.pallas_call(
        kernel,
        out_shape=outs,
        in_specs=[whole] * len(operands),
        out_specs=[whole] * len(outs),
        scratch_shapes=scratch,
        compiler_params=pltpu.CompilerParams(vmem_limit_bytes=vmem_mib << 20),
        cost_estimate=pl.CostEstimate(flops=1 << 20, bytes_accessed=1 << 20, transcendentals=0),
    )(*operands)


def in_hbm(array):
    return pltpu.with_memory_space_constraint(array, pltpu.HBM)


def staged(*groups):
    groups = [
        [piece if isinstance(piece, tuple) else (piece, 0, piece.shape[0]) for piece in group]
        for group in groups
    ]
    arrays = []
    for piece in (piece for group in groups for piece in group):
        if not any(piece[0] is array for array in arrays):
            arrays.append(piece[0])
    places = [
        [next(k for k, array in enumerate(arrays) if array is piece[0]) for piece in group]
        for group in groups
    ]
    count = sum(len(group) for group in groups)

    def kernel(*refs):
        sources, targets, sems = refs[: len(arrays)], refs[len(arrays) : -1], refs[-1]
        copies = []
        for group, place, target in zip(groups, places, targets):
            at = 0
            for (_, start, rows), k in zip(group, place):
                copies.append(
                    pltpu.make_async_copy(
                        sources[k].at[pl.ds(start, rows), :],
                        target.at[pl.ds(at, rows), :],
                        sems.at[len(copies)],
                    )
                )
                copies[-1].start()
                at += rows
        for copy in copies:
            copy.wait()

    outs = [(sum(piece[2] for piece in group), group[0][0].shape[1]) for group in groups]
    size = sum(rows * columns for rows, columns in outs)
    return pl.pallas_call(
        kernel,
        out_shape=[pltpu.VMEM(shape, group[0][0].dtype) for shape, group in zip(outs, groups)],
        in_specs=[pl.BlockSpec(memory_space=pl.ANY)] * len(arrays),
        out_specs=[pl.BlockSpec(memory_space=pltpu.VMEM)] * len(groups),
        scratch_shapes=[pltpu.SemaphoreType.DMA((count,))],
        compiler_params=pltpu.CompilerParams(vmem_limit_bytes=1 << 20),
        cost_estimate=pl.CostEstimate(flops=0, bytes_accessed=4 * size, transcendentals=0),
    )(*arrays)


def stacked(*arrays):
    rows, columns = arrays[0].shape

    def kernel(*refs):
        sources, target, buffer, sems_in, sems_out = refs[:-4], *refs[-4:]
        into = [
            pltpu.make_async_copy(source, buffer.at[k], sems_in.at[k])
            for k, source in enumerate(sources)
        ]
        out = [
            pltpu.make_async_copy(
                buffer.at[k], target.at[pl.ds(k * rows, rows), :], sems_out.at[k]
            )
            for k in range(len(sources))
        ]
        for copy in into:
            copy.start()
        for copy_in, copy_out in zip(into, out):
            copy_in.wait()
            copy_out.start()
        for copy in out:
            copy.wait()

    count = len(arrays)
    return pl.pallas_call(
        kernel,
        out_shape=pltpu.HBM((count * rows, columns), arrays[0].dtype),
        in_specs=[pl.BlockSpec(memory_space=pl.ANY)] * count,
        out_specs=pl.BlockSpec(memory_space=pltpu.HBM),
        scratch_shapes=[
            pltpu.VMEM((count, rows, columns), arrays[0].dtype),
            pltpu.SemaphoreType.DMA((count,)),
            pltpu.SemaphoreType.DMA((count,)),
        ],
        compiler_params=pltpu.CompilerParams(vmem_limit_bytes=8 << 20),
        cost_estimate=pl.CostEstimate(flops=0, bytes_accessed=1 << 20, transcendentals=0),
    )(*(in_hbm(array) for array in arrays))


NT = (((1,), (1,)), ((), ()))


def attention_kernel(
    block_0,
    block_1,
    block_2,
    block_3,
    query_weight,
    key_weight,
    value_weight,
    output_weight,
    query_down,
    value_down,
    query_up,
    value_up,
    query_gain,
    key_gain,
    cosine,
    sine,
    slot_mask,
    allowed,
    out_0,
    out_1,
    out_2,
    out_3,
    rows,
    context,
):
    tok_dev = block_0.shape[0]
    for k, block in enumerate((block_0, block_1, block_2, block_3)):
        rows[k * tok_dev : (k + 1) * tok_dev, :] = block[...]

    def project(weight):
        return jnp.dot(rows[...], weight[...], preferred_element_type=jnp.float32)

    def adapted(weight, down, up):
        low = project(down).astype(jnp.bfloat16) * slot_mask[...]
        return project(weight) + adapter_scale * jnp.dot(
            low, up[...], preferred_element_type=jnp.float32
        )

    def heads(inputs, gain):
        inputs = rms_scale(inputs) * gain
        turned = pltpu.roll(inputs, HEAD_SIZE // 2, 1)
        return (inputs * cosine[...] + turned * sine[...]).astype(jnp.bfloat16)

    queries = adapted(query_weight, query_down, query_up)
    keys = project(key_weight)
    values = adapted(value_weight, value_down, value_up).astype(jnp.bfloat16)
    for start in range(0, queries.shape[1], HEAD_SIZE):
        at = slice(start, start + HEAD_SIZE)
        scores = lax.dot_general(
            heads(queries[:, at], query_gain[:, at]),
            heads(keys[:, at], key_gain[:, at]),
            NT,
            preferred_element_type=jnp.float32,
        ) * HEAD_SIZE ** (-0.5)
        scores = jnp.where(allowed[...] > 0, scores, -1e30)
        weights = jnp.exp(scores - jnp.max(scores, axis=-1, keepdims=True))
        weights = (weights / jnp.sum(weights, axis=-1, keepdims=True)).astype(jnp.bfloat16)
        context[:, at] = jnp.dot(
            weights, values[:, at], preferred_element_type=jnp.float32
        ).astype(jnp.bfloat16)
    step = 1024
    for start in range(0, output_weight.shape[1], step):
        at = slice(start, start + step)
        part = jnp.dot(context[...], output_weight[:, at], preferred_element_type=jnp.float32)
        part = part.astype(jnp.bfloat16)
        for k, out in enumerate((out_0, out_1, out_2, out_3)):
            out[:, at] = part[k * tok_dev : (k + 1) * tok_dev]


def hidden_kernel(states, gate_rows, up_rows, out):
    step = 256
    for start in range(0, gate_rows.shape[0], step):
        at = slice(start, start + step)
        gate_act = lax.dot_general(
            states[...], gate_rows[at, :], NT, preferred_element_type=jnp.float32
        )
        up_act = lax.dot_general(
            states[...], up_rows[at, :], NT, preferred_element_type=jnp.float32
        )
        hidden = gate_act / (1.0 + jnp.exp(-gate_act)) * up_act
        out[:, at] = hidden.astype(jnp.bfloat16)


def down_kernel(own, other, far_own, far_other, near_rows, far_rows, out_0, out_1, out_2, out_3):
    tok_dev = out_0.shape[0] // 2
    step = 512
    for start in range(0, near_rows.shape[1], step):
        at = slice(start, start + step)
        for side, (near, far) in enumerate(((own, far_own), (other, far_other))):
            part = jnp.dot(near[...], near_rows[:, at], preferred_element_type=jnp.float32)
            part += jnp.dot(far[...], far_rows[:, at], preferred_element_type=jnp.float32)
            part = part.astype(jnp.bfloat16)
            for k, out in enumerate((out_0, out_1, out_2, out_3)):
                out[side * tok_dev : (side + 1) * tok_dev, at] = part[
                    k * tok_dev : (k + 1) * tok_dev
                ]


def add_normed(base, added, gain):
    return (base.astype(jnp.float32) + rms_scale(added) * gain).astype(jnp.bfloat16)


def layer_direct(
    layer_input, angles, slot_mask, allowed, projections, adapters, head_gains, gains, ffn_rows
):
    tok_dev, width = layer_input.shape
    gate_rows, up_rows, down_rows = ffn_rows
    y = lax.axis_index("y")
    half = width // 2
    units = gate_rows.shape[0]
    near = lax.dynamic_slice_in_dim(down_rows, y * half, half, axis=1)
    far = exchange(lax.dynamic_slice_in_dim(down_rows, (1 - y) * half, half, axis=1), "y")
    gate_up = stacked(gate_rows, up_rows)
    gate_up_x = exchange(gate_up, "x")
    cosine, sine = jnp.cos(angles), jnp.sin(angles)
    block = jax.ShapeDtypeStruct((tok_dev, width), jnp.bfloat16)
    *staged_rows, own_block = staged(
        *([in_hbm(array)] for array in (*projections, *adapters, *head_gains, layer_input))
    )
    *blocks, far = together(*line_gather(layer_input)[1:], far)
    parts = vmem_call(
        attention_kernel,
        [block] * 4,
        [
            pltpu.VMEM((4 * tok_dev, width), jnp.bfloat16),
            pltpu.VMEM((4 * tok_dev, projections[0].shape[1]), jnp.bfloat16),
        ],
        [
            own_block,
            *blocks,
            *staged_rows,
            jnp.concatenate([cosine, cosine], axis=1),
            jnp.concatenate([-sine, sine], axis=1),
            slot_mask,
            allowed,
        ],
        8,
    )
    near_x = [exchange(rows, "x") for rows in jnp.split(near, 2)]
    attn_own = line_scatter(parts)
    residual_own = add_normed(layer_input, attn_own, gains[0])
    own, *line, other = together(*line_gather(residual_own), exchange(residual_own, "y"))
    line, gate_up_x, near_x[0] = together(jnp.concatenate(line), gate_up_x, near_x[0])
    far_x = exchange(far, "x")
    pieces = [exchange(gate_up, "core"), gate_up_x, exchange(gate_up_x, "core")]
    gate_all, up_all = staged(
        [in_hbm(gate_rows), *((piece, 0, units) for piece in pieces)],
        [in_hbm(up_rows), *((piece, units, units) for piece in pieces)],
    )

    def hidden_units_of(first, others):
        (hidden,) = vmem_call(
            hidden_kernel,
            [jax.ShapeDtypeStruct((4 * tok_dev, gate_all.shape[0]), jnp.bfloat16)],
            [],
            [jnp.concatenate([first, others]), gate_all, up_all],
            8,
        )
        return hidden

    line_other = exchange(line, "y")
    hidden_own = hidden_units_of(own, line)
    line_other, hidden_own, far_x = together(line_other, hidden_own, far_x)
    from_own = exchange(hidden_own, "y")
    far_pieces = four_pieces(far, far_x)
    hidden_other, near_x[1] = together(hidden_units_of(other, line_other), near_x[1])
    from_other = exchange(hidden_other, "y")
    near_pieces = four_pieces(near, jnp.concatenate(near_x))
    from_own, *pieces = together(from_own, *near_pieces, *far_pieces)
    near_all, far_all = staged(pieces[:4], pieces[4:])
    parts = vmem_call(
        down_kernel,
        [jax.ShapeDtypeStruct((2 * tok_dev, half), jnp.bfloat16)] * 4,
        [],
        [hidden_own, hidden_other, from_other, from_own, near_all, far_all],
        8,
    )
    summed = line_scatter(parts)
    own_half = summed[:tok_dev]
    other_half = exchange(summed[tok_dev:].astype(jnp.bfloat16), "y").astype(jnp.float32)
    mlp_own = jnp.concatenate(
        [jnp.where(y == 1, other_half, own_half), jnp.where(y == 1, own_half, other_half)], axis=1
    )
    return add_normed(residual_own, mlp_own, gains[1])


def shards(
    layer_input,
    request_lengths,
    request_adapter,
    slot_adapter_index,
    query_weight,
    key_weight,
    value_weight,
    output_weight,
    query_norm_gain,
    key_norm_gain,
    query_down_factors,
    value_down_factors,
    query_up_factors,
    value_up_factors,
    attention_norm_gain,
    feedforward_norm_gain,
    gate_weight,
    up_weight,
    down_weight_transposed,
):
    tok_dev = layer_input.shape[0]
    tok_group = tok_dev * lax.axis_size("mlp")
    window = tok_group * 3 // 8
    heads_local = query_weight.shape[1] // HEAD_SIZE
    direct = [lax.axis_size(axis) for axis in (*REQ, "mlp")] == [2, 2, 2, 4]
    places = jnp.arange(tok_group, dtype=jnp.int32)
    if direct:
        places = (places + lax.axis_index("mlp") * tok_dev) % tok_group
    request, position, token_slot = layout(
        request_lengths[0], request_adapter[0], slot_adapter_index, places
    )
    columns = jnp.arange(ADAPTER_SLOTS * ADAPTER_RANK, dtype=jnp.int32) // ADAPTER_RANK
    slot_match_mask = (columns[None, :] == token_slot[:, None]).astype(jnp.bfloat16)
    gate_rows, up_rows, down_rows = gate_weight.T, up_weight.T, down_weight_transposed.T
    if direct:
        return layer_direct(
            layer_input,
            rotary_angles(position),
            slot_match_mask,
            allowed_keys(request, position, window).astype(jnp.float32),
            (query_weight, key_weight, value_weight, output_weight),
            (query_down_factors, value_down_factors, query_up_factors, value_up_factors),
            (query_norm_gain[None, :], key_norm_gain[None, :]),
            (attention_norm_gain, feedforward_norm_gain),
            (gate_rows, up_rows, down_rows),
        )
    group_token_rows = lax.all_gather(layer_input, "mlp", axis=0, tiled=True)
    query_reduced = (
        jnp.dot(group_token_rows, query_down_factors, preferred_element_type=jnp.float32).astype(
            jnp.bfloat16
        )
        * slot_match_mask
    )
    value_reduced = (
        jnp.dot(group_token_rows, value_down_factors, preferred_element_type=jnp.float32).astype(
            jnp.bfloat16
        )
        * slot_match_mask
    )
    query_before_norm = jnp.dot(
        group_token_rows, query_weight, preferred_element_type=jnp.float32
    ) + adapter_scale * jnp.dot(query_reduced, query_up_factors, preferred_element_type=jnp.float32)
    key_pre = jnp.dot(group_token_rows, key_weight, preferred_element_type=jnp.float32)
    value_before_adapter = jnp.dot(
        group_token_rows, value_weight, preferred_element_type=jnp.float32
    ) + adapter_scale * jnp.dot(value_reduced, value_up_factors, preferred_element_type=jnp.float32)
    queries = rotary(
        rms_scale(query_before_norm.reshape(tok_group, heads_local, HEAD_SIZE))
        * query_norm_gain.reshape(heads_local, HEAD_SIZE),
        position,
    ).astype(jnp.bfloat16)
    key_heads = rotary(
        rms_scale(key_pre.reshape(tok_group, heads_local, HEAD_SIZE))
        * key_norm_gain.reshape(heads_local, HEAD_SIZE),
        position,
    ).astype(jnp.bfloat16)
    value_heads = value_before_adapter.astype(jnp.bfloat16).reshape(
        tok_group, heads_local, HEAD_SIZE
    )
    context = attention(queries, key_heads, value_heads, request, position, window).reshape(
        tok_group, heads_local * HEAD_SIZE
    )
    attn_own = lax.psum_scatter(
        jnp.dot(context, output_weight, preferred_element_type=jnp.float32).astype(jnp.bfloat16),
        "mlp",
        scatter_dimension=0,
        tiled=True,
    ).astype(jnp.float32)
    residual_own = add_normed(layer_input, attn_own, attention_norm_gain)
    gate_rows, up_rows, down_rows = (
        lax.all_gather(rows, REQ, axis=0, tiled=True) for rows in (gate_rows, up_rows, down_rows)
    )
    hidden = hidden_units(
        lax.all_gather(residual_own, "mlp", axis=0, tiled=True), gate_rows, up_rows
    )
    part = jnp.dot(hidden, down_rows, preferred_element_type=jnp.float32)
    mlp_own = lax.psum_scatter(
        part.astype(jnp.bfloat16), "mlp", scatter_dimension=0, tiled=True
    ).astype(jnp.float32)
    return add_normed(residual_own, mlp_own, feedforward_norm_gain)


def solution(mesh):
    req, mlp = mesh.devices.shape
    side = math.isqrt(req // 2)
    fine = Mesh(mesh.devices.reshape(req // 2 // side, side, 2, mlp), ("y", "x", "core", "mlp"))
    return jax.shard_map(
        shards,
        mesh=fine,
        in_specs=(
            P((*REQ, "mlp"), None),
            P(REQ, None),
            P(REQ, None),
            P(),
            P(None, "mlp"),
            P(None, "mlp"),
            P(None, "mlp"),
            P("mlp", None),
            P("mlp"),
            P("mlp"),
            P(),
            P(),
            P(None, "mlp"),
            P(None, "mlp"),
            P(),
            P(),
            P(None, (*REQ, "mlp")),
            P(None, (*REQ, "mlp")),
            P(None, (*REQ, "mlp")),
        ),
        out_specs=P((*REQ, "mlp"), None),
        check_vma=False,
    )
```

```python
import math

import jax
import jax.numpy as jnp
from jax import lax
from jax.experimental import pallas as pl
from jax.experimental.pallas import tpu as pltpu
from jax.sharding import Mesh, PartitionSpec as P

HEAD_SIZE = 128
ADAPTER_RANK = 16
ADAPTER_SLOTS = 8
SINKS = 4
REQ = ("y", "x", "core")


epsilon = 1e-06
adapter_scale = 0.5
rope_theta = 500000.0


def rms_scale(inputs):
    return inputs * lax.rsqrt(jnp.mean(inputs * inputs, axis=-1, keepdims=True) + epsilon)


def rotary_angles(position):
    exponent = jnp.arange(HEAD_SIZE // 2, dtype=jnp.float32) * (2.0 / HEAD_SIZE)
    frequency = rope_theta ** (-exponent)
    return position.astype(jnp.float32)[:, None] * frequency[None, :]


def rotary(inputs, position):
    half_dim = inputs.shape[-1] // 2
    angles = rotary_angles(position)
    cosine = jnp.cos(angles)[:, None, :]
    sine_part = jnp.sin(angles)[:, None, :]
    first_half = inputs[..., :half_dim]
    second = inputs[..., half_dim:]
    return jnp.concatenate(
        [first_half * cosine - second * sine_part, second * cosine + first_half * sine_part],
        axis=-1,
    )


def layout(lengths, adapters, slot_adapter_index, places):
    req_ends = jnp.cumsum(lengths)
    starts = req_ends - lengths
    member = ((places[:, None] >= starts[None, :]) & (places[:, None] < req_ends[None, :])).astype(
        jnp.int32
    )
    request = jnp.sum(member * jnp.arange(lengths.shape[0], dtype=jnp.int32)[None, :], axis=1)
    position = places - jnp.sum(member * starts[None, :], axis=1)
    chosen = jnp.sum(member * adapters[None, :], axis=1)
    slot_ids = jnp.arange(slot_adapter_index.shape[0], dtype=jnp.int32)
    token_slot = jnp.sum(
        (chosen[:, None] == slot_adapter_index[None, :]).astype(jnp.int32) * slot_ids[None, :],
        axis=1,
    )
    return (request, position, token_slot)


def allowed_keys(request, position, window):
    distance = position[:, None] - position[None, :]
    return (
        (request[:, None] == request[None, :])
        & (distance >= 0)
        & ((distance < window) | (position[None, :] < SINKS))
    )


def attention(queries, key_heads, value_heads, request, position, window):
    scores = jnp.einsum(
        "qhd,khd->hqk", queries, key_heads, preferred_element_type=jnp.float32
    ) * HEAD_SIZE ** (-0.5)
    allowed = allowed_keys(request, position, window)
    scores = jnp.where(allowed[None, :, :], scores, -1e30)
    row_peak = jnp.max(scores, axis=-1, keepdims=True)
    weights = jnp.exp(scores - row_peak)
    weights = (weights / jnp.sum(weights, axis=-1, keepdims=True)).astype(jnp.bfloat16)
    context = jnp.einsum("hqk,khd->qhd", weights, value_heads, preferred_element_type=jnp.float32)
    return context.astype(jnp.bfloat16)


def hidden_units(states, gate_rows, up_rows):
    contract = (((1,), (1,)), ((), ()))
    gate_act = lax.dot_general(states, gate_rows, contract, preferred_element_type=jnp.float32)
    up_act = lax.dot_general(states, up_rows, contract, preferred_element_type=jnp.float32)
    return (jax.nn.silu(gate_act) * up_act).astype(jnp.bfloat16)


def exchange(block, axis):
    return lax.ppermute(block, axis, [(0, 1), (1, 0)])


def shift(block, hops):
    return lax.ppermute(block, "mlp", [((k + hops) % 4, k) for k in range(4)])


def line_gather(block):
    across = shift(block, 2)
    return [block, shift(block, 1), across, shift(block, 3)]


def line_scatter(parts):
    across = shift(parts[2], 2)
    arrived = (parts[0], shift(parts[3], 1), across, shift(parts[1], 3))
    return sum(part.astype(jnp.float32) for part in arrived)


def together(*values):
    return lax.optimization_barrier(values)


def four_pieces(rows, rows_x):
    return [rows, exchange(rows, "core"), rows_x, exchange(rows_x, "core")]


def vmem_call(kernel, outs, scratch, operands, vmem_mib):
    whole = pl.BlockSpec(memory_space=pltpu.VMEM)
    return pl.pallas_call(
        kernel,
        out_shape=outs,
        in_specs=[whole] * len(operands),
        out_specs=[whole] * len(outs),
        scratch_shapes=scratch,
        compiler_params=pltpu.CompilerParams(vmem_limit_bytes=vmem_mib << 20),
        cost_estimate=pl.CostEstimate(flops=1 << 20, bytes_accessed=1 << 20, transcendentals=0),
    )(*operands)


def in_hbm(array):
    return pltpu.with_memory_space_constraint(array, pltpu.HBM)


def staged(*groups):
    groups = [
        [piece if isinstance(piece, tuple) else (piece, 0, piece.shape[0]) for piece in group]
        for group in groups
    ]
    arrays = []
    for piece in (piece for group in groups for piece in group):
        if not any(piece[0] is array for array in arrays):
            arrays.append(piece[0])
    places = [
        [next(k for k, array in enumerate(arrays) if array is piece[0]) for piece in group]
        for group in groups
    ]
    count = sum(len(group) for group in groups)

    def kernel(*refs):
        sources, targets, sems = refs[: len(arrays)], refs[len(arrays) : -1], refs[-1]
        copies = []
        for group, place, target in zip(groups, places, targets):
            at = 0
            for (_, start, rows), k in zip(group, place):
                copies.append(
                    pltpu.make_async_copy(
                        sources[k].at[pl.ds(start, rows), :],
                        target.at[pl.ds(at, rows), :],
                        sems.at[len(copies)],
                    )
                )
                copies[-1].start()
                at += rows
        for copy in copies:
            copy.wait()

    outs = [(sum(piece[2] for piece in group), group[0][0].shape[1]) for group in groups]
    size = sum(rows * columns for rows, columns in outs)
    return pl.pallas_call(
        kernel,
        out_shape=[pltpu.VMEM(shape, group[0][0].dtype) for shape, group in zip(outs, groups)],
        in_specs=[pl.BlockSpec(memory_space=pl.ANY)] * len(arrays),
        out_specs=[pl.BlockSpec(memory_space=pltpu.VMEM)] * len(groups),
        scratch_shapes=[pltpu.SemaphoreType.DMA((count,))],
        compiler_params=pltpu.CompilerParams(vmem_limit_bytes=1 << 20),
        cost_estimate=pl.CostEstimate(flops=0, bytes_accessed=4 * size, transcendentals=0),
    )(*arrays)


def stacked(*arrays):
    rows, columns = arrays[0].shape

    def kernel(*refs):
        sources, target, buffer, sems_in, sems_out = refs[:-4], *refs[-4:]
        into = [
            pltpu.make_async_copy(source, buffer.at[k], sems_in.at[k])
            for k, source in enumerate(sources)
        ]
        out = [
            pltpu.make_async_copy(
                buffer.at[k], target.at[pl.ds(k * rows, rows), :], sems_out.at[k]
            )
            for k in range(len(sources))
        ]
        for copy in into:
            copy.start()
        for copy_in, copy_out in zip(into, out):
            copy_in.wait()
            copy_out.start()
        for copy in out:
            copy.wait()

    count = len(arrays)
    return pl.pallas_call(
        kernel,
        out_shape=pltpu.HBM((count * rows, columns), arrays[0].dtype),
        in_specs=[pl.BlockSpec(memory_space=pl.ANY)] * count,
        out_specs=pl.BlockSpec(memory_space=pltpu.HBM),
        scratch_shapes=[
            pltpu.VMEM((count, rows, columns), arrays[0].dtype),
            pltpu.SemaphoreType.DMA((count,)),
            pltpu.SemaphoreType.DMA((count,)),
        ],
        compiler_params=pltpu.CompilerParams(vmem_limit_bytes=8 << 20),
        cost_estimate=pl.CostEstimate(flops=0, bytes_accessed=1 << 20, transcendentals=0),
    )(*(in_hbm(array) for array in arrays))


NT = (((1,), (1,)), ((), ()))


def attention_kernel(
    block_0,
    block_1,
    block_2,
    block_3,
    query_weight,
    key_weight,
    value_weight,
    output_weight,
    query_down,
    value_down,
    query_up,
    value_up,
    query_gain,
    key_gain,
    cosine,
    sine,
    slot_mask,
    allowed,
    out_0,
    out_1,
    out_2,
    out_3,
    rows,
    context,
):
    tok_dev = block_0.shape[0]
    for k, block in enumerate((block_0, block_1, block_2, block_3)):
        rows[k * tok_dev : (k + 1) * tok_dev, :] = block[...]

    def project(weight):
        return jnp.dot(rows[...], weight[...], preferred_element_type=jnp.float32)

    def adapted(weight, down, up):
        low = project(down).astype(jnp.bfloat16) * slot_mask[...]
        return project(weight) + adapter_scale * jnp.dot(
            low, up[...], preferred_element_type=jnp.float32
        )

    def heads(inputs, gain):
        inputs = rms_scale(inputs) * gain
        turned = pltpu.roll(inputs, HEAD_SIZE // 2, 1)
        return (inputs * cosine[...] + turned * sine[...]).astype(jnp.bfloat16)

    queries = adapted(query_weight, query_down, query_up)
    keys = project(key_weight)
    values = adapted(value_weight, value_down, value_up).astype(jnp.bfloat16)
    for start in range(0, queries.shape[1], HEAD_SIZE):
        at = slice(start, start + HEAD_SIZE)
        scores = lax.dot_general(
            heads(queries[:, at], query_gain[:, at]),
            heads(keys[:, at], key_gain[:, at]),
            NT,
            preferred_element_type=jnp.float32,
        ) * HEAD_SIZE ** (-0.5)
        scores = jnp.where(allowed[...] > 0, scores, -1e30)
        weights = jnp.exp(scores - jnp.max(scores, axis=-1, keepdims=True))
        weights = (weights / jnp.sum(weights, axis=-1, keepdims=True)).astype(jnp.bfloat16)
        context[:, at] = jnp.dot(
            weights, values[:, at], preferred_element_type=jnp.float32
        ).astype(jnp.bfloat16)
    step = 1024
    for start in range(0, output_weight.shape[1], step):
        at = slice(start, start + step)
        part = jnp.dot(context[...], output_weight[:, at], preferred_element_type=jnp.float32)
        part = part.astype(jnp.bfloat16)
        for k, out in enumerate((out_0, out_1, out_2, out_3)):
            out[:, at] = part[k * tok_dev : (k + 1) * tok_dev]


def hidden_kernel(states, gate_rows, up_rows, out):
    step = 256
    for start in range(0, gate_rows.shape[0], step):
        at = slice(start, start + step)
        gate_act = lax.dot_general(
            states[...], gate_rows[at, :], NT, preferred_element_type=jnp.float32
        )
        up_act = lax.dot_general(
            states[...], up_rows[at, :], NT, preferred_element_type=jnp.float32
        )
        hidden = gate_act / (1.0 + jnp.exp(-gate_act)) * up_act
        out[:, at] = hidden.astype(jnp.bfloat16)


def down_kernel(near, far, near_rows, far_rows, out_0, out_1, out_2, out_3):
    tok_dev = out_0.shape[0]
    step = 512
    for start in range(0, near_rows.shape[1], step):
        at = slice(start, start + step)
        part = jnp.dot(near[...], near_rows[:, at], preferred_element_type=jnp.float32)
        part += jnp.dot(far[...], far_rows[:, at], preferred_element_type=jnp.float32)
        part = part.astype(jnp.bfloat16)
        for k, out in enumerate((out_0, out_1, out_2, out_3)):
            out[:, at] = part[k * tok_dev : (k + 1) * tok_dev]


def add_normed(base, added, gain):
    return (base.astype(jnp.float32) + rms_scale(added) * gain).astype(jnp.bfloat16)


def layer_direct(
    layer_input, angles, slot_mask, allowed, projections, adapters, head_gains, gains, ffn_rows
):
    tok_dev, width = layer_input.shape
    gate_rows, up_rows, down_rows = ffn_rows
    y = lax.axis_index("y")
    half = width // 2
    units = gate_rows.shape[0]
    near = lax.dynamic_slice_in_dim(down_rows, y * half, half, axis=1)
    far = exchange(lax.dynamic_slice_in_dim(down_rows, (1 - y) * half, half, axis=1), "y")
    gate_up, line_input = together(stacked(gate_rows, up_rows), layer_input)
    gate_up_x = exchange(gate_up, "x")
    cosine, sine = jnp.cos(angles), jnp.sin(angles)
    block = jax.ShapeDtypeStruct((tok_dev, width), jnp.bfloat16)
    *staged_rows, own_block = staged(
        *([in_hbm(array)] for array in (*projections, *adapters, *head_gains, layer_input))
    )
    *blocks, far = together(*line_gather(line_input)[1:], far)
    parts = vmem_call(
        attention_kernel,
        [block] * 4,
        [
            pltpu.VMEM((4 * tok_dev, width), jnp.bfloat16),
            pltpu.VMEM((4 * tok_dev, projections[0].shape[1]), jnp.bfloat16),
        ],
        [
            own_block,
            *blocks,
            *staged_rows,
            jnp.concatenate([cosine, cosine], axis=1),
            jnp.concatenate([-sine, sine], axis=1),
            slot_mask,
            allowed,
        ],
        8,
    )
    near_x = [exchange(rows, "x") for rows in jnp.split(near, 2)]
    attn_own = line_scatter(parts)
    residual_own = add_normed(layer_input, attn_own, gains[0])
    own, *line, other = together(*line_gather(residual_own), exchange(residual_own, "y"))
    line, gate_up_x, near_x[0] = together(jnp.concatenate(line), gate_up_x, near_x[0])
    far_x = exchange(far, "x")
    pieces = [exchange(gate_up, "core"), gate_up_x, exchange(gate_up_x, "core")]
    gate_all, up_all = staged(
        [in_hbm(gate_rows), *((piece, 0, units) for piece in pieces)],
        [in_hbm(up_rows), *((piece, units, units) for piece in pieces)],
    )

    def hidden_units_of(first, others):
        (hidden,) = vmem_call(
            hidden_kernel,
            [jax.ShapeDtypeStruct((4 * tok_dev, gate_all.shape[0]), jnp.bfloat16)],
            [],
            [jnp.concatenate([first, others]), gate_all, up_all],
            8,
        )
        return hidden

    line_other = exchange(line, "y")
    hidden_own = hidden_units_of(own, line)
    line_other, hidden_own, far_x, near_x[1] = together(line_other, hidden_own, far_x, near_x[1])
    from_own = exchange(hidden_own, "y")
    far_pieces = four_pieces(far, far_x)
    hidden_other = hidden_units_of(other, line_other)
    from_other = exchange(hidden_other, "y")
    near_pieces = four_pieces(near, jnp.concatenate(near_x))
    near_all, far_all = staged(near_pieces, far_pieces)

    def summed_down(hidden, from_y):
        parts = vmem_call(
            down_kernel,
            [jax.ShapeDtypeStruct((tok_dev, half), jnp.bfloat16)] * 4,
            [],
            [hidden, from_y, near_all, far_all],
            8,
        )
        return line_scatter(parts)

    other_half = exchange(summed_down(hidden_other, from_own).astype(jnp.bfloat16), "y")
    own_half = summed_down(hidden_own, from_other)
    other_half = other_half.astype(jnp.float32)
    mlp_own = jnp.concatenate(
        [jnp.where(y == 1, other_half, own_half), jnp.where(y == 1, own_half, other_half)], axis=1
    )
    return add_normed(residual_own, mlp_own, gains[1])


def shards(
    layer_input,
    request_lengths,
    request_adapter,
    slot_adapter_index,
    query_weight,
    key_weight,
    value_weight,
    output_weight,
    query_norm_gain,
    key_norm_gain,
    query_down_factors,
    value_down_factors,
    query_up_factors,
    value_up_factors,
    attention_norm_gain,
    feedforward_norm_gain,
    gate_weight,
    up_weight,
    down_weight_transposed,
):
    tok_dev = layer_input.shape[0]
    tok_group = tok_dev * lax.axis_size("mlp")
    window = tok_group * 3 // 8
    heads_local = query_weight.shape[1] // HEAD_SIZE
    direct = [lax.axis_size(axis) for axis in (*REQ, "mlp")] == [2, 2, 2, 4]
    places = jnp.arange(tok_group, dtype=jnp.int32)
    if direct:
        places = (places + lax.axis_index("mlp") * tok_dev) % tok_group
    request, position, token_slot = layout(
        request_lengths[0], request_adapter[0], slot_adapter_index, places
    )
    columns = jnp.arange(ADAPTER_SLOTS * ADAPTER_RANK, dtype=jnp.int32) // ADAPTER_RANK
    slot_match_mask = (columns[None, :] == token_slot[:, None]).astype(jnp.bfloat16)
    gate_rows, up_rows, down_rows = gate_weight.T, up_weight.T, down_weight_transposed.T
    if direct:
        return layer_direct(
            layer_input,
            rotary_angles(position),
            slot_match_mask,
            allowed_keys(request, position, window).astype(jnp.float32),
            (query_weight, key_weight, value_weight, output_weight),
            (query_down_factors, value_down_factors, query_up_factors, value_up_factors),
            (query_norm_gain[None, :], key_norm_gain[None, :]),
            (attention_norm_gain, feedforward_norm_gain),
            (gate_rows, up_rows, down_rows),
        )
    group_token_rows = lax.all_gather(layer_input, "mlp", axis=0, tiled=True)
    query_reduced = (
        jnp.dot(group_token_rows, query_down_factors, preferred_element_type=jnp.float32).astype(
            jnp.bfloat16
        )
        * slot_match_mask
    )
    value_reduced = (
        jnp.dot(group_token_rows, value_down_factors, preferred_element_type=jnp.float32).astype(
            jnp.bfloat16
        )
        * slot_match_mask
    )
    query_before_norm = jnp.dot(
        group_token_rows, query_weight, preferred_element_type=jnp.float32
    ) + adapter_scale * jnp.dot(query_reduced, query_up_factors, preferred_element_type=jnp.float32)
    key_pre = jnp.dot(group_token_rows, key_weight, preferred_element_type=jnp.float32)
    value_before_adapter = jnp.dot(
        group_token_rows, value_weight, preferred_element_type=jnp.float32
    ) + adapter_scale * jnp.dot(value_reduced, value_up_factors, preferred_element_type=jnp.float32)
    queries = rotary(
        rms_scale(query_before_norm.reshape(tok_group, heads_local, HEAD_SIZE))
        * query_norm_gain.reshape(heads_local, HEAD_SIZE),
        position,
    ).astype(jnp.bfloat16)
    key_heads = rotary(
        rms_scale(key_pre.reshape(tok_group, heads_local, HEAD_SIZE))
        * key_norm_gain.reshape(heads_local, HEAD_SIZE),
        position,
    ).astype(jnp.bfloat16)
    value_heads = value_before_adapter.astype(jnp.bfloat16).reshape(
        tok_group, heads_local, HEAD_SIZE
    )
    context = attention(queries, key_heads, value_heads, request, position, window).reshape(
        tok_group, heads_local * HEAD_SIZE
    )
    attn_own = lax.psum_scatter(
        jnp.dot(context, output_weight, preferred_element_type=jnp.float32).astype(jnp.bfloat16),
        "mlp",
        scatter_dimension=0,
        tiled=True,
    ).astype(jnp.float32)
    residual_own = add_normed(layer_input, attn_own, attention_norm_gain)
    gate_rows, up_rows, down_rows = (
        lax.all_gather(rows, REQ, axis=0, tiled=True) for rows in (gate_rows, up_rows, down_rows)
    )
    hidden = hidden_units(
        lax.all_gather(residual_own, "mlp", axis=0, tiled=True), gate_rows, up_rows
    )
    part = jnp.dot(hidden, down_rows, preferred_element_type=jnp.float32)
    mlp_own = lax.psum_scatter(
        part.astype(jnp.bfloat16), "mlp", scatter_dimension=0, tiled=True
    ).astype(jnp.float32)
    return add_normed(residual_own, mlp_own, feedforward_norm_gain)


def solution(mesh):
    req, mlp = mesh.devices.shape
    side = math.isqrt(req // 2)
    fine = Mesh(mesh.devices.reshape(req // 2 // side, side, 2, mlp), ("y", "x", "core", "mlp"))
    return jax.shard_map(
        shards,
        mesh=fine,
        in_specs=(
            P((*REQ, "mlp"), None),
            P(REQ, None),
            P(REQ, None),
            P(),
            P(None, "mlp"),
            P(None, "mlp"),
            P(None, "mlp"),
            P("mlp", None),
            P("mlp"),
            P("mlp"),
            P(),
            P(),
            P(None, "mlp"),
            P(None, "mlp"),
            P(),
            P(),
            P(None, (*REQ, "mlp")),
            P(None, (*REQ, "mlp")),
            P(None, (*REQ, "mlp")),
        ),
        out_specs=P((*REQ, "mlp"), None),
        check_vma=False,
    )
```

```python
import math

import jax
import jax.numpy as jnp
from jax import lax
from jax.experimental import pallas as pl
from jax.experimental.pallas import tpu as pltpu
from jax.sharding import Mesh, PartitionSpec as P

HEAD_SIZE = 128
ADAPTER_RANK = 16
ADAPTER_SLOTS = 8
SINKS = 4
REQ = ("y", "x", "core")


epsilon = 1e-06
adapter_scale = 0.5
rope_theta = 500000.0


def rms_scale(inputs):
    return inputs * lax.rsqrt(jnp.mean(inputs * inputs, axis=-1, keepdims=True) + epsilon)


def rotary_angles(position):
    exponent = jnp.arange(HEAD_SIZE // 2, dtype=jnp.float32) * (2.0 / HEAD_SIZE)
    frequency = rope_theta ** (-exponent)
    return position.astype(jnp.float32)[:, None] * frequency[None, :]


def rotary(inputs, position):
    half_dim = inputs.shape[-1] // 2
    angles = rotary_angles(position)
    cosine = jnp.cos(angles)[:, None, :]
    sine_part = jnp.sin(angles)[:, None, :]
    first_half = inputs[..., :half_dim]
    second = inputs[..., half_dim:]
    return jnp.concatenate(
        [first_half * cosine - second * sine_part, second * cosine + first_half * sine_part],
        axis=-1,
    )


def layout(lengths, adapters, slot_adapter_index, places):
    req_ends = jnp.cumsum(lengths)
    starts = req_ends - lengths
    member = ((places[:, None] >= starts[None, :]) & (places[:, None] < req_ends[None, :])).astype(
        jnp.int32
    )
    request = jnp.sum(member * jnp.arange(lengths.shape[0], dtype=jnp.int32)[None, :], axis=1)
    position = places - jnp.sum(member * starts[None, :], axis=1)
    chosen = jnp.sum(member * adapters[None, :], axis=1)
    slot_ids = jnp.arange(slot_adapter_index.shape[0], dtype=jnp.int32)
    token_slot = jnp.sum(
        (chosen[:, None] == slot_adapter_index[None, :]).astype(jnp.int32) * slot_ids[None, :],
        axis=1,
    )
    return (request, position, token_slot)


def allowed_keys(request, position, window):
    distance = position[:, None] - position[None, :]
    return (
        (request[:, None] == request[None, :])
        & (distance >= 0)
        & ((distance < window) | (position[None, :] < SINKS))
    )


def attention(queries, key_heads, value_heads, request, position, window):
    scores = jnp.einsum(
        "qhd,khd->hqk", queries, key_heads, preferred_element_type=jnp.float32
    ) * HEAD_SIZE ** (-0.5)
    allowed = allowed_keys(request, position, window)
    scores = jnp.where(allowed[None, :, :], scores, -1e30)
    row_peak = jnp.max(scores, axis=-1, keepdims=True)
    weights = jnp.exp(scores - row_peak)
    weights = (weights / jnp.sum(weights, axis=-1, keepdims=True)).astype(jnp.bfloat16)
    context = jnp.einsum("hqk,khd->qhd", weights, value_heads, preferred_element_type=jnp.float32)
    return context.astype(jnp.bfloat16)


def hidden_units(states, gate_rows, up_rows):
    contract = (((1,), (1,)), ((), ()))
    gate_act = lax.dot_general(states, gate_rows, contract, preferred_element_type=jnp.float32)
    up_act = lax.dot_general(states, up_rows, contract, preferred_element_type=jnp.float32)
    return (jax.nn.silu(gate_act) * up_act).astype(jnp.bfloat16)


def exchange(block, axis):
    return lax.ppermute(block, axis, [(0, 1), (1, 0)])


def shift(block, hops):
    return lax.ppermute(block, "mlp", [((k + hops) % 4, k) for k in range(4)])


def line_gather(block):
    across = shift(block, 2)
    return [block, shift(block, 1), across, shift(block, 3)]


def line_arrivals(parts):
    across = shift(parts[2], 2)
    return [shift(parts[3], 1), across, shift(parts[1], 3), parts[0]]


def line_sum(arrivals):
    return sum(part.astype(jnp.float32) for part in arrivals)


def together(*values):
    return lax.optimization_barrier(values)


def both_halves(*rows):
    (half,) = staged(rows)
    return half, pltpu.with_memory_space_constraint(exchange(half, "core"), pltpu.VMEM)


def vmem_call(kernel, outs, scratch, operands, vmem_mib):
    whole = pl.BlockSpec(memory_space=pltpu.VMEM)
    return pl.pallas_call(
        kernel,
        out_shape=outs,
        in_specs=[whole] * len(operands),
        out_specs=[whole] * len(outs),
        scratch_shapes=scratch,
        compiler_params=pltpu.CompilerParams(vmem_limit_bytes=vmem_mib << 20),
        cost_estimate=pl.CostEstimate(flops=1 << 20, bytes_accessed=1 << 20, transcendentals=0),
    )(*operands)


def in_hbm(array):
    return pltpu.with_memory_space_constraint(array, pltpu.HBM)


def staged(*groups):
    groups = [
        [piece if isinstance(piece, tuple) else (piece, 0, piece.shape[0]) for piece in group]
        for group in groups
    ]
    arrays = []
    for piece in (piece for group in groups for piece in group):
        if not any(piece[0] is array for array in arrays):
            arrays.append(piece[0])
    places = [
        [next(k for k, array in enumerate(arrays) if array is piece[0]) for piece in group]
        for group in groups
    ]
    count = sum(len(group) for group in groups)

    def kernel(*refs):
        sources, targets, sems = refs[: len(arrays)], refs[len(arrays) : -1], refs[-1]
        copies = []
        for group, place, target in zip(groups, places, targets):
            at = 0
            for (_, start, rows), k in zip(group, place):
                copies.append(
                    pltpu.make_async_copy(
                        sources[k].at[pl.ds(start, rows), :],
                        target.at[pl.ds(at, rows), :],
                        sems.at[len(copies)],
                    )
                )
                copies[-1].start()
                at += rows
        for copy in copies:
            copy.wait()

    outs = [(sum(piece[2] for piece in group), group[0][0].shape[1]) for group in groups]
    size = sum(rows * columns for rows, columns in outs)
    return pl.pallas_call(
        kernel,
        out_shape=[pltpu.VMEM(shape, group[0][0].dtype) for shape, group in zip(outs, groups)],
        in_specs=[pl.BlockSpec(memory_space=pl.ANY)] * len(arrays),
        out_specs=[pl.BlockSpec(memory_space=pltpu.VMEM)] * len(groups),
        scratch_shapes=[pltpu.SemaphoreType.DMA((count,))],
        compiler_params=pltpu.CompilerParams(vmem_limit_bytes=1 << 20),
        cost_estimate=pl.CostEstimate(flops=0, bytes_accessed=4 * size, transcendentals=0),
    )(*arrays)


NT = (((1,), (1,)), ((), ()))


def attention_kernel(
    block_0,
    block_1,
    block_2,
    block_3,
    query_weight,
    key_weight,
    value_weight,
    output_weight,
    query_down,
    value_down,
    query_up,
    value_up,
    query_gain,
    key_gain,
    cosine,
    sine,
    slot_mask,
    allowed,
    out_0,
    out_1,
    out_2,
    out_3,
    rows,
    context,
):
    tok_dev = block_0.shape[0]
    for k, block in enumerate((block_0, block_1, block_2, block_3)):
        rows[k * tok_dev : (k + 1) * tok_dev, :] = block[...]

    def project(weight):
        return jnp.dot(rows[...], weight[...], preferred_element_type=jnp.float32)

    def adapted(weight, down, up):
        low = project(down).astype(jnp.bfloat16) * slot_mask[...]
        return project(weight) + adapter_scale * jnp.dot(
            low, up[...], preferred_element_type=jnp.float32
        )

    def heads(inputs, gain):
        inputs = rms_scale(inputs) * gain
        turned = pltpu.roll(inputs, HEAD_SIZE // 2, 1)
        return (inputs * cosine[...] + turned * sine[...]).astype(jnp.bfloat16)

    queries = adapted(query_weight, query_down, query_up)
    keys = project(key_weight)
    values = adapted(value_weight, value_down, value_up).astype(jnp.bfloat16)
    for start in range(0, queries.shape[1], HEAD_SIZE):
        at = slice(start, start + HEAD_SIZE)
        scores = lax.dot_general(
            heads(queries[:, at], query_gain[:, at]),
            heads(keys[:, at], key_gain[:, at]),
            NT,
            preferred_element_type=jnp.float32,
        ) * HEAD_SIZE ** (-0.5)
        scores = jnp.where(allowed[...] > 0, scores, -1e30)
        weights = jnp.exp(scores - jnp.max(scores, axis=-1, keepdims=True))
        weights = (weights / jnp.sum(weights, axis=-1, keepdims=True)).astype(jnp.bfloat16)
        context[:, at] = jnp.dot(
            weights, values[:, at], preferred_element_type=jnp.float32
        ).astype(jnp.bfloat16)
    step = 1024
    for start in range(0, output_weight.shape[1], step):
        at = slice(start, start + step)
        part = jnp.dot(context[...], output_weight[:, at], preferred_element_type=jnp.float32)
        part = part.astype(jnp.bfloat16)
        for k, out in enumerate((out_0, out_1, out_2, out_3)):
            out[:, at] = part[k * tok_dev : (k + 1) * tok_dev]


def hidden_kernel(states, gate_0, gate_1, up_0, up_1, out):
    count = gate_0.shape[0]
    for k, (gate_rows, up_rows) in enumerate(((gate_0, up_0), (gate_1, up_1))):
        gate_act = lax.dot_general(
            states[...], gate_rows[...], NT, preferred_element_type=jnp.float32
        )
        up_act = lax.dot_general(states[...], up_rows[...], NT, preferred_element_type=jnp.float32)
        hidden = gate_act / (1.0 + jnp.exp(-gate_act)) * up_act
        out[:, k * count : (k + 1) * count] = hidden.astype(jnp.bfloat16)


def down_kernel(near, far, near_0, near_1, far_0, far_1, out_0, out_1, out_2, out_3):
    tok_dev, count = out_0.shape[0], near_0.shape[0]
    step = 512
    for start in range(0, near_0.shape[1], step):
        at = slice(start, start + step)
        part = 0.0
        for hidden, halves in ((near, (near_0, near_1)), (far, (far_0, far_1))):
            for k, rows in enumerate(halves):
                part += jnp.dot(
                    hidden[:, k * count : (k + 1) * count],
                    rows[:, at],
                    preferred_element_type=jnp.float32,
                )
        part = part.astype(jnp.bfloat16)
        for k, out in enumerate((out_0, out_1, out_2, out_3)):
            out[:, at] = part[k * tok_dev : (k + 1) * tok_dev]


def add_normed(base, added, gain):
    return (base.astype(jnp.float32) + rms_scale(added) * gain).astype(jnp.bfloat16)


def layer_direct(
    layer_input, angles, slot_mask, allowed, projections, adapters, head_gains, gains, ffn_rows
):
    tok_dev, width = layer_input.shape
    gate_rows, up_rows, down_rows = ffn_rows
    y = lax.axis_index("y")
    half = width // 2
    near = lax.dynamic_slice_in_dim(down_rows, y * half, half, axis=1)
    far = exchange(lax.dynamic_slice_in_dim(down_rows, (1 - y) * half, half, axis=1), "y")
    gate_x = exchange(gate_rows, "x")
    cosine, sine = jnp.cos(angles), jnp.sin(angles)
    block = jax.ShapeDtypeStruct((tok_dev, width), jnp.bfloat16)
    *staged_rows, own_block = staged(
        *([in_hbm(array)] for array in (*projections, *adapters, *head_gains, layer_input))
    )
    *blocks, far = together(*line_gather(layer_input)[1:], far)
    parts = vmem_call(
        attention_kernel,
        [block] * 4,
        [
            pltpu.VMEM((4 * tok_dev, width), jnp.bfloat16),
            pltpu.VMEM((4 * tok_dev, projections[0].shape[1]), jnp.bfloat16),
        ],
        [
            own_block,
            *blocks,
            *staged_rows,
            jnp.concatenate([cosine, cosine], axis=1),
            jnp.concatenate([-sine, sine], axis=1),
            slot_mask,
            allowed,
        ],
        8,
    )
    near_x = [exchange(rows, "x") for rows in jnp.split(near, [near.shape[0] // 6])]
    arrivals = line_arrivals(parts)
    arrivals[0], gate_x, up_late = together(arrivals[0], gate_x, up_rows)
    units = up_late.shape[0]
    up_parts = jnp.split(up_late, [units * 5 // 12])
    up_x = [exchange(up_parts[0], "x")]
    attn_own, up_x[0], up_part = together(line_sum(arrivals), up_x[0], up_parts[1])
    up_x.append(exchange(up_part, "x"))
    residual_own = add_normed(layer_input, attn_own, gains[0])
    own, *line, other = together(*line_gather(residual_own), exchange(residual_own, "y"))
    line, gate_x, *up_x, near_x[0] = together(jnp.concatenate(line), gate_x, *up_x, near_x[0])
    far_x = exchange(far, "x")
    halves = [*both_halves(in_hbm(gate_rows), gate_x), *both_halves(in_hbm(up_rows), *up_x)]

    def hidden_units_of(first, others):
        (hidden,) = vmem_call(
            hidden_kernel,
            [jax.ShapeDtypeStruct((4 * tok_dev, 4 * gate_rows.shape[0]), jnp.bfloat16)],
            [],
            [jnp.concatenate([first, others]), *halves],
            8,
        )
        return hidden

    line_other = exchange(line, "y")
    hidden_own = hidden_units_of(own, line)
    line_other, hidden_own, far_x, near_x[1] = together(line_other, hidden_own, far_x, near_x[1])
    from_own = exchange(hidden_own, "y")
    hidden_other = hidden_units_of(other, line_other)
    from_other = exchange(hidden_other, "y")
    down_halves = [*both_halves(near, *near_x), *both_halves(far, far_x)]

    def summed_down(hidden, from_y):
        parts = vmem_call(
            down_kernel,
            [jax.ShapeDtypeStruct((tok_dev, half), jnp.bfloat16)] * 4,
            [],
            [hidden, from_y, *down_halves],
            8,
        )
        return line_sum(line_arrivals(parts))

    other_half = exchange(summed_down(hidden_other, from_own).astype(jnp.bfloat16), "y")
    own_half = summed_down(hidden_own, from_other)
    other_half = other_half.astype(jnp.float32)
    mlp_own = jnp.concatenate(
        [jnp.where(y == 1, other_half, own_half), jnp.where(y == 1, own_half, other_half)], axis=1
    )
    return add_normed(residual_own, mlp_own, gains[1])


def shards(
    layer_input,
    request_lengths,
    request_adapter,
    slot_adapter_index,
    query_weight,
    key_weight,
    value_weight,
    output_weight,
    query_norm_gain,
    key_norm_gain,
    query_down_factors,
    value_down_factors,
    query_up_factors,
    value_up_factors,
    attention_norm_gain,
    feedforward_norm_gain,
    gate_weight,
    up_weight,
    down_weight_transposed,
):
    tok_dev = layer_input.shape[0]
    tok_group = tok_dev * lax.axis_size("mlp")
    window = tok_group * 3 // 8
    heads_local = query_weight.shape[1] // HEAD_SIZE
    direct = [lax.axis_size(axis) for axis in (*REQ, "mlp")] == [2, 2, 2, 4]
    places = jnp.arange(tok_group, dtype=jnp.int32)
    if direct:
        places = (places + lax.axis_index("mlp") * tok_dev) % tok_group
    request, position, token_slot = layout(
        request_lengths[0], request_adapter[0], slot_adapter_index, places
    )
    columns = jnp.arange(ADAPTER_SLOTS * ADAPTER_RANK, dtype=jnp.int32) // ADAPTER_RANK
    slot_match_mask = (columns[None, :] == token_slot[:, None]).astype(jnp.bfloat16)
    gate_rows, up_rows, down_rows = gate_weight.T, up_weight.T, down_weight_transposed.T
    if direct:
        return layer_direct(
            layer_input,
            rotary_angles(position),
            slot_match_mask,
            allowed_keys(request, position, window).astype(jnp.float32),
            (query_weight, key_weight, value_weight, output_weight),
            (query_down_factors, value_down_factors, query_up_factors, value_up_factors),
            (query_norm_gain[None, :], key_norm_gain[None, :]),
            (attention_norm_gain, feedforward_norm_gain),
            (gate_rows, up_rows, down_rows),
        )
    group_token_rows = lax.all_gather(layer_input, "mlp", axis=0, tiled=True)
    query_reduced = (
        jnp.dot(group_token_rows, query_down_factors, preferred_element_type=jnp.float32).astype(
            jnp.bfloat16
        )
        * slot_match_mask
    )
    value_reduced = (
        jnp.dot(group_token_rows, value_down_factors, preferred_element_type=jnp.float32).astype(
            jnp.bfloat16
        )
        * slot_match_mask
    )
    query_before_norm = jnp.dot(
        group_token_rows, query_weight, preferred_element_type=jnp.float32
    ) + adapter_scale * jnp.dot(query_reduced, query_up_factors, preferred_element_type=jnp.float32)
    key_pre = jnp.dot(group_token_rows, key_weight, preferred_element_type=jnp.float32)
    value_before_adapter = jnp.dot(
        group_token_rows, value_weight, preferred_element_type=jnp.float32
    ) + adapter_scale * jnp.dot(value_reduced, value_up_factors, preferred_element_type=jnp.float32)
    queries = rotary(
        rms_scale(query_before_norm.reshape(tok_group, heads_local, HEAD_SIZE))
        * query_norm_gain.reshape(heads_local, HEAD_SIZE),
        position,
    ).astype(jnp.bfloat16)
    key_heads = rotary(
        rms_scale(key_pre.reshape(tok_group, heads_local, HEAD_SIZE))
        * key_norm_gain.reshape(heads_local, HEAD_SIZE),
        position,
    ).astype(jnp.bfloat16)
    value_heads = value_before_adapter.astype(jnp.bfloat16).reshape(
        tok_group, heads_local, HEAD_SIZE
    )
    context = attention(queries, key_heads, value_heads, request, position, window).reshape(
        tok_group, heads_local * HEAD_SIZE
    )
    attn_own = lax.psum_scatter(
        jnp.dot(context, output_weight, preferred_element_type=jnp.float32).astype(jnp.bfloat16),
        "mlp",
        scatter_dimension=0,
        tiled=True,
    ).astype(jnp.float32)
    residual_own = add_normed(layer_input, attn_own, attention_norm_gain)
    gate_rows, up_rows, down_rows = (
        lax.all_gather(rows, REQ, axis=0, tiled=True) for rows in (gate_rows, up_rows, down_rows)
    )
    hidden = hidden_units(
        lax.all_gather(residual_own, "mlp", axis=0, tiled=True), gate_rows, up_rows
    )
    part = jnp.dot(hidden, down_rows, preferred_element_type=jnp.float32)
    mlp_own = lax.psum_scatter(
        part.astype(jnp.bfloat16), "mlp", scatter_dimension=0, tiled=True
    ).astype(jnp.float32)
    return add_normed(residual_own, mlp_own, feedforward_norm_gain)


def solution(mesh):
    req, mlp = mesh.devices.shape
    side = math.isqrt(req // 2)
    fine = Mesh(mesh.devices.reshape(req // 2 // side, side, 2, mlp), ("y", "x", "core", "mlp"))
    return jax.shard_map(
        shards,
        mesh=fine,
        in_specs=(
            P((*REQ, "mlp"), None),
            P(REQ, None),
            P(REQ, None),
            P(),
            P(None, "mlp"),
            P(None, "mlp"),
            P(None, "mlp"),
            P("mlp", None),
            P("mlp"),
            P("mlp"),
            P(),
            P(),
            P(None, "mlp"),
            P(None, "mlp"),
            P(),
            P(),
            P(None, (*REQ, "mlp")),
            P(None, (*REQ, "mlp")),
            P(None, (*REQ, "mlp")),
        ),
        out_specs=P((*REQ, "mlp"), None),
        check_vma=False,
    )
```

```python
import math

import jax
import jax.numpy as jnp
from jax import lax
from jax.experimental import pallas as pl
from jax.experimental.pallas import tpu as pltpu
from jax.sharding import Mesh, PartitionSpec as P

HEAD_SIZE = 128
ADAPTER_RANK = 16
ADAPTER_SLOTS = 8
SINKS = 4
REQ = ("y", "x", "core")


epsilon = 1e-06
adapter_scale = 0.5
rope_theta = 500000.0


def rms_scale(inputs):
    return inputs * lax.rsqrt(jnp.mean(inputs * inputs, axis=-1, keepdims=True) + epsilon)


def rotary_angles(position):
    exponent = jnp.arange(HEAD_SIZE // 2, dtype=jnp.float32) * (2.0 / HEAD_SIZE)
    frequency = rope_theta ** (-exponent)
    return position.astype(jnp.float32)[:, None] * frequency[None, :]


def rotary(inputs, position):
    half_dim = inputs.shape[-1] // 2
    angles = rotary_angles(position)
    cosine = jnp.cos(angles)[:, None, :]
    sine_part = jnp.sin(angles)[:, None, :]
    first_half = inputs[..., :half_dim]
    second = inputs[..., half_dim:]
    return jnp.concatenate(
        [first_half * cosine - second * sine_part, second * cosine + first_half * sine_part],
        axis=-1,
    )


def layout(lengths, adapters, slot_adapter_index, places):
    req_ends = jnp.cumsum(lengths)
    starts = req_ends - lengths
    member = ((places[:, None] >= starts[None, :]) & (places[:, None] < req_ends[None, :])).astype(
        jnp.int32
    )
    request = jnp.sum(member * jnp.arange(lengths.shape[0], dtype=jnp.int32)[None, :], axis=1)
    position = places - jnp.sum(member * starts[None, :], axis=1)
    chosen = jnp.sum(member * adapters[None, :], axis=1)
    slot_ids = jnp.arange(slot_adapter_index.shape[0], dtype=jnp.int32)
    token_slot = jnp.sum(
        (chosen[:, None] == slot_adapter_index[None, :]).astype(jnp.int32) * slot_ids[None, :],
        axis=1,
    )
    return (request, position, token_slot)


def allowed_keys(request, position, window):
    distance = position[:, None] - position[None, :]
    return (
        (request[:, None] == request[None, :])
        & (distance >= 0)
        & ((distance < window) | (position[None, :] < SINKS))
    )


def attention(queries, key_heads, value_heads, request, position, window):
    scores = jnp.einsum(
        "qhd,khd->hqk", queries, key_heads, preferred_element_type=jnp.float32
    ) * HEAD_SIZE ** (-0.5)
    allowed = allowed_keys(request, position, window)
    scores = jnp.where(allowed[None, :, :], scores, -1e30)
    row_peak = jnp.max(scores, axis=-1, keepdims=True)
    weights = jnp.exp(scores - row_peak)
    weights = (weights / jnp.sum(weights, axis=-1, keepdims=True)).astype(jnp.bfloat16)
    context = jnp.einsum("hqk,khd->qhd", weights, value_heads, preferred_element_type=jnp.float32)
    return context.astype(jnp.bfloat16)


def hidden_units(states, gate_rows, up_rows):
    contract = (((1,), (1,)), ((), ()))
    gate_act = lax.dot_general(states, gate_rows, contract, preferred_element_type=jnp.float32)
    up_act = lax.dot_general(states, up_rows, contract, preferred_element_type=jnp.float32)
    return (jax.nn.silu(gate_act) * up_act).astype(jnp.bfloat16)


def exchange(block, axis):
    return lax.ppermute(block, axis, [(0, 1), (1, 0)])


def shift(block, hops):
    return lax.ppermute(block, "mlp", [((k + hops) % 4, k) for k in range(4)])


def line_gather(block):
    across = shift(block, 2)
    return [block, shift(block, 1), across, shift(block, 3)]


def line_arrivals(parts):
    across = shift(parts[2], 2)
    return [shift(parts[3], 1), across, shift(parts[1], 3), parts[0]]


def line_sum(arrivals):
    return sum(part.astype(jnp.float32) for part in arrivals)


def together(*values):
    return lax.optimization_barrier(values)


def both_halves(*rows):
    (half,) = staged(rows)
    return half, pltpu.with_memory_space_constraint(exchange(half, "core"), pltpu.VMEM)


def vmem_call(kernel, outs, scratch, operands, vmem_mib):
    whole = pl.BlockSpec(memory_space=pltpu.VMEM)
    return pl.pallas_call(
        kernel,
        out_shape=outs,
        in_specs=[whole] * len(operands),
        out_specs=[whole] * len(outs),
        scratch_shapes=scratch,
        compiler_params=pltpu.CompilerParams(vmem_limit_bytes=vmem_mib << 20),
        cost_estimate=pl.CostEstimate(flops=1 << 20, bytes_accessed=1 << 20, transcendentals=0),
    )(*operands)


def in_hbm(array):
    return pltpu.with_memory_space_constraint(array, pltpu.HBM)


def staged(*groups, weight=4):
    groups = [
        [piece if isinstance(piece, tuple) else (piece, 0, piece.shape[0]) for piece in group]
        for group in groups
    ]
    arrays = []
    for piece in (piece for group in groups for piece in group):
        if not any(piece[0] is array for array in arrays):
            arrays.append(piece[0])
    places = [
        [next(k for k, array in enumerate(arrays) if array is piece[0]) for piece in group]
        for group in groups
    ]
    count = sum(len(group) for group in groups)

    def kernel(*refs):
        sources, targets, sems = refs[: len(arrays)], refs[len(arrays) : -1], refs[-1]
        copies = []
        for group, place, target in zip(groups, places, targets):
            at = 0
            for (_, start, rows), k in zip(group, place):
                copies.append(
                    pltpu.make_async_copy(
                        sources[k].at[pl.ds(start, rows), :],
                        target.at[pl.ds(at, rows), :],
                        sems.at[len(copies)],
                    )
                )
                copies[-1].start()
                at += rows
        for copy in copies:
            copy.wait()

    outs = [(sum(piece[2] for piece in group), group[0][0].shape[1]) for group in groups]
    size = sum(rows * columns for rows, columns in outs)
    return pl.pallas_call(
        kernel,
        out_shape=[pltpu.VMEM(shape, group[0][0].dtype) for shape, group in zip(outs, groups)],
        in_specs=[pl.BlockSpec(memory_space=pl.ANY)] * len(arrays),
        out_specs=[pl.BlockSpec(memory_space=pltpu.VMEM)] * len(groups),
        scratch_shapes=[pltpu.SemaphoreType.DMA((count,))],
        compiler_params=pltpu.CompilerParams(vmem_limit_bytes=1 << 20),
        cost_estimate=pl.CostEstimate(flops=0, bytes_accessed=weight * size, transcendentals=0),
    )(*arrays)


NT = (((1,), (1,)), ((), ()))


def attention_kernel(
    block_0,
    block_1,
    block_2,
    block_3,
    query_weight,
    key_weight,
    value_weight,
    output_weight,
    query_down,
    value_down,
    query_up,
    value_up,
    query_gain,
    key_gain,
    cosine,
    sine,
    slot_mask,
    allowed,
    out_0,
    out_1,
    out_2,
    out_3,
    rows,
    context,
):
    tok_dev = block_0.shape[0]
    for k, block in enumerate((block_0, block_1, block_2, block_3)):
        rows[k * tok_dev : (k + 1) * tok_dev, :] = block[...]

    def project(weight):
        return jnp.dot(rows[...], weight[...], preferred_element_type=jnp.float32)

    def adapted(weight, down, up):
        low = project(down).astype(jnp.bfloat16) * slot_mask[...]
        return project(weight) + adapter_scale * jnp.dot(
            low, up[...], preferred_element_type=jnp.float32
        )

    def heads(inputs, gain):
        inputs = rms_scale(inputs) * gain
        turned = pltpu.roll(inputs, HEAD_SIZE // 2, 1)
        return (inputs * cosine[...] + turned * sine[...]).astype(jnp.bfloat16)

    queries = adapted(query_weight, query_down, query_up)
    keys = project(key_weight)
    values = adapted(value_weight, value_down, value_up).astype(jnp.bfloat16)
    for start in range(0, queries.shape[1], HEAD_SIZE):
        at = slice(start, start + HEAD_SIZE)
        scores = lax.dot_general(
            heads(queries[:, at], query_gain[:, at]),
            heads(keys[:, at], key_gain[:, at]),
            NT,
            preferred_element_type=jnp.float32,
        ) * HEAD_SIZE ** (-0.5)
        scores = jnp.where(allowed[...] > 0, scores, -1e30)
        weights = jnp.exp(scores - jnp.max(scores, axis=-1, keepdims=True))
        weights = (weights / jnp.sum(weights, axis=-1, keepdims=True)).astype(jnp.bfloat16)
        context[:, at] = jnp.dot(
            weights, values[:, at], preferred_element_type=jnp.float32
        ).astype(jnp.bfloat16)
    step = 1024
    for start in range(0, output_weight.shape[1], step):
        at = slice(start, start + step)
        part = jnp.dot(context[...], output_weight[:, at], preferred_element_type=jnp.float32)
        part = part.astype(jnp.bfloat16)
        for k, out in enumerate((out_0, out_1, out_2, out_3)):
            out[:, at] = part[k * tok_dev : (k + 1) * tok_dev]


def hidden_kernel(states, gate_0, gate_1, up_0, up_1, out):
    count = gate_0.shape[0]
    for k, (gate_rows, up_rows) in enumerate(((gate_0, up_0), (gate_1, up_1))):
        gate_act = lax.dot_general(
            states[...], gate_rows[...], NT, preferred_element_type=jnp.float32
        )
        up_act = lax.dot_general(states[...], up_rows[...], NT, preferred_element_type=jnp.float32)
        hidden = gate_act / (1.0 + jnp.exp(-gate_act)) * up_act
        out[:, k * count : (k + 1) * count] = hidden.astype(jnp.bfloat16)


def down_kernel(near, far, near_0, near_1, far_0, far_1, out_0, out_1, out_2, out_3):
    tok_dev, count = out_0.shape[0], near_0.shape[0]
    step = 512
    for start in range(0, near_0.shape[1], step):
        at = slice(start, start + step)
        part = 0.0
        for hidden, halves in ((near, (near_0, near_1)), (far, (far_0, far_1))):
            for k, rows in enumerate(halves):
                part += jnp.dot(
                    hidden[:, k * count : (k + 1) * count],
                    rows[:, at],
                    preferred_element_type=jnp.float32,
                )
        part = part.astype(jnp.bfloat16)
        for k, out in enumerate((out_0, out_1, out_2, out_3)):
            out[:, at] = part[k * tok_dev : (k + 1) * tok_dev]


def add_normed(base, added, gain):
    return (base.astype(jnp.float32) + rms_scale(added) * gain).astype(jnp.bfloat16)


def layer_direct(
    layer_input, angles, slot_mask, allowed, projections, adapters, head_gains, gains, ffn_rows
):
    tok_dev, width = layer_input.shape
    gate_rows, up_rows, down_rows = ffn_rows
    y = lax.axis_index("y")
    half = width // 2
    gate_x = exchange(gate_rows, "x")
    cosine, sine = jnp.cos(angles), jnp.sin(angles)
    block = jax.ShapeDtypeStruct((tok_dev, width), jnp.bfloat16)
    *staged_rows, own_block = staged(
        *([in_hbm(array)] for array in (*projections, *adapters, *head_gains, layer_input)),
        weight=0,
    )
    *blocks, own_block, down_rows = together(*line_gather(layer_input)[1:], own_block, down_rows)
    parts = vmem_call(
        attention_kernel,
        [block] * 4,
        [
            pltpu.VMEM((4 * tok_dev, width), jnp.bfloat16),
            pltpu.VMEM((4 * tok_dev, projections[0].shape[1]), jnp.bfloat16),
        ],
        [
            own_block,
            *blocks,
            *staged_rows,
            jnp.concatenate([cosine, cosine], axis=1),
            jnp.concatenate([-sine, sine], axis=1),
            slot_mask,
            allowed,
        ],
        8,
    )
    near = lax.dynamic_slice_in_dim(down_rows, y * half, half, axis=1)
    far = exchange(lax.dynamic_slice_in_dim(down_rows, (1 - y) * half, half, axis=1), "y")
    arrivals = line_arrivals(parts)
    arrivals[0], gate_x, up_late = together(arrivals[0], gate_x, up_rows)
    units = up_late.shape[0]
    up_parts = jnp.split(up_late, [units * 5 // 12])
    up_x = [exchange(up_parts[0], "x")]
    attn_own, up_x[0], up_part, near, far = together(
        line_sum(arrivals), up_x[0], up_parts[1], near, far
    )
    up_x.append(exchange(up_part, "x"))
    near_x = [exchange(rows, "x") for rows in jnp.split(near, [near.shape[0] // 6])]
    residual_own = add_normed(layer_input, attn_own, gains[0])
    own, *line, other = together(*line_gather(residual_own), exchange(residual_own, "y"))
    line, gate_x, *up_x, near_x[0] = together(jnp.concatenate(line), gate_x, *up_x, near_x[0])
    far_x = exchange(far, "x")
    halves = [*both_halves(in_hbm(gate_rows), gate_x), *both_halves(in_hbm(up_rows), *up_x)]

    def hidden_units_of(first, others):
        (hidden,) = vmem_call(
            hidden_kernel,
            [jax.ShapeDtypeStruct((4 * tok_dev, 4 * gate_rows.shape[0]), jnp.bfloat16)],
            [],
            [jnp.concatenate([first, others]), *halves],
            8,
        )
        return hidden

    line_other = exchange(line, "y")
    hidden_own = hidden_units_of(own, line)
    line_other, hidden_own, far_x, near_x[1] = together(line_other, hidden_own, far_x, near_x[1])
    from_own = exchange(hidden_own, "y")
    hidden_other = hidden_units_of(other, line_other)
    from_other = exchange(hidden_other, "y")
    down_halves = [*both_halves(near, *near_x), *both_halves(far, far_x)]

    def summed_down(hidden, from_y):
        parts = vmem_call(
            down_kernel,
            [jax.ShapeDtypeStruct((tok_dev, half), jnp.bfloat16)] * 4,
            [],
            [hidden, from_y, *down_halves],
            8,
        )
        return line_sum(line_arrivals(parts))

    other_half = exchange(summed_down(hidden_other, from_own).astype(jnp.bfloat16), "y")
    own_half = summed_down(hidden_own, from_other)
    other_half = other_half.astype(jnp.float32)
    mlp_own = jnp.concatenate(
        [jnp.where(y == 1, other_half, own_half), jnp.where(y == 1, own_half, other_half)], axis=1
    )
    return add_normed(residual_own, mlp_own, gains[1])


def shards(
    layer_input,
    request_lengths,
    request_adapter,
    slot_adapter_index,
    query_weight,
    key_weight,
    value_weight,
    output_weight,
    query_norm_gain,
    key_norm_gain,
    query_down_factors,
    value_down_factors,
    query_up_factors,
    value_up_factors,
    attention_norm_gain,
    feedforward_norm_gain,
    gate_weight,
    up_weight,
    down_weight_transposed,
):
    tok_dev = layer_input.shape[0]
    tok_group = tok_dev * lax.axis_size("mlp")
    window = tok_group * 3 // 8
    heads_local = query_weight.shape[1] // HEAD_SIZE
    direct = [lax.axis_size(axis) for axis in (*REQ, "mlp")] == [2, 2, 2, 4]
    places = jnp.arange(tok_group, dtype=jnp.int32)
    if direct:
        places = (places + lax.axis_index("mlp") * tok_dev) % tok_group
    request, position, token_slot = layout(
        request_lengths[0], request_adapter[0], slot_adapter_index, places
    )
    columns = jnp.arange(ADAPTER_SLOTS * ADAPTER_RANK, dtype=jnp.int32) // ADAPTER_RANK
    slot_match_mask = (columns[None, :] == token_slot[:, None]).astype(jnp.bfloat16)
    gate_rows, up_rows, down_rows = gate_weight.T, up_weight.T, down_weight_transposed.T
    if direct:
        return layer_direct(
            layer_input,
            rotary_angles(position),
            slot_match_mask,
            allowed_keys(request, position, window).astype(jnp.float32),
            (query_weight, key_weight, value_weight, output_weight),
            (query_down_factors, value_down_factors, query_up_factors, value_up_factors),
            (query_norm_gain[None, :], key_norm_gain[None, :]),
            (attention_norm_gain, feedforward_norm_gain),
            (gate_rows, up_rows, down_rows),
        )
    group_token_rows = lax.all_gather(layer_input, "mlp", axis=0, tiled=True)
    query_reduced = (
        jnp.dot(group_token_rows, query_down_factors, preferred_element_type=jnp.float32).astype(
            jnp.bfloat16
        )
        * slot_match_mask
    )
    value_reduced = (
        jnp.dot(group_token_rows, value_down_factors, preferred_element_type=jnp.float32).astype(
            jnp.bfloat16
        )
        * slot_match_mask
    )
    query_before_norm = jnp.dot(
        group_token_rows, query_weight, preferred_element_type=jnp.float32
    ) + adapter_scale * jnp.dot(query_reduced, query_up_factors, preferred_element_type=jnp.float32)
    key_pre = jnp.dot(group_token_rows, key_weight, preferred_element_type=jnp.float32)
    value_before_adapter = jnp.dot(
        group_token_rows, value_weight, preferred_element_type=jnp.float32
    ) + adapter_scale * jnp.dot(value_reduced, value_up_factors, preferred_element_type=jnp.float32)
    queries = rotary(
        rms_scale(query_before_norm.reshape(tok_group, heads_local, HEAD_SIZE))
        * query_norm_gain.reshape(heads_local, HEAD_SIZE),
        position,
    ).astype(jnp.bfloat16)
    key_heads = rotary(
        rms_scale(key_pre.reshape(tok_group, heads_local, HEAD_SIZE))
        * key_norm_gain.reshape(heads_local, HEAD_SIZE),
        position,
    ).astype(jnp.bfloat16)
    value_heads = value_before_adapter.astype(jnp.bfloat16).reshape(
        tok_group, heads_local, HEAD_SIZE
    )
    context = attention(queries, key_heads, value_heads, request, position, window).reshape(
        tok_group, heads_local * HEAD_SIZE
    )
    attn_own = lax.psum_scatter(
        jnp.dot(context, output_weight, preferred_element_type=jnp.float32).astype(jnp.bfloat16),
        "mlp",
        scatter_dimension=0,
        tiled=True,
    ).astype(jnp.float32)
    residual_own = add_normed(layer_input, attn_own, attention_norm_gain)
    gate_rows, up_rows, down_rows = (
        lax.all_gather(rows, REQ, axis=0, tiled=True) for rows in (gate_rows, up_rows, down_rows)
    )
    hidden = hidden_units(
        lax.all_gather(residual_own, "mlp", axis=0, tiled=True), gate_rows, up_rows
    )
    part = jnp.dot(hidden, down_rows, preferred_element_type=jnp.float32)
    mlp_own = lax.psum_scatter(
        part.astype(jnp.bfloat16), "mlp", scatter_dimension=0, tiled=True
    ).astype(jnp.float32)
    return add_normed(residual_own, mlp_own, feedforward_norm_gain)


def solution(mesh):
    req, mlp = mesh.devices.shape
    side = math.isqrt(req // 2)
    fine = Mesh(mesh.devices.reshape(req // 2 // side, side, 2, mlp), ("y", "x", "core", "mlp"))
    return jax.shard_map(
        shards,
        mesh=fine,
        in_specs=(
            P((*REQ, "mlp"), None),
            P(REQ, None),
            P(REQ, None),
            P(),
            P(None, "mlp"),
            P(None, "mlp"),
            P(None, "mlp"),
            P("mlp", None),
            P("mlp"),
            P("mlp"),
            P(),
            P(),
            P(None, "mlp"),
            P(None, "mlp"),
            P(),
            P(),
            P(None, (*REQ, "mlp")),
            P(None, (*REQ, "mlp")),
            P(None, (*REQ, "mlp")),
        ),
        out_specs=P((*REQ, "mlp"), None),
        check_vma=False,
    )
```

```python
import math

import jax
import jax.numpy as jnp
from jax import lax
from jax.experimental import pallas as pl
from jax.experimental.pallas import tpu as pltpu
from jax.sharding import Mesh, PartitionSpec as P

HEAD_SIZE = 128
ADAPTER_RANK = 16
ADAPTER_SLOTS = 8
SINKS = 4
REQ = ("y", "x", "core")


epsilon = 1e-06
adapter_scale = 0.5
rope_theta = 500000.0


def rms_scale(inputs):
    return inputs * lax.rsqrt(jnp.mean(inputs * inputs, axis=-1, keepdims=True) + epsilon)


def rotary_angles(position):
    exponent = jnp.arange(HEAD_SIZE // 2, dtype=jnp.float32) * (2.0 / HEAD_SIZE)
    frequency = rope_theta ** (-exponent)
    return position.astype(jnp.float32)[:, None] * frequency[None, :]


def rotary(inputs, position):
    half_dim = inputs.shape[-1] // 2
    angles = rotary_angles(position)
    cosine = jnp.cos(angles)[:, None, :]
    sine_part = jnp.sin(angles)[:, None, :]
    first_half = inputs[..., :half_dim]
    second = inputs[..., half_dim:]
    return jnp.concatenate(
        [first_half * cosine - second * sine_part, second * cosine + first_half * sine_part],
        axis=-1,
    )


def layout(lengths, adapters, slot_adapter_index, places):
    req_ends = jnp.cumsum(lengths)
    starts = req_ends - lengths
    member = ((places[:, None] >= starts[None, :]) & (places[:, None] < req_ends[None, :])).astype(
        jnp.int32
    )
    request = jnp.sum(member * jnp.arange(lengths.shape[0], dtype=jnp.int32)[None, :], axis=1)
    position = places - jnp.sum(member * starts[None, :], axis=1)
    chosen = jnp.sum(member * adapters[None, :], axis=1)
    slot_ids = jnp.arange(slot_adapter_index.shape[0], dtype=jnp.int32)
    token_slot = jnp.sum(
        (chosen[:, None] == slot_adapter_index[None, :]).astype(jnp.int32) * slot_ids[None, :],
        axis=1,
    )
    return (request, position, token_slot)


def allowed_keys(request, position, window):
    distance = position[:, None] - position[None, :]
    return (
        (request[:, None] == request[None, :])
        & (distance >= 0)
        & ((distance < window) | (position[None, :] < SINKS))
    )


def attention(queries, key_heads, value_heads, request, position, window):
    scores = jnp.einsum(
        "qhd,khd->hqk", queries, key_heads, preferred_element_type=jnp.float32
    ) * HEAD_SIZE ** (-0.5)
    allowed = allowed_keys(request, position, window)
    scores = jnp.where(allowed[None, :, :], scores, -1e30)
    row_peak = jnp.max(scores, axis=-1, keepdims=True)
    weights = jnp.exp(scores - row_peak)
    weights = (weights / jnp.sum(weights, axis=-1, keepdims=True)).astype(jnp.bfloat16)
    context = jnp.einsum("hqk,khd->qhd", weights, value_heads, preferred_element_type=jnp.float32)
    return context.astype(jnp.bfloat16)


def hidden_units(states, gate_rows, up_rows):
    contract = (((1,), (1,)), ((), ()))
    gate_act = lax.dot_general(states, gate_rows, contract, preferred_element_type=jnp.float32)
    up_act = lax.dot_general(states, up_rows, contract, preferred_element_type=jnp.float32)
    return (jax.nn.silu(gate_act) * up_act).astype(jnp.bfloat16)


def exchange(block, axis):
    return lax.ppermute(block, axis, [(0, 1), (1, 0)])


def shift(block, hops):
    return lax.ppermute(block, "mlp", [((k + hops) % 4, k) for k in range(4)])


def line_gather(block):
    across = shift(block, 2)
    return [block, shift(block, 1), across, shift(block, 3)]


def line_arrivals(parts):
    across = shift(parts[2], 2)
    return [shift(parts[3], 1), across, shift(parts[1], 3), parts[0]]


def line_sum(arrivals):
    return sum(part.astype(jnp.float32) for part in arrivals)


def together(*values):
    return lax.optimization_barrier(values)


def both_halves(*rows):
    (half,) = staged(rows)
    return half, pltpu.with_memory_space_constraint(exchange(half, "core"), pltpu.VMEM)


def vmem_call(kernel, outs, scratch, operands, vmem_mib):
    whole = pl.BlockSpec(memory_space=pltpu.VMEM)
    return pl.pallas_call(
        kernel,
        out_shape=outs,
        in_specs=[whole] * len(operands),
        out_specs=[whole] * len(outs),
        scratch_shapes=scratch,
        compiler_params=pltpu.CompilerParams(vmem_limit_bytes=vmem_mib << 20),
        cost_estimate=pl.CostEstimate(flops=1 << 20, bytes_accessed=1 << 20, transcendentals=0),
    )(*operands)


def in_hbm(array):
    return pltpu.with_memory_space_constraint(array, pltpu.HBM)


def staged(*groups, weight=4):
    groups = [
        [piece if isinstance(piece, tuple) else (piece, 0, piece.shape[0]) for piece in group]
        for group in groups
    ]
    arrays = []
    for piece in (piece for group in groups for piece in group):
        if not any(piece[0] is array for array in arrays):
            arrays.append(piece[0])
    places = [
        [next(k for k, array in enumerate(arrays) if array is piece[0]) for piece in group]
        for group in groups
    ]
    count = sum(len(group) for group in groups)

    def kernel(*refs):
        sources, targets, sems = refs[: len(arrays)], refs[len(arrays) : -1], refs[-1]
        copies = []
        for group, place, target in zip(groups, places, targets):
            at = 0
            for (_, start, rows), k in zip(group, place):
                copies.append(
                    pltpu.make_async_copy(
                        sources[k].at[pl.ds(start, rows), :],
                        target.at[pl.ds(at, rows), :],
                        sems.at[len(copies)],
                    )
                )
                copies[-1].start()
                at += rows
        for copy in copies:
            copy.wait()

    outs = [(sum(piece[2] for piece in group), group[0][0].shape[1]) for group in groups]
    size = sum(rows * columns for rows, columns in outs)
    return pl.pallas_call(
        kernel,
        out_shape=[pltpu.VMEM(shape, group[0][0].dtype) for shape, group in zip(outs, groups)],
        in_specs=[pl.BlockSpec(memory_space=pl.ANY)] * len(arrays),
        out_specs=[pl.BlockSpec(memory_space=pltpu.VMEM)] * len(groups),
        scratch_shapes=[pltpu.SemaphoreType.DMA((count,))],
        compiler_params=pltpu.CompilerParams(vmem_limit_bytes=1 << 20),
        cost_estimate=pl.CostEstimate(flops=0, bytes_accessed=weight * size, transcendentals=0),
    )(*arrays)


def stacked(*arrays):
    rows, columns = arrays[0].shape

    def kernel(*refs):
        sources, target, buffer, sems_in, sems_out = refs[:-4], *refs[-4:]
        into = [
            pltpu.make_async_copy(source, buffer.at[k], sems_in.at[k])
            for k, source in enumerate(sources)
        ]
        out = [
            pltpu.make_async_copy(
                buffer.at[k], target.at[pl.ds(k * rows, rows), :], sems_out.at[k]
            )
            for k in range(len(sources))
        ]
        for copy in into:
            copy.start()
        for copy_in, copy_out in zip(into, out):
            copy_in.wait()
            copy_out.start()
        for copy in out:
            copy.wait()

    count = len(arrays)
    return pl.pallas_call(
        kernel,
        out_shape=pltpu.HBM((count * rows, columns), arrays[0].dtype),
        in_specs=[pl.BlockSpec(memory_space=pl.ANY)] * count,
        out_specs=pl.BlockSpec(memory_space=pltpu.HBM),
        scratch_shapes=[
            pltpu.VMEM((count, rows, columns), arrays[0].dtype),
            pltpu.SemaphoreType.DMA((count,)),
            pltpu.SemaphoreType.DMA((count,)),
        ],
        compiler_params=pltpu.CompilerParams(vmem_limit_bytes=8 << 20),
        cost_estimate=pl.CostEstimate(flops=0, bytes_accessed=1 << 20, transcendentals=0),
    )(*(in_hbm(array) for array in arrays))


NT = (((1,), (1,)), ((), ()))


def attention_kernel(
    block_0,
    block_1,
    block_2,
    block_3,
    query_weight,
    key_weight,
    value_weight,
    output_weight,
    query_down,
    value_down,
    query_up,
    value_up,
    query_gain,
    key_gain,
    cosine,
    sine,
    slot_mask,
    allowed,
    out_0,
    out_1,
    out_2,
    out_3,
    rows,
    context,
):
    tok_dev = block_0.shape[0]
    for k, block in enumerate((block_0, block_1, block_2, block_3)):
        rows[k * tok_dev : (k + 1) * tok_dev, :] = block[...]

    def project(weight):
        return jnp.dot(rows[...], weight[...], preferred_element_type=jnp.float32)

    def adapted(weight, down, up):
        low = project(down).astype(jnp.bfloat16) * slot_mask[...]
        return project(weight) + adapter_scale * jnp.dot(
            low, up[...], preferred_element_type=jnp.float32
        )

    def heads(inputs, gain):
        inputs = rms_scale(inputs) * gain
        turned = pltpu.roll(inputs, HEAD_SIZE // 2, 1)
        return (inputs * cosine[...] + turned * sine[...]).astype(jnp.bfloat16)

    queries = adapted(query_weight, query_down, query_up)
    keys = project(key_weight)
    values = adapted(value_weight, value_down, value_up).astype(jnp.bfloat16)
    for start in range(0, queries.shape[1], HEAD_SIZE):
        at = slice(start, start + HEAD_SIZE)
        scores = lax.dot_general(
            heads(queries[:, at], query_gain[:, at]),
            heads(keys[:, at], key_gain[:, at]),
            NT,
            preferred_element_type=jnp.float32,
        ) * HEAD_SIZE ** (-0.5)
        scores = jnp.where(allowed[...] > 0, scores, -1e30)
        weights = jnp.exp(scores - jnp.max(scores, axis=-1, keepdims=True))
        weights = (weights / jnp.sum(weights, axis=-1, keepdims=True)).astype(jnp.bfloat16)
        context[:, at] = jnp.dot(
            weights, values[:, at], preferred_element_type=jnp.float32
        ).astype(jnp.bfloat16)
    step = 1024
    for start in range(0, output_weight.shape[1], step):
        at = slice(start, start + step)
        part = jnp.dot(context[...], output_weight[:, at], preferred_element_type=jnp.float32)
        part = part.astype(jnp.bfloat16)
        for k, out in enumerate((out_0, out_1, out_2, out_3)):
            out[:, at] = part[k * tok_dev : (k + 1) * tok_dev]


def hidden_kernel(states, gate_0, gate_1, up_0, up_1, out):
    count = gate_0.shape[0]
    for k, (gate_rows, up_rows) in enumerate(((gate_0, up_0), (gate_1, up_1))):
        gate_act = lax.dot_general(
            states[...], gate_rows[...], NT, preferred_element_type=jnp.float32
        )
        up_act = lax.dot_general(states[...], up_rows[...], NT, preferred_element_type=jnp.float32)
        hidden = gate_act / (1.0 + jnp.exp(-gate_act)) * up_act
        out[:, k * count : (k + 1) * count] = hidden.astype(jnp.bfloat16)


def down_kernel(near, far, near_0, near_1, far_0, far_1, out_0, out_1, out_2, out_3):
    tok_dev, count = out_0.shape[0], near_0.shape[0]
    step = 512
    for start in range(0, near_0.shape[1], step):
        at = slice(start, start + step)
        part = 0.0
        for hidden, halves in ((near, (near_0, near_1)), (far, (far_0, far_1))):
            for k, rows in enumerate(halves):
                part += jnp.dot(
                    hidden[:, k * count : (k + 1) * count],
                    rows[:, at],
                    preferred_element_type=jnp.float32,
                )
        part = part.astype(jnp.bfloat16)
        for k, out in enumerate((out_0, out_1, out_2, out_3)):
            out[:, at] = part[k * tok_dev : (k + 1) * tok_dev]


def add_normed(base, added, gain):
    return (base.astype(jnp.float32) + rms_scale(added) * gain).astype(jnp.bfloat16)


def layer_direct(
    layer_input, angles, slot_mask, allowed, projections, adapters, head_gains, gains, ffn_rows
):
    tok_dev, width = layer_input.shape
    gate_rows, up_rows, down_rows = ffn_rows
    y = lax.axis_index("y")
    half = width // 2
    units = gate_rows.shape[0]
    gate_up_x = exchange(stacked(gate_rows, up_rows), "x")
    cosine, sine = jnp.cos(angles), jnp.sin(angles)
    block = jax.ShapeDtypeStruct((tok_dev, width), jnp.bfloat16)
    *staged_rows, own_block = staged(
        *([in_hbm(array)] for array in (*projections, *adapters, *head_gains, layer_input)),
        weight=0,
    )
    *blocks, own_block, down_rows = together(*line_gather(layer_input)[1:], own_block, down_rows)
    parts = vmem_call(
        attention_kernel,
        [block] * 4,
        [
            pltpu.VMEM((4 * tok_dev, width), jnp.bfloat16),
            pltpu.VMEM((4 * tok_dev, projections[0].shape[1]), jnp.bfloat16),
        ],
        [
            own_block,
            *blocks,
            *staged_rows,
            jnp.concatenate([cosine, cosine], axis=1),
            jnp.concatenate([-sine, sine], axis=1),
            slot_mask,
            allowed,
        ],
        8,
    )
    near = lax.dynamic_slice_in_dim(down_rows, y * half, half, axis=1)
    far = exchange(lax.dynamic_slice_in_dim(down_rows, (1 - y) * half, half, axis=1), "y")
    arrivals = line_arrivals(parts)
    attn_own, near, far = together(line_sum(arrivals), near, far)
    near_x = [exchange(rows, "x") for rows in jnp.split(near, 2)]
    residual_own = add_normed(layer_input, attn_own, gains[0])
    own, *line, other = together(*line_gather(residual_own), exchange(residual_own, "y"))
    line, gate_up_x, near_x[0] = together(jnp.concatenate(line), gate_up_x, near_x[0])
    far_x = exchange(far, "x")
    halves = [
        *both_halves(in_hbm(gate_rows), (gate_up_x, 0, units)),
        *both_halves(in_hbm(up_rows), (gate_up_x, units, units)),
    ]

    def hidden_units_of(first, others):
        (hidden,) = vmem_call(
            hidden_kernel,
            [jax.ShapeDtypeStruct((4 * tok_dev, 4 * gate_rows.shape[0]), jnp.bfloat16)],
            [],
            [jnp.concatenate([first, others]), *halves],
            8,
        )
        return hidden

    line_other = exchange(line, "y")
    hidden_own = hidden_units_of(own, line)
    line_other, hidden_own = together(line_other, hidden_own)
    from_own = exchange(hidden_own, "y")
    hidden_other = hidden_units_of(other, line_other)
    hidden_other, from_own, far_x, near_x[1] = together(hidden_other, from_own, far_x, near_x[1])
    from_other = exchange(hidden_other, "y")
    down_halves = [*both_halves(near, *near_x), *both_halves(far, far_x)]

    def summed_down(hidden, from_y):
        parts = vmem_call(
            down_kernel,
            [jax.ShapeDtypeStruct((tok_dev, half), jnp.bfloat16)] * 4,
            [],
            [hidden, from_y, *down_halves],
            8,
        )
        return line_sum(line_arrivals(parts))

    other_half = exchange(summed_down(hidden_other, from_own).astype(jnp.bfloat16), "y")
    own_half = summed_down(hidden_own, from_other)
    other_half = other_half.astype(jnp.float32)
    mlp_own = jnp.concatenate(
        [jnp.where(y == 1, other_half, own_half), jnp.where(y == 1, own_half, other_half)], axis=1
    )
    return add_normed(residual_own, mlp_own, gains[1])


def shards(
    layer_input,
    request_lengths,
    request_adapter,
    slot_adapter_index,
    query_weight,
    key_weight,
    value_weight,
    output_weight,
    query_norm_gain,
    key_norm_gain,
    query_down_factors,
    value_down_factors,
    query_up_factors,
    value_up_factors,
    attention_norm_gain,
    feedforward_norm_gain,
    gate_weight,
    up_weight,
    down_weight_transposed,
):
    tok_dev = layer_input.shape[0]
    tok_group = tok_dev * lax.axis_size("mlp")
    window = tok_group * 3 // 8
    heads_local = query_weight.shape[1] // HEAD_SIZE
    direct = [lax.axis_size(axis) for axis in (*REQ, "mlp")] == [2, 2, 2, 4]
    places = jnp.arange(tok_group, dtype=jnp.int32)
    if direct:
        places = (places + lax.axis_index("mlp") * tok_dev) % tok_group
    request, position, token_slot = layout(
        request_lengths[0], request_adapter[0], slot_adapter_index, places
    )
    columns = jnp.arange(ADAPTER_SLOTS * ADAPTER_RANK, dtype=jnp.int32) // ADAPTER_RANK
    slot_match_mask = (columns[None, :] == token_slot[:, None]).astype(jnp.bfloat16)
    gate_rows, up_rows, down_rows = gate_weight.T, up_weight.T, down_weight_transposed.T
    if direct:
        return layer_direct(
            layer_input,
            rotary_angles(position),
            slot_match_mask,
            allowed_keys(request, position, window).astype(jnp.float32),
            (query_weight, key_weight, value_weight, output_weight),
            (query_down_factors, value_down_factors, query_up_factors, value_up_factors),
            (query_norm_gain[None, :], key_norm_gain[None, :]),
            (attention_norm_gain, feedforward_norm_gain),
            (gate_rows, up_rows, down_rows),
        )
    group_token_rows = lax.all_gather(layer_input, "mlp", axis=0, tiled=True)
    query_reduced = (
        jnp.dot(group_token_rows, query_down_factors, preferred_element_type=jnp.float32).astype(
            jnp.bfloat16
        )
        * slot_match_mask
    )
    value_reduced = (
        jnp.dot(group_token_rows, value_down_factors, preferred_element_type=jnp.float32).astype(
            jnp.bfloat16
        )
        * slot_match_mask
    )
    query_before_norm = jnp.dot(
        group_token_rows, query_weight, preferred_element_type=jnp.float32
    ) + adapter_scale * jnp.dot(query_reduced, query_up_factors, preferred_element_type=jnp.float32)
    key_pre = jnp.dot(group_token_rows, key_weight, preferred_element_type=jnp.float32)
    value_before_adapter = jnp.dot(
        group_token_rows, value_weight, preferred_element_type=jnp.float32
    ) + adapter_scale * jnp.dot(value_reduced, value_up_factors, preferred_element_type=jnp.float32)
    queries = rotary(
        rms_scale(query_before_norm.reshape(tok_group, heads_local, HEAD_SIZE))
        * query_norm_gain.reshape(heads_local, HEAD_SIZE),
        position,
    ).astype(jnp.bfloat16)
    key_heads = rotary(
        rms_scale(key_pre.reshape(tok_group, heads_local, HEAD_SIZE))
        * key_norm_gain.reshape(heads_local, HEAD_SIZE),
        position,
    ).astype(jnp.bfloat16)
    value_heads = value_before_adapter.astype(jnp.bfloat16).reshape(
        tok_group, heads_local, HEAD_SIZE
    )
    context = attention(queries, key_heads, value_heads, request, position, window).reshape(
        tok_group, heads_local * HEAD_SIZE
    )
    attn_own = lax.psum_scatter(
        jnp.dot(context, output_weight, preferred_element_type=jnp.float32).astype(jnp.bfloat16),
        "mlp",
        scatter_dimension=0,
        tiled=True,
    ).astype(jnp.float32)
    residual_own = add_normed(layer_input, attn_own, attention_norm_gain)
    gate_rows, up_rows, down_rows = (
        lax.all_gather(rows, REQ, axis=0, tiled=True) for rows in (gate_rows, up_rows, down_rows)
    )
    hidden = hidden_units(
        lax.all_gather(residual_own, "mlp", axis=0, tiled=True), gate_rows, up_rows
    )
    part = jnp.dot(hidden, down_rows, preferred_element_type=jnp.float32)
    mlp_own = lax.psum_scatter(
        part.astype(jnp.bfloat16), "mlp", scatter_dimension=0, tiled=True
    ).astype(jnp.float32)
    return add_normed(residual_own, mlp_own, feedforward_norm_gain)


def solution(mesh):
    req, mlp = mesh.devices.shape
    side = math.isqrt(req // 2)
    fine = Mesh(mesh.devices.reshape(req // 2 // side, side, 2, mlp), ("y", "x", "core", "mlp"))
    return jax.shard_map(
        shards,
        mesh=fine,
        in_specs=(
            P((*REQ, "mlp"), None),
            P(REQ, None),
            P(REQ, None),
            P(),
            P(None, "mlp"),
            P(None, "mlp"),
            P(None, "mlp"),
            P("mlp", None),
            P("mlp"),
            P("mlp"),
            P(),
            P(),
            P(None, "mlp"),
            P(None, "mlp"),
            P(),
            P(),
            P(None, (*REQ, "mlp")),
            P(None, (*REQ, "mlp")),
            P(None, (*REQ, "mlp")),
        ),
        out_specs=P((*REQ, "mlp"), None),
        check_vma=False,
    )
```

```python
import math

import jax
import jax.numpy as jnp
from jax import lax
from jax.experimental import pallas as pl
from jax.experimental.pallas import tpu as pltpu
from jax.sharding import Mesh, PartitionSpec as P

HEAD_SIZE = 128
ADAPTER_RANK = 16
ADAPTER_SLOTS = 8
SINKS = 4
REQ = ("y", "x", "core")


epsilon = 1e-06
adapter_scale = 0.5
rope_theta = 500000.0


def rms_scale(inputs):
    return inputs * lax.rsqrt(jnp.mean(inputs * inputs, axis=-1, keepdims=True) + epsilon)


def rotary_angles(position):
    exponent = jnp.arange(HEAD_SIZE // 2, dtype=jnp.float32) * (2.0 / HEAD_SIZE)
    frequency = rope_theta ** (-exponent)
    return position.astype(jnp.float32)[:, None] * frequency[None, :]


def rotary(inputs, position):
    half_dim = inputs.shape[-1] // 2
    angles = rotary_angles(position)
    cosine = jnp.cos(angles)[:, None, :]
    sine_part = jnp.sin(angles)[:, None, :]
    first_half = inputs[..., :half_dim]
    second = inputs[..., half_dim:]
    return jnp.concatenate(
        [first_half * cosine - second * sine_part, second * cosine + first_half * sine_part],
        axis=-1,
    )


def layout(lengths, adapters, slot_adapter_index, places):
    req_ends = jnp.cumsum(lengths)
    starts = req_ends - lengths
    member = ((places[:, None] >= starts[None, :]) & (places[:, None] < req_ends[None, :])).astype(
        jnp.int32
    )
    request = jnp.sum(member * jnp.arange(lengths.shape[0], dtype=jnp.int32)[None, :], axis=1)
    position = places - jnp.sum(member * starts[None, :], axis=1)
    chosen = jnp.sum(member * adapters[None, :], axis=1)
    slot_ids = jnp.arange(slot_adapter_index.shape[0], dtype=jnp.int32)
    token_slot = jnp.sum(
        (chosen[:, None] == slot_adapter_index[None, :]).astype(jnp.int32) * slot_ids[None, :],
        axis=1,
    )
    return (request, position, token_slot)


def allowed_keys(request, position, window):
    distance = position[:, None] - position[None, :]
    return (
        (request[:, None] == request[None, :])
        & (distance >= 0)
        & ((distance < window) | (position[None, :] < SINKS))
    )


def attention(queries, key_heads, value_heads, request, position, window):
    scores = jnp.einsum(
        "qhd,khd->hqk", queries, key_heads, preferred_element_type=jnp.float32
    ) * HEAD_SIZE ** (-0.5)
    allowed = allowed_keys(request, position, window)
    scores = jnp.where(allowed[None, :, :], scores, -1e30)
    row_peak = jnp.max(scores, axis=-1, keepdims=True)
    weights = jnp.exp(scores - row_peak)
    weights = (weights / jnp.sum(weights, axis=-1, keepdims=True)).astype(jnp.bfloat16)
    context = jnp.einsum("hqk,khd->qhd", weights, value_heads, preferred_element_type=jnp.float32)
    return context.astype(jnp.bfloat16)


def hidden_units(states, gate_rows, up_rows):
    contract = (((1,), (1,)), ((), ()))
    gate_act = lax.dot_general(states, gate_rows, contract, preferred_element_type=jnp.float32)
    up_act = lax.dot_general(states, up_rows, contract, preferred_element_type=jnp.float32)
    return (jax.nn.silu(gate_act) * up_act).astype(jnp.bfloat16)


def exchange(block, axis):
    return lax.ppermute(block, axis, [(0, 1), (1, 0)])


def shift(block, hops):
    return lax.ppermute(block, "mlp", [((k + hops) % 4, k) for k in range(4)])


def line_gather(block):
    across = shift(block, 2)
    return [block, shift(block, 1), across, shift(block, 3)]


def line_arrivals(parts):
    across = shift(parts[2], 2)
    return [shift(parts[3], 1), across, shift(parts[1], 3), parts[0]]


def line_sum(arrivals):
    return sum(part.astype(jnp.float32) for part in arrivals)


def together(*values):
    return lax.optimization_barrier(values)


def both_halves(*rows):
    (half,) = staged(rows)
    return half, pltpu.with_memory_space_constraint(exchange(half, "core"), pltpu.VMEM)


def vmem_call(kernel, outs, scratch, operands, vmem_mib):
    whole = pl.BlockSpec(memory_space=pltpu.VMEM)
    return pl.pallas_call(
        kernel,
        out_shape=outs,
        in_specs=[whole] * len(operands),
        out_specs=[whole] * len(outs),
        scratch_shapes=scratch,
        compiler_params=pltpu.CompilerParams(vmem_limit_bytes=vmem_mib << 20),
        cost_estimate=pl.CostEstimate(flops=1 << 20, bytes_accessed=1 << 20, transcendentals=0),
    )(*operands)


def in_hbm(array):
    return pltpu.with_memory_space_constraint(array, pltpu.HBM)


def staged(*groups, weight=4):
    groups = [
        [piece if isinstance(piece, tuple) else (piece, 0, piece.shape[0]) for piece in group]
        for group in groups
    ]
    arrays = []
    for piece in (piece for group in groups for piece in group):
        if not any(piece[0] is array for array in arrays):
            arrays.append(piece[0])
    places = [
        [next(k for k, array in enumerate(arrays) if array is piece[0]) for piece in group]
        for group in groups
    ]
    count = sum(len(group) for group in groups)

    def kernel(*refs):
        sources, targets, sems = refs[: len(arrays)], refs[len(arrays) : -1], refs[-1]
        copies = []
        for group, place, target in zip(groups, places, targets):
            at = 0
            for (_, start, rows), k in zip(group, place):
                copies.append(
                    pltpu.make_async_copy(
                        sources[k].at[pl.ds(start, rows), :],
                        target.at[pl.ds(at, rows), :],
                        sems.at[len(copies)],
                    )
                )
                copies[-1].start()
                at += rows
        for copy in copies:
            copy.wait()

    outs = [(sum(piece[2] for piece in group), group[0][0].shape[1]) for group in groups]
    size = sum(rows * columns for rows, columns in outs)
    return pl.pallas_call(
        kernel,
        out_shape=[pltpu.VMEM(shape, group[0][0].dtype) for shape, group in zip(outs, groups)],
        in_specs=[pl.BlockSpec(memory_space=pl.ANY)] * len(arrays),
        out_specs=[pl.BlockSpec(memory_space=pltpu.VMEM)] * len(groups),
        scratch_shapes=[pltpu.SemaphoreType.DMA((count,))],
        compiler_params=pltpu.CompilerParams(vmem_limit_bytes=1 << 20),
        cost_estimate=pl.CostEstimate(flops=0, bytes_accessed=weight * size, transcendentals=0),
    )(*arrays)


def stacked(*arrays):
    rows, columns = arrays[0].shape
    pieces = 3
    part = rows // pieces
    count = len(arrays) * pieces

    def kernel(*refs):
        sources, target, buffer, sems_in, sems_out = refs[:-4], *refs[-4:]
        into = [
            pltpu.make_async_copy(
                sources[k // pieces].at[pl.ds(k % pieces * part, part), :],
                buffer.at[k],
                sems_in.at[k],
            )
            for k in range(count)
        ]
        out = [
            pltpu.make_async_copy(
                buffer.at[k], target.at[pl.ds(k * part, part), :], sems_out.at[k]
            )
            for k in range(count)
        ]
        for copy in into:
            copy.start()
        for copy_in, copy_out in zip(into, out):
            copy_in.wait()
            copy_out.start()
        for copy in out:
            copy.wait()

    return pl.pallas_call(
        kernel,
        out_shape=pltpu.HBM((len(arrays) * rows, columns), arrays[0].dtype),
        in_specs=[pl.BlockSpec(memory_space=pl.ANY)] * len(arrays),
        out_specs=pl.BlockSpec(memory_space=pltpu.HBM),
        scratch_shapes=[
            pltpu.VMEM((count, part, columns), arrays[0].dtype),
            pltpu.SemaphoreType.DMA((count,)),
            pltpu.SemaphoreType.DMA((count,)),
        ],
        compiler_params=pltpu.CompilerParams(vmem_limit_bytes=8 << 20),
        cost_estimate=pl.CostEstimate(flops=0, bytes_accessed=1 << 20, transcendentals=0),
    )(*(in_hbm(array) for array in arrays))


NT = (((1,), (1,)), ((), ()))


def attention_kernel(
    block_0,
    block_1,
    block_2,
    block_3,
    query_weight,
    key_weight,
    value_weight,
    output_weight,
    query_down,
    value_down,
    query_up,
    value_up,
    query_gain,
    key_gain,
    cosine,
    sine,
    slot_mask,
    allowed,
    out_0,
    out_1,
    out_2,
    out_3,
    rows,
    context,
):
    tok_dev = block_0.shape[0]
    for k, block in enumerate((block_0, block_1, block_2, block_3)):
        rows[k * tok_dev : (k + 1) * tok_dev, :] = block[...]

    def project(weight):
        return jnp.dot(rows[...], weight[...], preferred_element_type=jnp.float32)

    def adapted(weight, down, up):
        low = project(down).astype(jnp.bfloat16) * slot_mask[...]
        return project(weight) + adapter_scale * jnp.dot(
            low, up[...], preferred_element_type=jnp.float32
        )

    def heads(inputs, gain):
        inputs = rms_scale(inputs) * gain
        turned = pltpu.roll(inputs, HEAD_SIZE // 2, 1)
        return (inputs * cosine[...] + turned * sine[...]).astype(jnp.bfloat16)

    queries = adapted(query_weight, query_down, query_up)
    keys = project(key_weight)
    values = adapted(value_weight, value_down, value_up).astype(jnp.bfloat16)
    for start in range(0, queries.shape[1], HEAD_SIZE):
        at = slice(start, start + HEAD_SIZE)
        scores = lax.dot_general(
            heads(queries[:, at], query_gain[:, at]),
            heads(keys[:, at], key_gain[:, at]),
            NT,
            preferred_element_type=jnp.float32,
        ) * HEAD_SIZE ** (-0.5)
        scores = jnp.where(allowed[...] > 0, scores, -1e30)
        weights = jnp.exp(scores - jnp.max(scores, axis=-1, keepdims=True))
        weights = (weights / jnp.sum(weights, axis=-1, keepdims=True)).astype(jnp.bfloat16)
        context[:, at] = jnp.dot(
            weights, values[:, at], preferred_element_type=jnp.float32
        ).astype(jnp.bfloat16)
    step = 1024
    for start in range(0, output_weight.shape[1], step):
        at = slice(start, start + step)
        part = jnp.dot(context[...], output_weight[:, at], preferred_element_type=jnp.float32)
        part = part.astype(jnp.bfloat16)
        for k, out in enumerate((out_0, out_1, out_2, out_3)):
            out[:, at] = part[k * tok_dev : (k + 1) * tok_dev]


def hidden_kernel(states, gate_0, gate_1, up_0, up_1, out):
    count = gate_0.shape[0]
    for k, (gate_rows, up_rows) in enumerate(((gate_0, up_0), (gate_1, up_1))):
        gate_act = lax.dot_general(
            states[...], gate_rows[...], NT, preferred_element_type=jnp.float32
        )
        up_act = lax.dot_general(states[...], up_rows[...], NT, preferred_element_type=jnp.float32)
        hidden = gate_act / (1.0 + jnp.exp(-gate_act)) * up_act
        out[:, k * count : (k + 1) * count] = hidden.astype(jnp.bfloat16)


def down_kernel(near, far, near_0, near_1, far_0, far_1, out_0, out_1, out_2, out_3):
    tok_dev, count = out_0.shape[0], near_0.shape[0]
    step = 512
    for start in range(0, near_0.shape[1], step):
        at = slice(start, start + step)
        part = 0.0
        for hidden, halves in ((near, (near_0, near_1)), (far, (far_0, far_1))):
            for k, rows in enumerate(halves):
                part += jnp.dot(
                    hidden[:, k * count : (k + 1) * count],
                    rows[:, at],
                    preferred_element_type=jnp.float32,
                )
        part = part.astype(jnp.bfloat16)
        for k, out in enumerate((out_0, out_1, out_2, out_3)):
            out[:, at] = part[k * tok_dev : (k + 1) * tok_dev]


def add_normed(base, added, gain):
    return (base.astype(jnp.float32) + rms_scale(added) * gain).astype(jnp.bfloat16)


def layer_direct(
    layer_input, angles, slot_mask, allowed, projections, adapters, head_gains, gains, ffn_rows
):
    tok_dev, width = layer_input.shape
    gate_rows, up_rows, down_rows = ffn_rows
    y = lax.axis_index("y")
    half = width // 2
    units = gate_rows.shape[0]
    gate_up_x = exchange(stacked(gate_rows, up_rows), "x")
    cosine, sine = jnp.cos(angles), jnp.sin(angles)
    block = jax.ShapeDtypeStruct((tok_dev, width), jnp.bfloat16)
    *staged_rows, own_block = staged(
        *([in_hbm(array)] for array in (*projections, *adapters, *head_gains, layer_input)),
        weight=0,
    )
    *blocks, own_block, down_rows = together(*line_gather(layer_input)[1:], own_block, down_rows)
    parts = vmem_call(
        attention_kernel,
        [block] * 4,
        [
            pltpu.VMEM((4 * tok_dev, width), jnp.bfloat16),
            pltpu.VMEM((4 * tok_dev, projections[0].shape[1]), jnp.bfloat16),
        ],
        [
            own_block,
            *blocks,
            *staged_rows,
            jnp.concatenate([cosine, cosine], axis=1),
            jnp.concatenate([-sine, sine], axis=1),
            slot_mask,
            allowed,
        ],
        8,
    )
    near = lax.dynamic_slice_in_dim(down_rows, y * half, half, axis=1)
    far = exchange(lax.dynamic_slice_in_dim(down_rows, (1 - y) * half, half, axis=1), "y")
    arrivals = line_arrivals(parts)
    attn_own, near, far = together(line_sum(arrivals), near, far)
    near_x = [exchange(rows, "x") for rows in jnp.split(near, 2)]
    residual_own = add_normed(layer_input, attn_own, gains[0])
    own, *line, other = together(*line_gather(residual_own), exchange(residual_own, "y"))
    line, gate_up_x, near_x[0] = together(jnp.concatenate(line), gate_up_x, near_x[0])
    far_x = exchange(far, "x")
    halves = [
        *both_halves(in_hbm(gate_rows), (gate_up_x, 0, units)),
        *both_halves(in_hbm(up_rows), (gate_up_x, units, units)),
    ]

    def hidden_units_of(first, others):
        (hidden,) = vmem_call(
            hidden_kernel,
            [jax.ShapeDtypeStruct((4 * tok_dev, 4 * gate_rows.shape[0]), jnp.bfloat16)],
            [],
            [jnp.concatenate([first, others]), *halves],
            8,
        )
        return hidden

    line_other = exchange(line, "y")
    hidden_own = hidden_units_of(own, line)
    line_other, hidden_own, near_x[1] = together(line_other, hidden_own, near_x[1])
    from_own = exchange(hidden_own, "y")
    hidden_other = hidden_units_of(other, line_other)
    hidden_other, from_own, far_x = together(hidden_other, from_own, far_x)
    from_other = exchange(hidden_other, "y")
    down_halves = [*both_halves(near, *near_x), *both_halves(far, far_x)]

    def summed_down(hidden, from_y):
        parts = vmem_call(
            down_kernel,
            [jax.ShapeDtypeStruct((tok_dev, half), jnp.bfloat16)] * 4,
            [],
            [hidden, from_y, *down_halves],
            8,
        )
        return line_sum(line_arrivals(parts))

    other_half = exchange(summed_down(hidden_other, from_own).astype(jnp.bfloat16), "y")
    own_half = summed_down(hidden_own, from_other)
    other_half = other_half.astype(jnp.float32)
    mlp_own = jnp.concatenate(
        [jnp.where(y == 1, other_half, own_half), jnp.where(y == 1, own_half, other_half)], axis=1
    )
    return add_normed(residual_own, mlp_own, gains[1])


def shards(
    layer_input,
    request_lengths,
    request_adapter,
    slot_adapter_index,
    query_weight,
    key_weight,
    value_weight,
    output_weight,
    query_norm_gain,
    key_norm_gain,
    query_down_factors,
    value_down_factors,
    query_up_factors,
    value_up_factors,
    attention_norm_gain,
    feedforward_norm_gain,
    gate_weight,
    up_weight,
    down_weight_transposed,
):
    tok_dev = layer_input.shape[0]
    tok_group = tok_dev * lax.axis_size("mlp")
    window = tok_group * 3 // 8
    heads_local = query_weight.shape[1] // HEAD_SIZE
    direct = [lax.axis_size(axis) for axis in (*REQ, "mlp")] == [2, 2, 2, 4]
    places = jnp.arange(tok_group, dtype=jnp.int32)
    if direct:
        places = (places + lax.axis_index("mlp") * tok_dev) % tok_group
    request, position, token_slot = layout(
        request_lengths[0], request_adapter[0], slot_adapter_index, places
    )
    columns = jnp.arange(ADAPTER_SLOTS * ADAPTER_RANK, dtype=jnp.int32) // ADAPTER_RANK
    slot_match_mask = (columns[None, :] == token_slot[:, None]).astype(jnp.bfloat16)
    gate_rows, up_rows, down_rows = gate_weight.T, up_weight.T, down_weight_transposed.T
    if direct:
        return layer_direct(
            layer_input,
            rotary_angles(position),
            slot_match_mask,
            allowed_keys(request, position, window).astype(jnp.float32),
            (query_weight, key_weight, value_weight, output_weight),
            (query_down_factors, value_down_factors, query_up_factors, value_up_factors),
            (query_norm_gain[None, :], key_norm_gain[None, :]),
            (attention_norm_gain, feedforward_norm_gain),
            (gate_rows, up_rows, down_rows),
        )
    group_token_rows = lax.all_gather(layer_input, "mlp", axis=0, tiled=True)
    query_reduced = (
        jnp.dot(group_token_rows, query_down_factors, preferred_element_type=jnp.float32).astype(
            jnp.bfloat16
        )
        * slot_match_mask
    )
    value_reduced = (
        jnp.dot(group_token_rows, value_down_factors, preferred_element_type=jnp.float32).astype(
            jnp.bfloat16
        )
        * slot_match_mask
    )
    query_before_norm = jnp.dot(
        group_token_rows, query_weight, preferred_element_type=jnp.float32
    ) + adapter_scale * jnp.dot(query_reduced, query_up_factors, preferred_element_type=jnp.float32)
    key_pre = jnp.dot(group_token_rows, key_weight, preferred_element_type=jnp.float32)
    value_before_adapter = jnp.dot(
        group_token_rows, value_weight, preferred_element_type=jnp.float32
    ) + adapter_scale * jnp.dot(value_reduced, value_up_factors, preferred_element_type=jnp.float32)
    queries = rotary(
        rms_scale(query_before_norm.reshape(tok_group, heads_local, HEAD_SIZE))
        * query_norm_gain.reshape(heads_local, HEAD_SIZE),
        position,
    ).astype(jnp.bfloat16)
    key_heads = rotary(
        rms_scale(key_pre.reshape(tok_group, heads_local, HEAD_SIZE))
        * key_norm_gain.reshape(heads_local, HEAD_SIZE),
        position,
    ).astype(jnp.bfloat16)
    value_heads = value_before_adapter.astype(jnp.bfloat16).reshape(
        tok_group, heads_local, HEAD_SIZE
    )
    context = attention(queries, key_heads, value_heads, request, position, window).reshape(
        tok_group, heads_local * HEAD_SIZE
    )
    attn_own = lax.psum_scatter(
        jnp.dot(context, output_weight, preferred_element_type=jnp.float32).astype(jnp.bfloat16),
        "mlp",
        scatter_dimension=0,
        tiled=True,
    ).astype(jnp.float32)
    residual_own = add_normed(layer_input, attn_own, attention_norm_gain)
    gate_rows, up_rows, down_rows = (
        lax.all_gather(rows, REQ, axis=0, tiled=True) for rows in (gate_rows, up_rows, down_rows)
    )
    hidden = hidden_units(
        lax.all_gather(residual_own, "mlp", axis=0, tiled=True), gate_rows, up_rows
    )
    part = jnp.dot(hidden, down_rows, preferred_element_type=jnp.float32)
    mlp_own = lax.psum_scatter(
        part.astype(jnp.bfloat16), "mlp", scatter_dimension=0, tiled=True
    ).astype(jnp.float32)
    return add_normed(residual_own, mlp_own, feedforward_norm_gain)


def solution(mesh):
    req, mlp = mesh.devices.shape
    side = math.isqrt(req // 2)
    fine = Mesh(mesh.devices.reshape(req // 2 // side, side, 2, mlp), ("y", "x", "core", "mlp"))
    return jax.shard_map(
        shards,
        mesh=fine,
        in_specs=(
            P((*REQ, "mlp"), None),
            P(REQ, None),
            P(REQ, None),
            P(),
            P(None, "mlp"),
            P(None, "mlp"),
            P(None, "mlp"),
            P("mlp", None),
            P("mlp"),
            P("mlp"),
            P(),
            P(),
            P(None, "mlp"),
            P(None, "mlp"),
            P(),
            P(),
            P(None, (*REQ, "mlp")),
            P(None, (*REQ, "mlp")),
            P(None, (*REQ, "mlp")),
        ),
        out_specs=P((*REQ, "mlp"), None),
        check_vma=False,
    )
```

```python
import math

import jax
import jax.numpy as jnp
from jax import lax
from jax.experimental import pallas as pl
from jax.experimental.pallas import tpu as pltpu
from jax.sharding import Mesh, PartitionSpec as P

HEAD_SIZE = 128
ADAPTER_RANK = 16
ADAPTER_SLOTS = 8
SINKS = 4
REQ = ("y", "x", "core")


epsilon = 1e-06
adapter_scale = 0.5
rope_theta = 500000.0


def rms_scale(inputs):
    return inputs * lax.rsqrt(jnp.mean(inputs * inputs, axis=-1, keepdims=True) + epsilon)


def rotary_angles(position):
    exponent = jnp.arange(HEAD_SIZE // 2, dtype=jnp.float32) * (2.0 / HEAD_SIZE)
    frequency = rope_theta ** (-exponent)
    return position.astype(jnp.float32)[:, None] * frequency[None, :]


def rotary(inputs, position):
    half_dim = inputs.shape[-1] // 2
    angles = rotary_angles(position)
    cosine = jnp.cos(angles)[:, None, :]
    sine_part = jnp.sin(angles)[:, None, :]
    first_half = inputs[..., :half_dim]
    second = inputs[..., half_dim:]
    return jnp.concatenate(
        [first_half * cosine - second * sine_part, second * cosine + first_half * sine_part],
        axis=-1,
    )


def layout(lengths, adapters, slot_adapter_index, places):
    req_ends = jnp.cumsum(lengths)
    starts = req_ends - lengths
    member = ((places[:, None] >= starts[None, :]) & (places[:, None] < req_ends[None, :])).astype(
        jnp.int32
    )
    request = jnp.sum(member * jnp.arange(lengths.shape[0], dtype=jnp.int32)[None, :], axis=1)
    position = places - jnp.sum(member * starts[None, :], axis=1)
    chosen = jnp.sum(member * adapters[None, :], axis=1)
    slot_ids = jnp.arange(slot_adapter_index.shape[0], dtype=jnp.int32)
    token_slot = jnp.sum(
        (chosen[:, None] == slot_adapter_index[None, :]).astype(jnp.int32) * slot_ids[None, :],
        axis=1,
    )
    return (request, position, token_slot)


def allowed_keys(request, position, window):
    distance = position[:, None] - position[None, :]
    return (
        (request[:, None] == request[None, :])
        & (distance >= 0)
        & ((distance < window) | (position[None, :] < SINKS))
    )


def attention(queries, key_heads, value_heads, request, position, window):
    scores = jnp.einsum(
        "qhd,khd->hqk", queries, key_heads, preferred_element_type=jnp.float32
    ) * HEAD_SIZE ** (-0.5)
    allowed = allowed_keys(request, position, window)
    scores = jnp.where(allowed[None, :, :], scores, -1e30)
    row_peak = jnp.max(scores, axis=-1, keepdims=True)
    weights = jnp.exp(scores - row_peak)
    weights = (weights / jnp.sum(weights, axis=-1, keepdims=True)).astype(jnp.bfloat16)
    context = jnp.einsum("hqk,khd->qhd", weights, value_heads, preferred_element_type=jnp.float32)
    return context.astype(jnp.bfloat16)


def hidden_units(states, gate_rows, up_rows):
    contract = (((1,), (1,)), ((), ()))
    gate_act = lax.dot_general(states, gate_rows, contract, preferred_element_type=jnp.float32)
    up_act = lax.dot_general(states, up_rows, contract, preferred_element_type=jnp.float32)
    return (jax.nn.silu(gate_act) * up_act).astype(jnp.bfloat16)


def exchange(block, axis):
    return lax.ppermute(block, axis, [(0, 1), (1, 0)])


def shift(block, hops):
    return lax.ppermute(block, "mlp", [((k + hops) % 4, k) for k in range(4)])


def line_gather(block):
    across = shift(block, 2)
    return [block, shift(block, 1), across, shift(block, 3)]


def line_arrivals(parts):
    across = shift(parts[2], 2)
    return [shift(parts[3], 1), across, shift(parts[1], 3), parts[0]]


def line_sum(arrivals):
    return sum(part.astype(jnp.float32) for part in arrivals)


def together(*values):
    return lax.optimization_barrier(values)


def swapped(half):
    return pltpu.with_memory_space_constraint(exchange(half, "core"), pltpu.VMEM)


def both_halves(*rows):
    (half,) = staged(rows)
    return half, swapped(half)


def vmem_call(kernel, outs, scratch, operands, vmem_mib):
    whole = pl.BlockSpec(memory_space=pltpu.VMEM)
    return pl.pallas_call(
        kernel,
        out_shape=outs,
        in_specs=[whole] * len(operands),
        out_specs=[whole] * len(outs),
        scratch_shapes=scratch,
        compiler_params=pltpu.CompilerParams(vmem_limit_bytes=vmem_mib << 20),
        cost_estimate=pl.CostEstimate(flops=1 << 20, bytes_accessed=1 << 20, transcendentals=0),
    )(*operands)


def in_hbm(array):
    return pltpu.with_memory_space_constraint(array, pltpu.HBM)


def staged(*groups, weight=4):
    groups = [
        [piece if isinstance(piece, tuple) else (piece, 0, piece.shape[0]) for piece in group]
        for group in groups
    ]
    arrays = []
    for piece in (piece for group in groups for piece in group):
        if not any(piece[0] is array for array in arrays):
            arrays.append(piece[0])
    places = [
        [next(k for k, array in enumerate(arrays) if array is piece[0]) for piece in group]
        for group in groups
    ]
    count = sum(len(group) for group in groups)

    def kernel(*refs):
        sources, targets, sems = refs[: len(arrays)], refs[len(arrays) : -1], refs[-1]
        copies = []
        for group, place, target in zip(groups, places, targets):
            at = 0
            for (_, start, rows), k in zip(group, place):
                copies.append(
                    pltpu.make_async_copy(
                        sources[k].at[pl.ds(start, rows), :],
                        target.at[pl.ds(at, rows), :],
                        sems.at[len(copies)],
                    )
                )
                copies[-1].start()
                at += rows
        for copy in copies:
            copy.wait()

    outs = [(sum(piece[2] for piece in group), group[0][0].shape[1]) for group in groups]
    size = sum(rows * columns for rows, columns in outs)
    return pl.pallas_call(
        kernel,
        out_shape=[pltpu.VMEM(shape, group[0][0].dtype) for shape, group in zip(outs, groups)],
        in_specs=[pl.BlockSpec(memory_space=pl.ANY)] * len(arrays),
        out_specs=[pl.BlockSpec(memory_space=pltpu.VMEM)] * len(groups),
        scratch_shapes=[pltpu.SemaphoreType.DMA((count,))],
        compiler_params=pltpu.CompilerParams(vmem_limit_bytes=1 << 20),
        cost_estimate=pl.CostEstimate(flops=0, bytes_accessed=weight * size, transcendentals=0),
    )(*arrays)


def stacked(*arrays):
    rows, columns = arrays[0].shape
    pieces = 3
    part = rows // pieces
    count = len(arrays) * pieces

    def kernel(*refs):
        sources, target, buffer, sems_in, sems_out = refs[:-4], *refs[-4:]
        into = [
            pltpu.make_async_copy(
                sources[k // pieces].at[pl.ds(k % pieces * part, part), :],
                buffer.at[k],
                sems_in.at[k],
            )
            for k in range(count)
        ]
        out = [
            pltpu.make_async_copy(
                buffer.at[k], target.at[pl.ds(k * part, part), :], sems_out.at[k]
            )
            for k in range(count)
        ]
        for copy in into:
            copy.start()
        for copy_in, copy_out in zip(into, out):
            copy_in.wait()
            copy_out.start()
        for copy in out:
            copy.wait()

    return pl.pallas_call(
        kernel,
        out_shape=pltpu.HBM((len(arrays) * rows, columns), arrays[0].dtype),
        in_specs=[pl.BlockSpec(memory_space=pl.ANY)] * len(arrays),
        out_specs=pl.BlockSpec(memory_space=pltpu.HBM),
        scratch_shapes=[
            pltpu.VMEM((count, part, columns), arrays[0].dtype),
            pltpu.SemaphoreType.DMA((count,)),
            pltpu.SemaphoreType.DMA((count,)),
        ],
        compiler_params=pltpu.CompilerParams(vmem_limit_bytes=8 << 20),
        cost_estimate=pl.CostEstimate(flops=0, bytes_accessed=1 << 20, transcendentals=0),
    )(*(in_hbm(array) for array in arrays))


NT = (((1,), (1,)), ((), ()))


def attention_kernel(
    block_0,
    block_1,
    block_2,
    block_3,
    query_weight,
    key_weight,
    value_weight,
    output_weight,
    query_down,
    value_down,
    query_up,
    value_up,
    query_gain,
    key_gain,
    cosine,
    sine,
    slot_mask,
    allowed,
    out_0,
    out_1,
    out_2,
    out_3,
    rows,
    context,
):
    tok_dev = block_0.shape[0]
    for k, block in enumerate((block_0, block_1, block_2, block_3)):
        rows[k * tok_dev : (k + 1) * tok_dev, :] = block[...]

    def project(weight):
        return jnp.dot(rows[...], weight[...], preferred_element_type=jnp.float32)

    def adapted(weight, down, up):
        low = project(down).astype(jnp.bfloat16) * slot_mask[...]
        return project(weight) + adapter_scale * jnp.dot(
            low, up[...], preferred_element_type=jnp.float32
        )

    def heads(inputs, gain):
        inputs = rms_scale(inputs) * gain
        turned = pltpu.roll(inputs, HEAD_SIZE // 2, 1)
        return (inputs * cosine[...] + turned * sine[...]).astype(jnp.bfloat16)

    queries = adapted(query_weight, query_down, query_up)
    keys = project(key_weight)
    values = adapted(value_weight, value_down, value_up).astype(jnp.bfloat16)
    for start in range(0, queries.shape[1], HEAD_SIZE):
        at = slice(start, start + HEAD_SIZE)
        scores = lax.dot_general(
            heads(queries[:, at], query_gain[:, at]),
            heads(keys[:, at], key_gain[:, at]),
            NT,
            preferred_element_type=jnp.float32,
        ) * HEAD_SIZE ** (-0.5)
        scores = jnp.where(allowed[...] > 0, scores, -1e30)
        weights = jnp.exp(scores - jnp.max(scores, axis=-1, keepdims=True))
        weights = (weights / jnp.sum(weights, axis=-1, keepdims=True)).astype(jnp.bfloat16)
        context[:, at] = jnp.dot(
            weights, values[:, at], preferred_element_type=jnp.float32
        ).astype(jnp.bfloat16)
    step = 1024
    for start in range(0, output_weight.shape[1], step):
        at = slice(start, start + step)
        part = jnp.dot(context[...], output_weight[:, at], preferred_element_type=jnp.float32)
        part = part.astype(jnp.bfloat16)
        for k, out in enumerate((out_0, out_1, out_2, out_3)):
            out[:, at] = part[k * tok_dev : (k + 1) * tok_dev]


def hidden_kernel(states, gate_0, gate_1, up_0, up_1, out):
    count = gate_0.shape[0]
    for k, (gate_rows, up_rows) in enumerate(((gate_0, up_0), (gate_1, up_1))):
        gate_act = lax.dot_general(
            states[...], gate_rows[...], NT, preferred_element_type=jnp.float32
        )
        up_act = lax.dot_general(states[...], up_rows[...], NT, preferred_element_type=jnp.float32)
        hidden = gate_act / (1.0 + jnp.exp(-gate_act)) * up_act
        out[:, k * count : (k + 1) * count] = hidden.astype(jnp.bfloat16)


def down_kernel(near, far, near_0, near_1, far_0, far_1, out_0, out_1, out_2, out_3):
    tok_dev, count = out_0.shape[0], near_0.shape[0]
    step = 512
    for start in range(0, near_0.shape[1], step):
        at = slice(start, start + step)
        part = 0.0
        for hidden, halves in ((near, (near_0, near_1)), (far, (far_0, far_1))):
            for k, rows in enumerate(halves):
                part += jnp.dot(
                    hidden[:, k * count : (k + 1) * count],
                    rows[:, at],
                    preferred_element_type=jnp.float32,
                )
        part = part.astype(jnp.bfloat16)
        for k, out in enumerate((out_0, out_1, out_2, out_3)):
            out[:, at] = part[k * tok_dev : (k + 1) * tok_dev]


def add_normed(base, added, gain):
    return (base.astype(jnp.float32) + rms_scale(added) * gain).astype(jnp.bfloat16)


def layer_direct(
    layer_input, angles, slot_mask, allowed, projections, adapters, head_gains, gains, ffn_rows
):
    tok_dev, width = layer_input.shape
    gate_rows, up_rows, down_rows = ffn_rows
    y = lax.axis_index("y")
    half = width // 2
    units = gate_rows.shape[0]
    gate_up_x = exchange(stacked(gate_rows, up_rows), "x")
    cosine, sine = jnp.cos(angles), jnp.sin(angles)
    block = jax.ShapeDtypeStruct((tok_dev, width), jnp.bfloat16)
    *staged_rows, own_block = staged(
        *([in_hbm(array)] for array in (*projections, *adapters, *head_gains, layer_input)),
        weight=0,
    )
    *blocks, own_block, down_rows = together(*line_gather(layer_input)[1:], own_block, down_rows)
    parts = vmem_call(
        attention_kernel,
        [block] * 4,
        [
            pltpu.VMEM((4 * tok_dev, width), jnp.bfloat16),
            pltpu.VMEM((4 * tok_dev, projections[0].shape[1]), jnp.bfloat16),
        ],
        [
            own_block,
            *blocks,
            *staged_rows,
            jnp.concatenate([cosine, cosine], axis=1),
            jnp.concatenate([-sine, sine], axis=1),
            slot_mask,
            allowed,
        ],
        8,
    )
    near = lax.dynamic_slice_in_dim(down_rows, y * half, half, axis=1)
    far = exchange(lax.dynamic_slice_in_dim(down_rows, (1 - y) * half, half, axis=1), "y")
    arrivals = line_arrivals(parts)
    attn_own, near, far = together(line_sum(arrivals), near, far)
    near_x = [exchange(rows, "x") for rows in jnp.split(near, 2)]
    residual_own = add_normed(layer_input, attn_own, gains[0])
    own, *line, other = together(*line_gather(residual_own), exchange(residual_own, "y"))
    line, gate_up_x, near_x[0] = together(jnp.concatenate(line), gate_up_x, near_x[0])
    far_x = exchange(far, "x")
    gate_half, up_half = staged(
        [in_hbm(gate_rows), (gate_up_x, 0, units)], [in_hbm(up_rows), (gate_up_x, units, units)]
    )
    halves = [gate_half, swapped(gate_half), up_half, swapped(up_half)]

    def hidden_units_of(first, others):
        (hidden,) = vmem_call(
            hidden_kernel,
            [jax.ShapeDtypeStruct((4 * tok_dev, 4 * gate_rows.shape[0]), jnp.bfloat16)],
            [],
            [jnp.concatenate([first, others]), *halves],
            8,
        )
        return hidden

    line_other = exchange(line, "y")
    hidden_own = hidden_units_of(own, line)
    line_other, hidden_own, near_x[1] = together(line_other, hidden_own, near_x[1])
    from_own = exchange(hidden_own, "y")
    hidden_other = hidden_units_of(other, line_other)
    hidden_other, from_own, far_x = together(hidden_other, from_own, far_x)
    from_other = exchange(hidden_other, "y")
    down_halves = [*both_halves(near, *near_x), *both_halves(far, far_x)]

    def summed_down(hidden, from_y):
        parts = vmem_call(
            down_kernel,
            [jax.ShapeDtypeStruct((tok_dev, half), jnp.bfloat16)] * 4,
            [],
            [hidden, from_y, *down_halves],
            8,
        )
        return line_sum(line_arrivals(parts))

    other_half = exchange(summed_down(hidden_other, from_own).astype(jnp.bfloat16), "y")
    own_half = summed_down(hidden_own, from_other)
    other_half = other_half.astype(jnp.float32)
    mlp_own = jnp.concatenate(
        [jnp.where(y == 1, other_half, own_half), jnp.where(y == 1, own_half, other_half)], axis=1
    )
    return add_normed(residual_own, mlp_own, gains[1])


def shards(
    layer_input,
    request_lengths,
    request_adapter,
    slot_adapter_index,
    query_weight,
    key_weight,
    value_weight,
    output_weight,
    query_norm_gain,
    key_norm_gain,
    query_down_factors,
    value_down_factors,
    query_up_factors,
    value_up_factors,
    attention_norm_gain,
    feedforward_norm_gain,
    gate_weight,
    up_weight,
    down_weight_transposed,
):
    tok_dev = layer_input.shape[0]
    tok_group = tok_dev * lax.axis_size("mlp")
    window = tok_group * 3 // 8
    heads_local = query_weight.shape[1] // HEAD_SIZE
    direct = [lax.axis_size(axis) for axis in (*REQ, "mlp")] == [2, 2, 2, 4]
    places = jnp.arange(tok_group, dtype=jnp.int32)
    if direct:
        places = (places + lax.axis_index("mlp") * tok_dev) % tok_group
    request, position, token_slot = layout(
        request_lengths[0], request_adapter[0], slot_adapter_index, places
    )
    columns = jnp.arange(ADAPTER_SLOTS * ADAPTER_RANK, dtype=jnp.int32) // ADAPTER_RANK
    slot_match_mask = (columns[None, :] == token_slot[:, None]).astype(jnp.bfloat16)
    gate_rows, up_rows, down_rows = gate_weight.T, up_weight.T, down_weight_transposed.T
    if direct:
        return layer_direct(
            layer_input,
            rotary_angles(position),
            slot_match_mask,
            allowed_keys(request, position, window).astype(jnp.float32),
            (query_weight, key_weight, value_weight, output_weight),
            (query_down_factors, value_down_factors, query_up_factors, value_up_factors),
            (query_norm_gain[None, :], key_norm_gain[None, :]),
            (attention_norm_gain, feedforward_norm_gain),
            (gate_rows, up_rows, down_rows),
        )
    group_token_rows = lax.all_gather(layer_input, "mlp", axis=0, tiled=True)
    query_reduced = (
        jnp.dot(group_token_rows, query_down_factors, preferred_element_type=jnp.float32).astype(
            jnp.bfloat16
        )
        * slot_match_mask
    )
    value_reduced = (
        jnp.dot(group_token_rows, value_down_factors, preferred_element_type=jnp.float32).astype(
            jnp.bfloat16
        )
        * slot_match_mask
    )
    query_before_norm = jnp.dot(
        group_token_rows, query_weight, preferred_element_type=jnp.float32
    ) + adapter_scale * jnp.dot(query_reduced, query_up_factors, preferred_element_type=jnp.float32)
    key_pre = jnp.dot(group_token_rows, key_weight, preferred_element_type=jnp.float32)
    value_before_adapter = jnp.dot(
        group_token_rows, value_weight, preferred_element_type=jnp.float32
    ) + adapter_scale * jnp.dot(value_reduced, value_up_factors, preferred_element_type=jnp.float32)
    queries = rotary(
        rms_scale(query_before_norm.reshape(tok_group, heads_local, HEAD_SIZE))
        * query_norm_gain.reshape(heads_local, HEAD_SIZE),
        position,
    ).astype(jnp.bfloat16)
    key_heads = rotary(
        rms_scale(key_pre.reshape(tok_group, heads_local, HEAD_SIZE))
        * key_norm_gain.reshape(heads_local, HEAD_SIZE),
        position,
    ).astype(jnp.bfloat16)
    value_heads = value_before_adapter.astype(jnp.bfloat16).reshape(
        tok_group, heads_local, HEAD_SIZE
    )
    context = attention(queries, key_heads, value_heads, request, position, window).reshape(
        tok_group, heads_local * HEAD_SIZE
    )
    attn_own = lax.psum_scatter(
        jnp.dot(context, output_weight, preferred_element_type=jnp.float32).astype(jnp.bfloat16),
        "mlp",
        scatter_dimension=0,
        tiled=True,
    ).astype(jnp.float32)
    residual_own = add_normed(layer_input, attn_own, attention_norm_gain)
    gate_rows, up_rows, down_rows = (
        lax.all_gather(rows, REQ, axis=0, tiled=True) for rows in (gate_rows, up_rows, down_rows)
    )
    hidden = hidden_units(
        lax.all_gather(residual_own, "mlp", axis=0, tiled=True), gate_rows, up_rows
    )
    part = jnp.dot(hidden, down_rows, preferred_element_type=jnp.float32)
    mlp_own = lax.psum_scatter(
        part.astype(jnp.bfloat16), "mlp", scatter_dimension=0, tiled=True
    ).astype(jnp.float32)
    return add_normed(residual_own, mlp_own, feedforward_norm_gain)


def solution(mesh):
    req, mlp = mesh.devices.shape
    side = math.isqrt(req // 2)
    fine = Mesh(mesh.devices.reshape(req // 2 // side, side, 2, mlp), ("y", "x", "core", "mlp"))
    return jax.shard_map(
        shards,
        mesh=fine,
        in_specs=(
            P((*REQ, "mlp"), None),
            P(REQ, None),
            P(REQ, None),
            P(),
            P(None, "mlp"),
            P(None, "mlp"),
            P(None, "mlp"),
            P("mlp", None),
            P("mlp"),
            P("mlp"),
            P(),
            P(),
            P(None, "mlp"),
            P(None, "mlp"),
            P(),
            P(),
            P(None, (*REQ, "mlp")),
            P(None, (*REQ, "mlp")),
            P(None, (*REQ, "mlp")),
        ),
        out_specs=P((*REQ, "mlp"), None),
        check_vma=False,
    )
```

```python
import math

import jax
import jax.numpy as jnp
from jax import lax
from jax.experimental import pallas as pl
from jax.experimental.pallas import tpu as pltpu
from jax.sharding import Mesh, PartitionSpec as P

HEAD_SIZE = 128
ADAPTER_RANK = 16
ADAPTER_SLOTS = 8
SINKS = 4
REQ = ("y", "x", "core")


epsilon = 1e-06
adapter_scale = 0.5
rope_theta = 500000.0


def rms_scale(inputs):
    return inputs * lax.rsqrt(jnp.mean(inputs * inputs, axis=-1, keepdims=True) + epsilon)


def rotary_angles(position):
    exponent = jnp.arange(HEAD_SIZE // 2, dtype=jnp.float32) * (2.0 / HEAD_SIZE)
    frequency = rope_theta ** (-exponent)
    return position.astype(jnp.float32)[:, None] * frequency[None, :]


def rotary(inputs, position):
    half_dim = inputs.shape[-1] // 2
    angles = rotary_angles(position)
    cosine = jnp.cos(angles)[:, None, :]
    sine_part = jnp.sin(angles)[:, None, :]
    first_half = inputs[..., :half_dim]
    second = inputs[..., half_dim:]
    return jnp.concatenate(
        [first_half * cosine - second * sine_part, second * cosine + first_half * sine_part],
        axis=-1,
    )


def layout(lengths, adapters, slot_adapter_index, places):
    req_ends = jnp.cumsum(lengths)
    starts = req_ends - lengths
    member = ((places[:, None] >= starts[None, :]) & (places[:, None] < req_ends[None, :])).astype(
        jnp.int32
    )
    request = jnp.sum(member * jnp.arange(lengths.shape[0], dtype=jnp.int32)[None, :], axis=1)
    position = places - jnp.sum(member * starts[None, :], axis=1)
    chosen = jnp.sum(member * adapters[None, :], axis=1)
    slot_ids = jnp.arange(slot_adapter_index.shape[0], dtype=jnp.int32)
    token_slot = jnp.sum(
        (chosen[:, None] == slot_adapter_index[None, :]).astype(jnp.int32) * slot_ids[None, :],
        axis=1,
    )
    return (request, position, token_slot)


def allowed_keys(request, position, window):
    distance = position[:, None] - position[None, :]
    return (
        (request[:, None] == request[None, :])
        & (distance >= 0)
        & ((distance < window) | (position[None, :] < SINKS))
    )


def attention(queries, key_heads, value_heads, request, position, window):
    scores = jnp.einsum(
        "qhd,khd->hqk", queries, key_heads, preferred_element_type=jnp.float32
    ) * HEAD_SIZE ** (-0.5)
    allowed = allowed_keys(request, position, window)
    scores = jnp.where(allowed[None, :, :], scores, -1e30)
    row_peak = jnp.max(scores, axis=-1, keepdims=True)
    weights = jnp.exp(scores - row_peak)
    weights = (weights / jnp.sum(weights, axis=-1, keepdims=True)).astype(jnp.bfloat16)
    context = jnp.einsum("hqk,khd->qhd", weights, value_heads, preferred_element_type=jnp.float32)
    return context.astype(jnp.bfloat16)


def hidden_units(states, gate_rows, up_rows):
    contract = (((1,), (1,)), ((), ()))
    gate_act = lax.dot_general(states, gate_rows, contract, preferred_element_type=jnp.float32)
    up_act = lax.dot_general(states, up_rows, contract, preferred_element_type=jnp.float32)
    return (jax.nn.silu(gate_act) * up_act).astype(jnp.bfloat16)


def exchange(block, axis):
    return lax.ppermute(block, axis, [(0, 1), (1, 0)])


def shift(block, hops):
    return lax.ppermute(block, "mlp", [((k + hops) % 4, k) for k in range(4)])


def line_gather(block):
    across = shift(block, 2)
    return [block, shift(block, 1), across, shift(block, 3)]


def line_arrivals(parts):
    across = shift(parts[2], 2)
    return [shift(parts[3], 1), across, shift(parts[1], 3), parts[0]]


def line_sum(arrivals):
    return sum(part.astype(jnp.float32) for part in arrivals)


def together(*values):
    return lax.optimization_barrier(values)


def swapped(half):
    return pltpu.with_memory_space_constraint(exchange(half, "core"), pltpu.VMEM)


def both_halves(*rows):
    (half,) = staged(rows)
    return half, swapped(half)


def vmem_call(kernel, outs, scratch, operands, vmem_mib):
    whole = pl.BlockSpec(memory_space=pltpu.VMEM)
    return pl.pallas_call(
        kernel,
        out_shape=outs,
        in_specs=[whole] * len(operands),
        out_specs=[whole] * len(outs),
        scratch_shapes=scratch,
        compiler_params=pltpu.CompilerParams(vmem_limit_bytes=vmem_mib << 20),
        cost_estimate=pl.CostEstimate(flops=1 << 20, bytes_accessed=1 << 20, transcendentals=0),
    )(*operands)


def in_hbm(array):
    return pltpu.with_memory_space_constraint(array, pltpu.HBM)


def staged(*groups, weight=4):
    groups = [
        [piece if isinstance(piece, tuple) else (piece, 0, piece.shape[0]) for piece in group]
        for group in groups
    ]
    arrays = []
    for piece in (piece for group in groups for piece in group):
        if not any(piece[0] is array for array in arrays):
            arrays.append(piece[0])
    places = [
        [next(k for k, array in enumerate(arrays) if array is piece[0]) for piece in group]
        for group in groups
    ]
    count = sum(len(group) for group in groups)

    def kernel(*refs):
        sources, targets, sems = refs[: len(arrays)], refs[len(arrays) : -1], refs[-1]
        copies = []
        for group, place, target in zip(groups, places, targets):
            at = 0
            for (_, start, rows), k in zip(group, place):
                copies.append(
                    pltpu.make_async_copy(
                        sources[k].at[pl.ds(start, rows), :],
                        target.at[pl.ds(at, rows), :],
                        sems.at[len(copies)],
                    )
                )
                copies[-1].start()
                at += rows
        for copy in copies:
            copy.wait()

    outs = [(sum(piece[2] for piece in group), group[0][0].shape[1]) for group in groups]
    size = sum(rows * columns for rows, columns in outs)
    return pl.pallas_call(
        kernel,
        out_shape=[pltpu.VMEM(shape, group[0][0].dtype) for shape, group in zip(outs, groups)],
        in_specs=[pl.BlockSpec(memory_space=pl.ANY)] * len(arrays),
        out_specs=[pl.BlockSpec(memory_space=pltpu.VMEM)] * len(groups),
        scratch_shapes=[pltpu.SemaphoreType.DMA((count,))],
        compiler_params=pltpu.CompilerParams(vmem_limit_bytes=1 << 20),
        cost_estimate=pl.CostEstimate(flops=0, bytes_accessed=weight * size, transcendentals=0),
    )(*arrays)


def stacked(*arrays):
    rows, columns = arrays[0].shape
    pieces = 3
    part = rows // pieces
    count = len(arrays) * pieces

    def kernel(*refs):
        sources, target, buffer, sems_in, sems_out = refs[:-4], *refs[-4:]
        into = [
            pltpu.make_async_copy(
                sources[k // pieces].at[pl.ds(k % pieces * part, part), :],
                buffer.at[k],
                sems_in.at[k],
            )
            for k in range(count)
        ]
        out = [
            pltpu.make_async_copy(
                buffer.at[k], target.at[pl.ds(k * part, part), :], sems_out.at[k]
            )
            for k in range(count)
        ]
        for copy in into:
            copy.start()
        for copy_in, copy_out in zip(into, out):
            copy_in.wait()
            copy_out.start()
        for copy in out:
            copy.wait()

    return pl.pallas_call(
        kernel,
        out_shape=pltpu.HBM((len(arrays) * rows, columns), arrays[0].dtype),
        in_specs=[pl.BlockSpec(memory_space=pl.ANY)] * len(arrays),
        out_specs=pl.BlockSpec(memory_space=pltpu.HBM),
        scratch_shapes=[
            pltpu.VMEM((count, part, columns), arrays[0].dtype),
            pltpu.SemaphoreType.DMA((count,)),
            pltpu.SemaphoreType.DMA((count,)),
        ],
        compiler_params=pltpu.CompilerParams(vmem_limit_bytes=8 << 20),
        cost_estimate=pl.CostEstimate(flops=0, bytes_accessed=1 << 20, transcendentals=0),
    )(*(in_hbm(array) for array in arrays))


NT = (((1,), (1,)), ((), ()))


def attention_kernel(
    block_0,
    block_1,
    block_2,
    block_3,
    query_weight,
    key_weight,
    value_weight,
    output_weight,
    query_down,
    value_down,
    query_up,
    value_up,
    query_gain,
    key_gain,
    cosine,
    sine,
    slot_mask,
    allowed,
    out_0,
    out_1,
    out_2,
    out_3,
    rows,
    context,
):
    tok_dev = block_0.shape[0]
    for k, block in enumerate((block_0, block_1, block_2, block_3)):
        rows[k * tok_dev : (k + 1) * tok_dev, :] = block[...]

    def project(weight):
        return jnp.dot(rows[...], weight[...], preferred_element_type=jnp.float32)

    def adapted(weight, down, up):
        low = project(down).astype(jnp.bfloat16) * slot_mask[...]
        return project(weight) + adapter_scale * jnp.dot(
            low, up[...], preferred_element_type=jnp.float32
        )

    def heads(inputs, gain):
        inputs = rms_scale(inputs) * gain
        turned = pltpu.roll(inputs, HEAD_SIZE // 2, 1)
        return (inputs * cosine[...] + turned * sine[...]).astype(jnp.bfloat16)

    queries = adapted(query_weight, query_down, query_up)
    keys = project(key_weight)
    values = adapted(value_weight, value_down, value_up).astype(jnp.bfloat16)
    for start in range(0, queries.shape[1], HEAD_SIZE):
        at = slice(start, start + HEAD_SIZE)
        scores = lax.dot_general(
            heads(queries[:, at], query_gain[:, at]),
            heads(keys[:, at], key_gain[:, at]),
            NT,
            preferred_element_type=jnp.float32,
        ) * HEAD_SIZE ** (-0.5)
        scores = jnp.where(allowed[...] > 0, scores, -1e30)
        weights = jnp.exp(scores - jnp.max(scores, axis=-1, keepdims=True))
        weights = (weights / jnp.sum(weights, axis=-1, keepdims=True)).astype(jnp.bfloat16)
        context[:, at] = jnp.dot(
            weights, values[:, at], preferred_element_type=jnp.float32
        ).astype(jnp.bfloat16)
    step = 1024
    for start in range(0, output_weight.shape[1], step):
        at = slice(start, start + step)
        part = jnp.dot(context[...], output_weight[:, at], preferred_element_type=jnp.float32)
        part = part.astype(jnp.bfloat16)
        for k, out in enumerate((out_0, out_1, out_2, out_3)):
            out[:, at] = part[k * tok_dev : (k + 1) * tok_dev]


def hidden_kernel(states, gate_0, gate_1, up_0, up_1, out):
    count = gate_0.shape[0]
    for k, (gate_rows, up_rows) in enumerate(((gate_0, up_0), (gate_1, up_1))):
        gate_act = lax.dot_general(
            states[...], gate_rows[...], NT, preferred_element_type=jnp.float32
        )
        up_act = lax.dot_general(states[...], up_rows[...], NT, preferred_element_type=jnp.float32)
        hidden = gate_act / (1.0 + jnp.exp(-gate_act)) * up_act
        out[:, k * count : (k + 1) * count] = hidden.astype(jnp.bfloat16)


def down_kernel(near, far, near_0, near_1, far_0, far_1, out_0, out_1, out_2, out_3):
    tok_dev, count = out_0.shape[0], near_0.shape[0]
    step = 512
    for start in range(0, near_0.shape[1], step):
        at = slice(start, start + step)
        part = 0.0
        for hidden, halves in ((near, (near_0, near_1)), (far, (far_0, far_1))):
            for k, rows in enumerate(halves):
                part += jnp.dot(
                    hidden[:, k * count : (k + 1) * count],
                    rows[:, at],
                    preferred_element_type=jnp.float32,
                )
        part = part.astype(jnp.bfloat16)
        for k, out in enumerate((out_0, out_1, out_2, out_3)):
            out[:, at] = part[k * tok_dev : (k + 1) * tok_dev]


def add_normed(base, added, gain):
    return (base.astype(jnp.float32) + rms_scale(added) * gain).astype(jnp.bfloat16)


def layer_direct(
    layer_input, angles, slot_mask, allowed, projections, adapters, head_gains, gains, ffn_rows
):
    tok_dev, width = layer_input.shape
    gate_rows, up_rows, down_rows = ffn_rows
    y = lax.axis_index("y")
    half = width // 2
    units = gate_rows.shape[0]
    gate_up_x = exchange(stacked(gate_rows, up_rows), "x")
    cosine, sine = jnp.cos(angles), jnp.sin(angles)
    block = jax.ShapeDtypeStruct((tok_dev, width), jnp.bfloat16)
    *staged_rows, own_block = staged(
        *([in_hbm(array)] for array in (*projections, *adapters, *head_gains, layer_input)),
        weight=0,
    )
    *blocks, own_block, down_rows = together(*line_gather(layer_input)[1:], own_block, down_rows)
    parts = vmem_call(
        attention_kernel,
        [block] * 4,
        [
            pltpu.VMEM((4 * tok_dev, width), jnp.bfloat16),
            pltpu.VMEM((4 * tok_dev, projections[0].shape[1]), jnp.bfloat16),
        ],
        [
            own_block,
            *blocks,
            *staged_rows,
            jnp.concatenate([cosine, cosine], axis=1),
            jnp.concatenate([-sine, sine], axis=1),
            slot_mask,
            allowed,
        ],
        8,
    )
    near = lax.dynamic_slice_in_dim(down_rows, y * half, half, axis=1)
    far = exchange(lax.dynamic_slice_in_dim(down_rows, (1 - y) * half, half, axis=1), "y")
    arrivals = line_arrivals(parts)
    attn_own, near, far = together(line_sum(arrivals), near, far)
    near_x = [exchange(rows, "x") for rows in jnp.split(near, 2)]
    residual_own = add_normed(layer_input, attn_own, gains[0])
    own, *line, other = together(*line_gather(residual_own), exchange(residual_own, "y"))
    line, gate_up_x, near_x[0] = together(jnp.concatenate(line), gate_up_x, near_x[0])
    far_x = exchange(far, "x")
    gate_half, up_half = staged(
        [in_hbm(gate_rows), (gate_up_x, 0, units)], [in_hbm(up_rows), (gate_up_x, units, units)]
    )
    halves = [gate_half, swapped(gate_half), up_half, swapped(up_half)]

    def hidden_units_of(first, others):
        (hidden,) = vmem_call(
            hidden_kernel,
            [jax.ShapeDtypeStruct((4 * tok_dev, 4 * gate_rows.shape[0]), jnp.bfloat16)],
            [],
            [jnp.concatenate([first, others]), *halves],
            8,
        )
        return hidden

    line_other = exchange(line, "y")
    hidden_own = hidden_units_of(own, line)
    line_other, hidden_own, near_x[1], far_late = together(
        line_other, hidden_own, near_x[1], far
    )
    far_core = exchange(far_late, "core")
    from_own = exchange(hidden_own, "y")
    hidden_other = hidden_units_of(other, line_other)
    hidden_other, from_own, far_x, far_core = together(hidden_other, from_own, far_x, far_core)
    from_other = exchange(hidden_other, "y")
    down_halves = [
        *both_halves(near, *near_x),
        *staged([far, far_x], [far_core, exchange(far_x, "core")]),
    ]

    def summed_down(hidden, from_y):
        parts = vmem_call(
            down_kernel,
            [jax.ShapeDtypeStruct((tok_dev, half), jnp.bfloat16)] * 4,
            [],
            [hidden, from_y, *down_halves],
            8,
        )
        return line_sum(line_arrivals(parts))

    other_half = exchange(summed_down(hidden_other, from_own).astype(jnp.bfloat16), "y")
    own_half = summed_down(hidden_own, from_other)
    other_half = other_half.astype(jnp.float32)
    mlp_own = jnp.concatenate(
        [jnp.where(y == 1, other_half, own_half), jnp.where(y == 1, own_half, other_half)], axis=1
    )
    return add_normed(residual_own, mlp_own, gains[1])


def shards(
    layer_input,
    request_lengths,
    request_adapter,
    slot_adapter_index,
    query_weight,
    key_weight,
    value_weight,
    output_weight,
    query_norm_gain,
    key_norm_gain,
    query_down_factors,
    value_down_factors,
    query_up_factors,
    value_up_factors,
    attention_norm_gain,
    feedforward_norm_gain,
    gate_weight,
    up_weight,
    down_weight_transposed,
):
    tok_dev = layer_input.shape[0]
    tok_group = tok_dev * lax.axis_size("mlp")
    window = tok_group * 3 // 8
    heads_local = query_weight.shape[1] // HEAD_SIZE
    direct = [lax.axis_size(axis) for axis in (*REQ, "mlp")] == [2, 2, 2, 4]
    places = jnp.arange(tok_group, dtype=jnp.int32)
    if direct:
        places = (places + lax.axis_index("mlp") * tok_dev) % tok_group
    request, position, token_slot = layout(
        request_lengths[0], request_adapter[0], slot_adapter_index, places
    )
    columns = jnp.arange(ADAPTER_SLOTS * ADAPTER_RANK, dtype=jnp.int32) // ADAPTER_RANK
    slot_match_mask = (columns[None, :] == token_slot[:, None]).astype(jnp.bfloat16)
    gate_rows, up_rows, down_rows = gate_weight.T, up_weight.T, down_weight_transposed.T
    if direct:
        return layer_direct(
            layer_input,
            rotary_angles(position),
            slot_match_mask,
            allowed_keys(request, position, window).astype(jnp.float32),
            (query_weight, key_weight, value_weight, output_weight),
            (query_down_factors, value_down_factors, query_up_factors, value_up_factors),
            (query_norm_gain[None, :], key_norm_gain[None, :]),
            (attention_norm_gain, feedforward_norm_gain),
            (gate_rows, up_rows, down_rows),
        )
    group_token_rows = lax.all_gather(layer_input, "mlp", axis=0, tiled=True)
    query_reduced = (
        jnp.dot(group_token_rows, query_down_factors, preferred_element_type=jnp.float32).astype(
            jnp.bfloat16
        )
        * slot_match_mask
    )
    value_reduced = (
        jnp.dot(group_token_rows, value_down_factors, preferred_element_type=jnp.float32).astype(
            jnp.bfloat16
        )
        * slot_match_mask
    )
    query_before_norm = jnp.dot(
        group_token_rows, query_weight, preferred_element_type=jnp.float32
    ) + adapter_scale * jnp.dot(query_reduced, query_up_factors, preferred_element_type=jnp.float32)
    key_pre = jnp.dot(group_token_rows, key_weight, preferred_element_type=jnp.float32)
    value_before_adapter = jnp.dot(
        group_token_rows, value_weight, preferred_element_type=jnp.float32
    ) + adapter_scale * jnp.dot(value_reduced, value_up_factors, preferred_element_type=jnp.float32)
    queries = rotary(
        rms_scale(query_before_norm.reshape(tok_group, heads_local, HEAD_SIZE))
        * query_norm_gain.reshape(heads_local, HEAD_SIZE),
        position,
    ).astype(jnp.bfloat16)
    key_heads = rotary(
        rms_scale(key_pre.reshape(tok_group, heads_local, HEAD_SIZE))
        * key_norm_gain.reshape(heads_local, HEAD_SIZE),
        position,
    ).astype(jnp.bfloat16)
    value_heads = value_before_adapter.astype(jnp.bfloat16).reshape(
        tok_group, heads_local, HEAD_SIZE
    )
    context = attention(queries, key_heads, value_heads, request, position, window).reshape(
        tok_group, heads_local * HEAD_SIZE
    )
    attn_own = lax.psum_scatter(
        jnp.dot(context, output_weight, preferred_element_type=jnp.float32).astype(jnp.bfloat16),
        "mlp",
        scatter_dimension=0,
        tiled=True,
    ).astype(jnp.float32)
    residual_own = add_normed(layer_input, attn_own, attention_norm_gain)
    gate_rows, up_rows, down_rows = (
        lax.all_gather(rows, REQ, axis=0, tiled=True) for rows in (gate_rows, up_rows, down_rows)
    )
    hidden = hidden_units(
        lax.all_gather(residual_own, "mlp", axis=0, tiled=True), gate_rows, up_rows
    )
    part = jnp.dot(hidden, down_rows, preferred_element_type=jnp.float32)
    mlp_own = lax.psum_scatter(
        part.astype(jnp.bfloat16), "mlp", scatter_dimension=0, tiled=True
    ).astype(jnp.float32)
    return add_normed(residual_own, mlp_own, feedforward_norm_gain)


def solution(mesh):
    req, mlp = mesh.devices.shape
    side = math.isqrt(req // 2)
    fine = Mesh(mesh.devices.reshape(req // 2 // side, side, 2, mlp), ("y", "x", "core", "mlp"))
    return jax.shard_map(
        shards,
        mesh=fine,
        in_specs=(
            P((*REQ, "mlp"), None),
            P(REQ, None),
            P(REQ, None),
            P(),
            P(None, "mlp"),
            P(None, "mlp"),
            P(None, "mlp"),
            P("mlp", None),
            P("mlp"),
            P("mlp"),
            P(),
            P(),
            P(None, "mlp"),
            P(None, "mlp"),
            P(),
            P(),
            P(None, (*REQ, "mlp")),
            P(None, (*REQ, "mlp")),
            P(None, (*REQ, "mlp")),
        ),
        out_specs=P((*REQ, "mlp"), None),
        check_vma=False,
    )
```
